32 devices in a mesh: dom: 8 (over z, y), shuf: 4 (over x, core).
Axes of the slice: x: 2, y: 2, z: 4, core: 2. Of those that a mesh axis runs over, the one named last changes fastest.
Arguments:
- features: float32 [8192, 128], P(('dom', 'shuf')), may hold values from -204 to 204
- tile_values: float32 [256, 128, 128], P(('dom', 'shuf')), may hold values from -0.375 to 0.375
- tile_dst: int32 [256], P(('dom', 'shuf')), may hold values from 0 to 1, as said below
- tile_src: int32 [256], P(('dom', 'shuf')), may hold values from 0 to 5
- tile_count: int32 [32], P(('dom', 'shuf')), may hold values from 2 to 8, as said below
- send_left: int32 [64], P(('dom', 'shuf')), may hold values from 0 to 1
- send_right: int32 [64], P(('dom', 'shuf')), may hold values from 0 to 1
- send_count: int32 [32, 2], P(('dom', 'shuf')), may hold values from 1 to 2, as said below
- batch_order: int32 [32, 256], P(('dom', 'shuf')), may hold values from 0 to 255, each once within a row
- labels: int32 [8192], P(('dom', 'shuf')), may hold values from 0 to 171
- w_branch: bfloat16 [4, 128, 1024], replicated, may hold values from -0.5 to 0.5
- w_class: bfloat16 [4096, 172], replicated
Outputs:
- loss_rows: float32 [8192], P(('dom', 'shuf'))
- grad_branch: float32 [4, 128, 1024], P(None, None, 'shuf')
- grad_class: float32 [4096, 172], P('shuf')
The draws below stay inside these ranges and needn't reach their ends.
Inputs may be any that keep to these rules, and one draw needn't show every extreme that they name: `tile_dst`: in each partition's first 2 tile slots every local block is the destination exactly once. `tile_count`: some partition has all 8 slots live. `send_count`: some list has all 2 slots live.
All inputs are finite; a program needn't handle non-finite values.
Results may differ from the reference program's by a relative error of at most 0.0045.
The reference program's roundings to bfloat16 on the way count: a program that leaves them out, or rounds other values in their place, can miss the bound.
Values may be sent and summed in bfloat16 or wider, within the bound.
No kernel may reach another device: no remote copies, remote signals or barrier semaphores. Data moves between devices by JAX's collectives and lax.ppermute only.
A program may use at most 64 MiB of HBM per device.

```python
import math
import jax
import jax.numpy as jnp
from jax import lax

F = 128
CLS = 172
HID = 1024
HOPS = 3
BLK = 128
SB = 2
LB = 2
TILES = 8
NODE_DEV = 256
NODES = 8192
CAT = 4096
N_DOM = 8
N_SHUF = 4


def draw_features(key, part):
    key = jax.random.fold_in(key, 5)
    value_key = jax.random.fold_in(key, 0)
    values = jax.random.truncated_normal(value_key, -6.0, 6.0, (NODES, F), jnp.float32)
    return values.astype(jnp.float32)


def draw_tile_dst(key, part):
    key = jax.random.fold_in(key, 11)
    first_key, other_key = jax.random.split(key)
    devices = N_DOM * N_SHUF
    scores = jax.random.randint(first_key, (devices, LB), 0, 1 << 20) * LB + jnp.arange(LB, dtype=jnp.int32)[None, :]
    leading = jnp.argsort(scores, axis=1).astype(jnp.int32)
    remainder = jax.random.randint(other_key, (devices, TILES - LB), 0, LB).astype(jnp.int32)
    return jnp.concatenate([leading, remainder], axis=1).reshape(devices * TILES).astype(jnp.int32)


def draw_tile_count(key, part):
    key = jax.random.fold_in(key, 23)
    count_key, chosen_key = jax.random.split(key)
    devices = N_DOM * N_SHUF
    counts = LB + jax.random.randint(count_key, (devices,), 0, LB + 1)
    chosen = jax.random.randint(chosen_key, (), 0, devices)
    return counts.at[chosen].set(TILES).astype(jnp.int32)


def draw_send_count(key, part):
    key = jax.random.fold_in(key, 37)
    count_key, chosen_key = jax.random.split(key)
    devices = N_DOM * N_SHUF
    counts = jax.random.randint(count_key, (devices * 2,), 1, SB + 1)
    chosen = jax.random.randint(chosen_key, (), 0, devices * 2)
    return counts.at[chosen].set(SB).reshape(devices, 2).astype(jnp.int32)


def pair_rows(leading, partner):
    return jnp.stack([leading, 0.25 * partner - leading], axis=1).reshape(CAT, CLS)


def draw_w_class(key, part):
    key = jax.random.fold_in(key, 53)
    first_key, second_key = jax.random.split(key, 2)
    scale = 6.0 / CAT ** 0.5
    leading = jax.random.normal(first_key, (CAT // 2, CLS), jnp.float32) * scale
    partner = jax.random.normal(second_key, (CAT // 2, CLS), jnp.float32) * scale
    weights = pair_rows(leading, partner)
    return weights.astype(jnp.bfloat16)


def with_ends(entries, stream_key, least, high):
    index_at = [jax.random.randint(jax.random.fold_in(stream_key, axis), (), 0, length) for axis, length in enumerate(entries.shape)]
    longest = entries.shape.index(max(entries.shape))
    next_to = index_at[:longest] + [(index_at[longest] + 1) % entries.shape[longest]] + index_at[longest + 1:]
    return entries.at[tuple(index_at)].set(least).at[tuple(next_to)].set(high)


def block_levels(own_key, dims, pieces, least, largest):
    def one(dim, shards_of):
        heights = jax.random.uniform(jax.random.fold_in(jax.random.fold_in(own_key, 6), dim), (shards_of,), jnp.float32, least / len(pieces), largest / len(pieces))
        return jnp.repeat(jnp.exp(heights), dims[dim] // shards_of).reshape((-1,) + (1,) * (len(dims) - dim - 1))

    level = one(*pieces[0])
    for cut in pieces[1:]:
        level = level * one(*cut)
    return level


def normal_values(rng, dims, width, limit, shards=(), kind=jnp.bfloat16):
    result = jax.random.normal(rng, dims, jnp.float32) * width
    if len(shards) > 0:
        result = block_levels(rng, dims, shards, -0.22, 0.18) * result
    return jnp.clip(result, min=-limit, max=limit).astype(kind)


def setup_inputs(seed: int = 0) -> dict:
    streams_of = jax.random.split(jax.random.key(seed), 13)
    return {
        "features": draw_features(jax.random.fold_in(streams_of[12], 71), 0),
        "tile_values": normal_values(streams_of[1], (N_DOM * N_SHUF * TILES, BLK, BLK), (2 * BLK) ** -0.5, 0.375, ((0, 32),), jnp.float32),
        "tile_dst": draw_tile_dst(jax.random.fold_in(streams_of[12], 71), 0),
        "tile_src": with_ends(jax.random.randint(streams_of[3], (N_DOM * N_SHUF * TILES,), 0, LB + 2 * SB), jax.random.fold_in(streams_of[3], 1), 0, (LB + 2 * SB) - 1).astype(jnp.int32),
        "tile_count": draw_tile_count(jax.random.fold_in(streams_of[12], 71), 0),
        "send_left": with_ends(jax.random.randint(streams_of[5], (N_DOM * N_SHUF * SB,), 0, LB), jax.random.fold_in(streams_of[5], 1), 0, LB - 1).astype(jnp.int32),
        "send_right": with_ends(jax.random.randint(streams_of[6], (N_DOM * N_SHUF * SB,), 0, LB), jax.random.fold_in(streams_of[6], 1), 0, LB - 1).astype(jnp.int32),
        "send_count": draw_send_count(jax.random.fold_in(streams_of[12], 71), 0),
        "batch_order": jax.vmap(lambda own: jax.random.permutation(own, NODE_DEV))(jax.random.split(streams_of[8], (N_DOM * N_SHUF))).reshape((N_DOM * N_SHUF, NODE_DEV)).astype(jnp.int32),
        "labels": with_ends(jax.random.randint(streams_of[9], (NODES,), 0, CLS), jax.random.fold_in(streams_of[9], 1), 0, CLS - 1).astype(jnp.int32),
        "w_branch": normal_values(streams_of[10], (HOPS + 1, F, HID), F ** -0.5, 0.5),
        "w_class": draw_w_class(jax.random.fold_in(streams_of[12], 71), 0),
    }


def local_terms(batch_rows, labels, w_branch, w_class, row_scale):
    branch_count = batch_rows.shape[0]
    hidden_width = w_branch.shape[2]
    branch_pre = [jnp.dot(batch_rows[branch_index], w_branch[branch_index], preferred_element_type=jnp.float32) for branch_index in range(branch_count)]
    hidden = jnp.concatenate([jax.nn.relu(branch_value) for branch_value in branch_pre], axis=1).astype(jnp.bfloat16)
    logits = jnp.dot(hidden, w_class, preferred_element_type=jnp.float32)
    row_max = lax.optimization_barrier(jnp.max(logits, axis=1, keepdims=True))
    log_total = row_max[:, 0] + jnp.log(lax.optimization_barrier(jnp.sum(jnp.exp(logits - row_max), axis=1)))
    classes = jnp.arange(logits.shape[1], dtype=jnp.int32)
    onehot = (labels[:, None] == classes[None, :]).astype(jnp.float32)
    loss_rows = log_total - lax.optimization_barrier(jnp.sum(logits * onehot, axis=1))
    softmax_rows = jnp.exp(logits - log_total[:, None])
    dlogits = ((softmax_rows - onehot) * row_scale).astype(jnp.bfloat16)
    grad_class = jnp.dot(hidden.T, dlogits, preferred_element_type=jnp.float32)
    dhidden = (jnp.dot(dlogits, w_class.T, preferred_element_type=jnp.float32) * (hidden > 0)).astype(jnp.bfloat16)
    grad_branch = jnp.stack([jnp.dot(batch_rows[branch_index].T, dhidden[:, branch_index * hidden_width:(branch_index + 1) * hidden_width], preferred_element_type=jnp.float32) for branch_index in range(branch_count)])
    return (loss_rows, grad_branch, grad_class)

def propagate_one(operands):
    extended, tile_block, dest_ids, source_ids, live_count = operands
    gathered = extended[source_ids]
    products = jnp.einsum('tij,tjf->tif', tile_block, gathered, precision=lax.Precision.HIGHEST)
    live_mask = jnp.arange(TILES, dtype=jnp.int32) < live_count
    onehot = ((dest_ids[None, :] == jnp.arange(LB, dtype=jnp.int32)[:, None]) & live_mask[None, :]).astype(jnp.float32)
    return jnp.einsum('bt,tif->bif', onehot, products, precision=lax.Precision.HIGHEST)

def pick_blocks(current, indices, live_count):
    picked = jax.vmap(jax.vmap(lambda blocks, wanted: blocks[wanted]))(current, indices)
    slot_ids = jnp.arange(SB, dtype=jnp.int32)
    keep = (slot_ids[None, None, :] < live_count[:, :, None]).astype(jnp.float32)
    return picked * keep[:, :, :, None, None]

def reference(features, tile_values, tile_dst, tile_src, tile_count, send_left, send_right, send_count, batch_order, labels, w_branch, w_class):
    devices = N_DOM * N_SHUF
    current = features.reshape(N_DOM, N_SHUF, LB, BLK, F)
    tile_all = tile_values.reshape(devices, TILES, BLK, BLK)
    dest_all = tile_dst.reshape(devices, TILES)
    source_all = tile_src.reshape(devices, TILES)
    left_ids = send_left.reshape(N_DOM, N_SHUF, SB)
    right_ids = send_right.reshape(N_DOM, N_SHUF, SB)
    slot_counts = send_count.reshape(N_DOM, N_SHUF, 2)
    hop_list = [features.reshape(N_DOM, N_SHUF, NODE_DEV, F)]
    for hop_index in range(HOPS):
        to_left = pick_blocks(current, left_ids, slot_counts[:, :, 0])
        to_right = pick_blocks(current, right_ids, slot_counts[:, :, 1])
        from_lower = jnp.roll(to_right, 1, axis=0)
        from_upper = jnp.roll(to_left, -1, axis=0)
        extended = jnp.concatenate([current, from_lower, from_upper], axis=2).reshape(devices, LB + 2 * SB, BLK, F)
        updated = lax.map(propagate_one, (extended, tile_all, dest_all, source_all, tile_count))
        current = updated.reshape(N_DOM, N_SHUF, LB, BLK, F)
        hop_list.append(current.reshape(N_DOM, N_SHUF, NODE_DEV, F))
    share = NODE_DEV // N_SHUF
    orders = batch_order.reshape(N_DOM, N_SHUF, NODE_DEV)
    batches = []
    for hop_rows in hop_list:
        sorted_rows = jax.vmap(jax.vmap(lambda rows_in, wanted: rows_in[wanted]))(hop_rows, orders)
        regrouped = sorted_rows.reshape(N_DOM, N_SHUF, N_SHUF, share, F).transpose(0, 2, 1, 3, 4)
        batches.append(regrouped.reshape(devices, NODE_DEV, F).astype(jnp.bfloat16))
    batch_all = jnp.stack(batches, axis=1)
    label_all = labels.reshape(devices, NODE_DEV)
    row_scale = 1.0 / math.sqrt(NODES)

    def accumulate(running, inputs):
        loss_rows, grad_branch, grad_class = local_terms(inputs[0], inputs[1], w_branch, w_class, row_scale)
        return ((running[0] + grad_branch, running[1] + grad_class), loss_rows)
    start = (jnp.zeros((HOPS + 1, F, HID), jnp.float32), jnp.zeros((CAT, CLS), jnp.float32))
    totals, losses = lax.scan(accumulate, start, (batch_all, label_all))
    return (losses.reshape(NODES), totals[0], totals[1])
```

```python
import functools
import math

import jax
import jax.numpy as jnp
from jax import lax
from jax.experimental import pallas as pl
from jax.experimental.pallas import tpu as pltpu
from jax.sharding import PartitionSpec as P

HOPS = 3
LANES = 128
VMEM_LIMIT = 24 * 1024 * 1024

IN_VMEM = pl.BlockSpec(memory_space=pltpu.VMEM)
IN_SMEM = pl.BlockSpec(memory_space=pltpu.SMEM)
BF16 = jnp.bfloat16
F32 = jnp.float32


def up_to(value, multiple):
    return -(-value // multiple) * multiple


def passed_along(value, axis, steps):
    count = lax.axis_size(axis)
    pairs = [(source, (source + steps) % count) for source in range(count)]
    return lax.ppermute(value, axis, pairs)


def matmul(left, right, dims=((1,), (0,)), precision=None):
    return lax.dot_general(
        left, right, (dims, ((), ())), precision=precision, preferred_element_type=F32
    )


def call(kernel, out_shape, in_specs, flops, scratch=()):
    outs = out_shape if isinstance(out_shape, (list, tuple)) else [out_shape]
    moved = sum(math.prod(one.shape) * one.dtype.itemsize for one in outs)
    return pl.pallas_call(
        kernel,
        out_shape=out_shape,
        in_specs=in_specs,
        out_specs=[IN_VMEM] * len(out_shape)
        if isinstance(out_shape, (list, tuple))
        else IN_VMEM,
        scratch_shapes=list(scratch),
        compiler_params=pltpu.CompilerParams(vmem_limit_bytes=VMEM_LIMIT),
        cost_estimate=pl.CostEstimate(
            flops=flops, bytes_accessed=3 * moved, transcendentals=0
        ),
    )


def write_sends(blocks, left_ref, right_ref, left_ids, right_ids, counts):
    for slot in range(left_ref.shape[0]):
        for out_ref, ids, live in (
            (left_ref, left_ids, counts(0)),
            (right_ref, right_ids, counts(1)),
        ):
            index = ids(slot)
            picked = blocks[0]
            for number in range(1, len(blocks)):
                picked = jnp.where(index == number, blocks[number], picked)
            out_ref[slot] = jnp.where(slot < live, picked, 0.0)


def first_kernel(sl_ref, sr_ref, sc_ref, feat_ref, left_ref, right_ref, b_ref):
    blocks = [feat_ref[number] for number in range(feat_ref.shape[0])]
    write_sends(
        blocks,
        left_ref,
        right_ref,
        lambda slot: sl_ref[slot],
        lambda slot: sr_ref[slot],
        lambda side: sc_ref[0, side],
    )
    for number, block in enumerate(blocks):
        size = block.shape[0]
        b_ref[number * size : (number + 1) * size] = block.astype(BF16)


def next_blocks(dst_ref, src_ref, count_ref, cur_ref, low_ref, high_ref, tiles_ref, ext_ref):
    local = cur_ref.shape[0]
    slots = low_ref.shape[0]
    ext_ref[:local] = cur_ref[...]
    ext_ref[local : local + slots] = low_ref[...]
    ext_ref[local + slots :] = high_ref[...]
    totals = [jnp.zeros(cur_ref.shape[1:], F32) for _ in range(local)]
    live = count_ref[0]
    for tile in range(tiles_ref.shape[0]):
        product = matmul(
            tiles_ref[tile], ext_ref[src_ref[tile]], precision=lax.Precision.HIGHEST
        )
        wanted = jnp.where(tile < live, dst_ref[tile], -1)
        for number in range(local):
            totals[number] = totals[number] + jnp.where(wanted == number, product, 0.0)
    return totals


def hop_kernel(
    dst_ref, src_ref, count_ref, sl_ref, sr_ref, sc_ref,
    cur_ref, low_ref, high_ref, tiles_ref,
    next_ref, left_ref, right_ref, b_ref, ext_ref,
):
    blocks = next_blocks(
        dst_ref, src_ref, count_ref, cur_ref, low_ref, high_ref, tiles_ref, ext_ref
    )
    write_sends(
        blocks,
        left_ref,
        right_ref,
        lambda slot: sl_ref[slot],
        lambda slot: sr_ref[slot],
        lambda side: sc_ref[0, side],
    )
    for number, block in enumerate(blocks):
        size = block.shape[0]
        next_ref[number] = block
        b_ref[number * size : (number + 1) * size] = block.astype(BF16)


def branch_logits(rows, w_ref, wc_ref):
    hidden = jnp.maximum(matmul(rows, w_ref[...]), 0.0).astype(BF16)
    return matmul(hidden, wc_ref[...])


def forward_kernel(b_ref, w_ref, wc_ref, out_ref):
    out_ref[...] = branch_logits(b_ref[...], w_ref, wc_ref)


def forward_more_kernel(b_ref, w_ref, wc_ref, before_ref, out_ref):
    out_ref[...] = before_ref[...] + branch_logits(b_ref[...], w_ref, wc_ref)


def last_kernel(
    classes, row_scale,
    dst_ref, src_ref, count_ref,
    cur_ref, low_ref, high_ref, tiles_ref,
    before_ref, w_ref, wc_ref, order_ref, label_ref,
    out_ref, ext_ref,
):
    blocks = next_blocks(
        dst_ref, src_ref, count_ref, cur_ref, low_ref, high_ref, tiles_ref, ext_ref
    )
    halves = [block.astype(BF16) for block in blocks]
    rows_b = jnp.concatenate(halves, axis=0)
    size = halves[0].shape[0]
    width = halves[0].shape[1]
    for number, half in enumerate(halves):
        out_ref[:size, number * width : (number + 1) * width] = half
    logits = before_ref[...] + branch_logits(rows_b, w_ref, wc_ref)
    rows, wide = logits.shape
    lane = lax.broadcasted_iota(jnp.int32, (rows, wide), 1)
    logits = jnp.where(lane < classes, logits, -jnp.inf)
    place = order_ref[...] == lax.broadcasted_iota(jnp.int32, (rows, rows), 0)
    label = jnp.sum(
        jnp.where(place, label_ref[...].astype(F32), 0.0), axis=1, keepdims=True
    ).astype(jnp.int32)
    hit = lane == label
    top = jnp.max(logits, axis=1, keepdims=True)
    log_total = top + jnp.log(jnp.sum(jnp.exp(logits - top), axis=1, keepdims=True))
    loss = log_total - jnp.sum(jnp.where(hit, logits, 0.0), axis=1, keepdims=True)
    dlogits = (jnp.exp(logits - log_total) - jnp.where(hit, 1.0, 0.0)) * row_scale
    kept = up_to(classes, 16)
    out_ref[size : size + kept] = dlogits.T[:kept].astype(BF16)
    ordered = jnp.sum(jnp.where(place, loss, 0.0), axis=0, keepdims=True)
    piece = lax.broadcasted_iota(jnp.int32, (16, rows), 0)
    rest = ordered
    packed = jnp.zeros((16, rows), F32)
    for number in range(3):
        part = rest.astype(BF16).astype(F32)
        packed = jnp.where(piece == number, part, packed)
        rest = rest - part
    out_ref[size + kept :] = packed.astype(BF16)


def grad_kernel(
    kept, which_ref, b0_ref, b1_ref, b2_ref, last_ref, wq_ref, wt_ref, wc_ref, out_ref,
):
    group = last_ref.shape[0]
    width = b0_ref.shape[2]
    size = b0_ref.shape[1] // (last_ref.shape[2] // width)
    branches = []
    for b_ref in (b0_ref, b1_ref, b2_ref):
        branches.append(b_ref[...].reshape(group * b_ref.shape[1], width))
    last_rows = []
    for member in range(group):
        for number in range(last_ref.shape[2] // width):
            last_rows.append(last_ref[member, :size, number * width : (number + 1) * width])
    branches.append(jnp.concatenate(last_rows, axis=0))
    dlogits_t = jnp.concatenate(
        [last_ref[member, size : size + kept] for member in range(group)], axis=1
    )
    which = which_ref[0]
    chosen = branches[0]
    for number in range(1, len(branches)):
        chosen = jnp.where(which == number, branches[number], chosen)
    hidden = jnp.maximum(matmul(chosen, wq_ref[...]), 0.0).astype(BF16)
    class_t = matmul(dlogits_t, hidden).astype(BF16)
    for chunk in range(out_ref.shape[0]):
        out_ref[chunk, :kept] = class_t[:, chunk * LANES : (chunk + 1) * LANES]
    per_branch = out_ref.shape[0] // len(branches)
    for number, rows in enumerate(branches):
        live = matmul(wt_ref[number], rows, ((1,), (1,))) > 0.0
        dhidden_t = jnp.where(live, matmul(wc_ref[number], dlogits_t), 0.0).astype(BF16)
        branch_t = matmul(dhidden_t, rows).astype(BF16)
        for part in range(per_branch):
            out_ref[number * per_branch + part, kept:] = branch_t[
                part * LANES : (part + 1) * LANES
            ]


def sum_kernel(in_ref, out_ref):
    total = in_ref[0].astype(F32)
    for number in range(1, in_ref.shape[0]):
        total = total + in_ref[number].astype(F32)
    out_ref[...] = total.astype(BF16)


def out_kernel(kept, in_ref, branch_ref, class_ref):
    chunks = in_ref.shape[0]
    per_branch = chunks // branch_ref.shape[0]
    classes = class_ref.shape[1]
    for chunk in range(chunks):
        turned = in_ref[chunk].astype(F32).T
        class_ref[chunk * LANES : (chunk + 1) * LANES] = turned[:, :classes]
        part = chunk % per_branch
        branch_ref[chunk // per_branch, :, part * LANES : (part + 1) * LANES] = in_ref[
            chunk, kept:
        ].astype(F32).T


def body(
    features, tile_values, tile_dst, tile_src, tile_count, send_left, send_right,
    send_count, batch_order, labels, w_branch, w_class,
):
    block = tile_values.shape[1]
    nodes, width = features.shape
    local = nodes // block
    slots = send_left.shape[0]
    tiles = tile_values.shape[0]
    branches, _, hid = w_branch.shape
    cat, classes = w_class.shape
    dom = lax.axis_size("dom")
    shuf = lax.axis_size("shuf")
    mine = lax.axis_index("shuf")
    share = nodes // shuf
    own = hid // shuf
    own_class = cat // shuf
    kept = up_to(classes, 16)
    wide = up_to(classes, LANES)
    row_scale = 1.0 / math.sqrt(float(nodes * dom * shuf))
    blocks_f32 = jax.ShapeDtypeStruct((local, block, width), F32)
    slots_f32 = jax.ShapeDtypeStruct((slots, block, width), F32)
    rows_b16 = jax.ShapeDtypeStruct((nodes, width), BF16)
    logits_f32 = jax.ShapeDtypeStruct((nodes, wide), F32)

    label_all = lax.all_gather(labels, "shuf").reshape(shuf, shuf, share)
    label_mine = lax.dynamic_index_in_dim(label_all, mine, 1, keepdims=False).reshape(1, nodes)

    wc_wide = jnp.pad(w_class, ((0, 0), (0, wide - classes))).reshape(branches, hid, wide)
    wc_own = jnp.pad(
        lax.dynamic_slice_in_dim(w_class.reshape(branches, hid, classes), mine * own, own, 1),
        ((0, 0), (0, 0), (0, kept - classes)),
    )
    w_own_t = lax.dynamic_slice_in_dim(w_branch, mine * own, own, 2).transpose(0, 2, 1)
    which = (mine * own_class) // hid
    w_class_own = lax.dynamic_slice(
        w_branch, (which, 0, (mine * own_class) % hid), (1, width, own_class)
    )[0]

    current = features.reshape(local, block, width)
    to_left, to_right, rows = call(
        first_kernel,
        [slots_f32, slots_f32, rows_b16],
        [IN_SMEM] * 3 + [IN_VMEM],
        1000,
    )(send_left, send_right, send_count, current)
    gathered = []
    logits = None
    hop_flops = 12 * tiles * block * block * width
    forward_flops = 2 * nodes * hid * (width + wide)
    ext = pltpu.VMEM((local + 2 * slots, block, width), F32)
    for hop in range(HOPS):
        from_lower = passed_along(to_right, "dom", 1)
        from_upper = passed_along(to_left, "dom", -1)
        gathered.append(lax.all_gather(rows, "shuf"))
        if logits is None:
            logits = call(forward_kernel, logits_f32, [IN_VMEM] * 3, forward_flops)(
                rows, w_branch[hop], wc_wide[hop]
            )
        else:
            logits = call(forward_more_kernel, logits_f32, [IN_VMEM] * 4, forward_flops)(
                rows, w_branch[hop], wc_wide[hop], logits
            )
        if hop < HOPS - 1:
            current, to_left, to_right, rows = call(
                hop_kernel,
                [blocks_f32, slots_f32, slots_f32, rows_b16],
                [IN_SMEM] * 6 + [IN_VMEM] * 4,
                hop_flops,
                [ext],
            )(
                tile_dst, tile_src, tile_count, send_left, send_right, send_count,
                current, from_lower, from_upper, tile_values,
            )
    payload = call(
        functools.partial(last_kernel, classes, row_scale),
        jax.ShapeDtypeStruct((block + kept + 16, local * width), BF16),
        [IN_SMEM] * 3 + [IN_VMEM] * 9,
        hop_flops + forward_flops,
        [ext],
    )(
        tile_dst, tile_src, tile_count, current, from_lower, from_upper, tile_values,
        logits, w_branch[HOPS], wc_wide[HOPS], batch_order, label_mine,
    )
    last_all = lax.all_gather(payload, "shuf")
    loss_parts = lax.dynamic_slice(
        last_all, (0, block + kept, mine * share), (shuf, 3, share)
    ).astype(F32)
    loss_rows = (loss_parts[:, 0] + loss_parts[:, 1] + loss_parts[:, 2]).reshape(nodes)

    chunks = own_class // LANES
    height = kept + width
    grads = call(
        functools.partial(grad_kernel, kept),
        jax.ShapeDtypeStruct((chunks, height, LANES), BF16),
        [IN_SMEM] + [IN_VMEM] * 7,
        2 * shuf * nodes * own_class * (2 * width + 2 * wide + width),
    )(
        jnp.reshape(which, (1,)).astype(jnp.int32),
        *gathered, last_all, w_class_own, w_own_t, wc_own,
    )
    if chunks == dom:
        parts = lax.all_to_all(grads, "dom", split_axis=0, concat_axis=0, tiled=True)
        part = call(
            sum_kernel, jax.ShapeDtypeStruct((height, LANES), BF16), [IN_VMEM], 1000
        )(parts)
        summed = lax.all_gather(part, "dom")
    else:
        summed = lax.psum(grads.astype(F32), "dom")
    grad_branch, grad_class = call(
        functools.partial(out_kernel, kept),
        [
            jax.ShapeDtypeStruct((branches, width, own), F32),
            jax.ShapeDtypeStruct((own_class, classes), F32),
        ],
        [IN_VMEM],
        1000,
    )(summed)
    return (loss_rows, grad_branch, grad_class)


def solution(mesh):
    return jax.shard_map(
        body,
        mesh=mesh,
        in_specs=(
            P(("dom", "shuf"), None),
            P(("dom", "shuf"), None, None),
            P(("dom", "shuf")),
            P(("dom", "shuf")),
            P(("dom", "shuf")),
            P(("dom", "shuf")),
            P(("dom", "shuf")),
            P(("dom", "shuf"), None),
            P(("dom", "shuf"), None),
            P(("dom", "shuf")),
            P(),
            P(),
        ),
        out_specs=(P(("dom", "shuf")), P(None, None, "shuf"), P("shuf", None)),
        check_vma=False,
    )
```

```python
import functools
import math

import jax
import jax.numpy as jnp
from jax import lax
from jax.experimental import pallas as pl
from jax.experimental.pallas import tpu as pltpu
from jax.sharding import PartitionSpec as P

HOPS = 3
LANES = 128
VMEM_LIMIT = 24 * 1024 * 1024

IN_VMEM = pl.BlockSpec(memory_space=pltpu.VMEM)
IN_SMEM = pl.BlockSpec(memory_space=pltpu.SMEM)
BF16 = jnp.bfloat16
F32 = jnp.float32


def up_to(value, multiple):
    return -(-value // multiple) * multiple


def passed_along(value, axis, steps):
    count = lax.axis_size(axis)
    pairs = [(source, (source + steps) % count) for source in range(count)]
    return lax.ppermute(value, axis, pairs)


def matmul(left, right, dims=((1,), (0,)), precision=None):
    return lax.dot_general(
        left, right, (dims, ((), ())), precision=precision, preferred_element_type=F32
    )


def call(kernel, out_shape, in_specs, flops, scratch=()):
    many = isinstance(out_shape, (list, tuple))
    outs = out_shape if many else [out_shape]
    moved = sum(math.prod(one.shape) * one.dtype.itemsize for one in outs)
    return pl.pallas_call(
        kernel,
        out_shape=out_shape,
        in_specs=in_specs,
        out_specs=[IN_VMEM] * len(outs) if many else IN_VMEM,
        scratch_shapes=list(scratch),
        compiler_params=pltpu.CompilerParams(vmem_limit_bytes=VMEM_LIMIT),
        cost_estimate=pl.CostEstimate(
            flops=flops, bytes_accessed=3 * moved, transcendentals=0
        ),
    )


class Plan:
    def __init__(self, tiles, slots):
        self.tiles = tiles
        self.slots = slots
        self.dst = 0
        self.src = tiles
        self.count = 2 * tiles
        self.left = 2 * tiles + 1
        self.right = self.left + slots
        self.sent = self.right + slots


def write_sends(plan, plan_ref, blocks, left_ref, right_ref):
    for slot in range(plan.slots):
        for out_ref, ids, side in ((left_ref, plan.left, 0), (right_ref, plan.right, 1)):
            index = plan_ref[ids + slot]
            picked = blocks[0]
            for number in range(1, len(blocks)):
                picked = jnp.where(index == number, blocks[number], picked)
            out_ref[slot] = jnp.where(slot < plan_ref[plan.sent + side], picked, 0.0)


def first_kernel(plan, plan_ref, feat_ref, label_ref, left_ref, right_ref, b_ref):
    blocks = [feat_ref[number] for number in range(feat_ref.shape[0])]
    write_sends(plan, plan_ref, blocks, left_ref, right_ref)
    size = blocks[0].shape[0]
    for number, block in enumerate(blocks):
        b_ref[number * size : (number + 1) * size] = block.astype(BF16)
    width = b_ref.shape[1]
    nodes = label_ref.shape[1]
    per_piece = nodes // width
    place = lax.broadcasted_iota(jnp.int32, (16, width), 0)
    packed = jnp.zeros((16, width), F32)
    for piece in range(2):
        value = label_ref[...] & 255 if piece == 0 else label_ref[...] >> 8
        value = value.astype(F32)
        for part in range(per_piece):
            packed = jnp.where(
                place == piece * per_piece + part,
                value[:, part * width : (part + 1) * width],
                packed,
            )
    b_ref[nodes:] = packed.astype(BF16)


def next_blocks(plan, plan_ref, cur_ref, low_ref, high_ref, tiles_ref, ext_ref):
    local = cur_ref.shape[0]
    slots = low_ref.shape[0]
    ext_ref[:local] = cur_ref[...]
    ext_ref[local : local + slots] = low_ref[...]
    ext_ref[local + slots :] = high_ref[...]
    totals = [jnp.zeros(cur_ref.shape[1:], F32) for _ in range(local)]
    live = plan_ref[plan.count]
    for tile in range(plan.tiles):
        product = matmul(
            tiles_ref[tile],
            ext_ref[plan_ref[plan.src + tile]],
            precision=lax.Precision.HIGHEST,
        )
        wanted = jnp.where(tile < live, plan_ref[plan.dst + tile], -1)
        for number in range(local):
            totals[number] = totals[number] + jnp.where(wanted == number, product, 0.0)
    return totals


def hop_kernel(
    plan, plan_ref, cur_ref, low_ref, high_ref, tiles_ref,
    next_ref, left_ref, right_ref, b_ref, ext_ref,
):
    blocks = next_blocks(plan, plan_ref, cur_ref, low_ref, high_ref, tiles_ref, ext_ref)
    write_sends(plan, plan_ref, blocks, left_ref, right_ref)
    for number, block in enumerate(blocks):
        size = block.shape[0]
        next_ref[number] = block
        b_ref[number * size : (number + 1) * size] = block.astype(BF16)


def branch_logits(branch, rows, w_ref, wc_ref):
    hidden = jnp.maximum(matmul(rows, w_ref[branch]), 0.0).astype(BF16)
    hid = hidden.shape[1]
    return matmul(wc_ref[:, branch * hid : (branch + 1) * hid], hidden, ((1,), (1,)))


def forward_kernel(branch, cur_ref, w_ref, wc_ref, *refs):
    rows = cur_ref[...].reshape(-1, cur_ref.shape[2]).astype(BF16)
    part = branch_logits(branch, rows, w_ref, wc_ref)
    if len(refs) == 2:
        part = refs[0][...] + part
    refs[-1][...] = part


def last_kernel(
    plan, row_scale, plan_ref,
    cur_ref, low_ref, high_ref, tiles_ref, before_ref, w_ref, wc_ref, order_ref, label_ref,
    out_ref, ext_ref,
):
    blocks = next_blocks(plan, plan_ref, cur_ref, low_ref, high_ref, tiles_ref, ext_ref)
    halves = [block.astype(BF16) for block in blocks]
    rows_b = jnp.concatenate(halves, axis=0)
    size, width = halves[0].shape
    for number, half in enumerate(halves):
        out_ref[:size, number * width : (number + 1) * width] = half
    logits = before_ref[...] + branch_logits(w_ref.shape[0] - 1, rows_b, w_ref, wc_ref)
    classes, rows = logits.shape
    kept = up_to(classes, 16)
    place = (order_ref[...] == lax.broadcasted_iota(jnp.int32, (rows, rows), 0)).astype(F32)
    place = place.astype(BF16)
    pieces = matmul(label_ref[...], place, ((1,), (1,)))
    label = (pieces[0:1] + 256.0 * pieces[1:2]).astype(jnp.int32)
    hit = lax.broadcasted_iota(jnp.int32, (classes, rows), 0) == label
    top = jnp.max(logits, axis=0, keepdims=True)
    log_total = top + jnp.log(jnp.sum(jnp.exp(logits - top), axis=0, keepdims=True))
    loss = log_total - jnp.sum(jnp.where(hit, logits, 0.0), axis=0, keepdims=True)
    dlogits = (jnp.exp(logits - log_total) - jnp.where(hit, 1.0, 0.0)) * row_scale
    out_ref[size + kept - 16 : size + kept] = jnp.zeros((16, rows), BF16)
    out_ref[size : size + classes] = dlogits.astype(BF16)
    number = lax.broadcasted_iota(jnp.int32, (16, rows), 0)
    packed = jnp.zeros((16, rows), F32)
    rest = loss
    for piece in range(3):
        part = rest.astype(BF16).astype(F32)
        packed = jnp.where(number == piece, part, packed)
        rest = rest - part
    out_ref[size + kept :] = matmul(packed.astype(BF16), place).astype(BF16)


def weights_kernel(w_ref, wc_ref, wt_ref, wct_ref, pad_ref):
    branches, own, kept = wct_ref.shape
    classes = wc_ref.shape[0]
    hid = w_ref.shape[2]
    first = lax.axis_index("shuf") * own
    pad_ref[...] = jnp.zeros_like(pad_ref)
    for branch in range(branches):
        columns = w_ref[branch, :, pl.ds(pl.multiple_of(first, LANES), own)]
        wt_ref[branch] = columns.astype(F32).T.astype(BF16)
        columns = wc_ref[:, pl.ds(pl.multiple_of(branch * hid + first, LANES), own)]
        pad_ref[:classes] = columns.astype(F32)
        wct_ref[branch] = pad_ref[...].T[:, :kept].astype(BF16)


def all_chunks(kept, b0_ref, b1_ref, b2_ref, last_ref, w_ref, wt_ref, wct_ref, chunks_ref):
    group = last_ref.shape[0]
    branches, own, width = wt_ref.shape
    nodes = b1_ref.shape[1]
    hid = w_ref.shape[2]
    parts = last_ref.shape[2] // width
    size = nodes // parts
    all_rows = []
    for b_ref in (b0_ref, b1_ref, b2_ref):
        all_rows.append(
            jnp.concatenate([b_ref[member, :nodes] for member in range(group)], axis=0)
        )
    last_rows = []
    for member in range(group):
        for part in range(parts):
            last_rows.append(last_ref[member, :size, part * width : (part + 1) * width])
    all_rows.append(jnp.concatenate(last_rows, axis=0))
    dlogits_t = jnp.concatenate(
        [last_ref[member, size : size + kept] for member in range(group)], axis=1
    )
    own_class = branches * own
    first = lax.axis_index("shuf") * own_class
    which = first // hid
    columns = pl.ds(pl.multiple_of(first - which * hid, LANES), own_class)
    chosen = all_rows[0]
    for branch in range(1, branches):
        chosen = jnp.where(which == branch, all_rows[branch], chosen)
    hidden = jnp.maximum(matmul(chosen, w_ref[which, :, columns]), 0.0).astype(BF16)
    class_t = matmul(dlogits_t, hidden)
    for chunk in range(chunks_ref.shape[0]):
        chunks_ref[chunk, :kept] = class_t[:, chunk * LANES : (chunk + 1) * LANES]
    per_branch = chunks_ref.shape[0] // branches
    for branch, rows in enumerate(all_rows):
        live = matmul(wt_ref[branch], rows, ((1,), (1,))) > 0.0
        dhidden_t = jnp.where(live, matmul(wct_ref[branch], dlogits_t), 0.0).astype(BF16)
        branch_t = matmul(dhidden_t, rows)
        for part in range(per_branch):
            chunks_ref[branch * per_branch + part, kept:] = branch_t[
                part * LANES : (part + 1) * LANES
            ]


def grad_kernel(kept, *refs):
    ins, outs, chunks_ref = refs[:7], refs[7:-1], refs[-1]
    all_chunks(kept, *ins, chunks_ref)
    dom = lax.axis_index("dom")
    half = len(outs) // 2
    for step in range(half):
        stays = dom ^ (2 * step)
        outs[step][...] = chunks_ref[stays]
        outs[half + step][...] = chunks_ref[stays ^ 1].astype(BF16)


def write_chunk(kept, chunk, value, branch_ref, class_ref):
    per_branch = branch_ref.shape[2] // LANES
    start = pl.multiple_of(chunk * LANES, LANES)
    class_ref[:, pl.ds(start, LANES)] = value[: class_ref.shape[0]]
    branch = chunk // per_branch
    start = pl.multiple_of((chunk - branch * per_branch) * LANES, LANES)
    branch_ref[branch, :, pl.ds(start, LANES)] = value[kept:].T


def out_kernel(kept, *refs):
    ins, branch_ref, class_ref = refs[:-2], refs[-2], refs[-1]
    dom = lax.axis_index("dom")
    half = len(ins) // 2
    for step in range(half):
        for side in range(2):
            value = ins[side * half + step][...].astype(F32)
            write_chunk(kept, dom ^ (2 * step + side), value, branch_ref, class_ref)


def plain_out_kernel(kept, in_ref, branch_ref, class_ref):
    for chunk in range(in_ref.shape[0]):
        write_chunk(kept, chunk, in_ref[chunk], branch_ref, class_ref)


def swapped(value, distance):
    pairs = [(source, source ^ distance) for source in range(lax.axis_size("dom"))]
    return lax.ppermute(value, "dom", pairs)


def body(
    features, tile_values, tile_dst, tile_src, tile_count, send_left, send_right,
    send_count, batch_order, labels, w_branch, w_class,
):
    block = tile_values.shape[1]
    nodes, width = features.shape
    local = nodes // block
    slots = send_left.shape[0]
    tiles = tile_values.shape[0]
    branches, _, hid = w_branch.shape
    cat, classes = w_class.shape
    dom = lax.axis_size("dom")
    shuf = lax.axis_size("shuf")
    mine = lax.axis_index("shuf")
    share = nodes // shuf
    own = hid // shuf
    own_class = cat // shuf
    kept = up_to(classes, 16)
    row_scale = 1.0 / math.sqrt(float(nodes * dom * shuf))
    plan = Plan(tiles, slots)
    small = jnp.concatenate(
        [tile_dst, tile_src, tile_count, send_left, send_right, send_count.reshape(-1)]
    )
    blocks_f32 = jax.ShapeDtypeStruct((local, block, width), F32)
    slots_f32 = jax.ShapeDtypeStruct((slots, block, width), F32)
    rows_b16 = jax.ShapeDtypeStruct((nodes, width), BF16)
    first_b16 = jax.ShapeDtypeStruct((nodes + 16, width), BF16)
    logits_f32 = jax.ShapeDtypeStruct((classes, nodes), F32)
    w_class_t = w_class.T

    current = features.reshape(local, block, width)
    to_left, to_right, rows = call(
        functools.partial(first_kernel, plan),
        [slots_f32, slots_f32, first_b16],
        [IN_SMEM, IN_VMEM, IN_VMEM],
        1000,
    )(small, current, labels.reshape(1, nodes))
    gathered = []
    logits = []
    hop_flops = 12 * tiles * block * block * width
    forward_flops = 2 * nodes * hid * (width + classes)
    ext = pltpu.VMEM((local + 2 * slots, block, width), F32)
    for hop in range(HOPS):
        from_lower = passed_along(to_right, "dom", 1)
        from_upper = passed_along(to_left, "dom", -1)
        gathered.append(lax.all_gather(rows, "shuf"))
        logits = [
            call(
                functools.partial(forward_kernel, hop),
                logits_f32,
                [IN_VMEM] * (3 + len(logits)),
                forward_flops,
            )(current, w_branch, w_class_t, *logits)
        ]
        if hop < HOPS - 1:
            current, to_left, to_right, rows = call(
                functools.partial(hop_kernel, plan),
                [blocks_f32, slots_f32, slots_f32, rows_b16],
                [IN_SMEM] + [IN_VMEM] * 4,
                hop_flops,
                [ext],
            )(small, current, from_lower, from_upper, tile_values)

    pieces = gathered[0][:, nodes : nodes + 2 * nodes // width].reshape(shuf, 2, shuf, share)
    pieces = lax.dynamic_index_in_dim(pieces, mine, 2, keepdims=False)
    label_mine = jnp.pad(pieces.transpose(1, 0, 2).reshape(2, nodes), ((0, 14), (0, 0)))

    wt_own, wct_own = call(
        weights_kernel,
        [
            jax.ShapeDtypeStruct((branches, own, width), BF16),
            jax.ShapeDtypeStruct((branches, own, kept), BF16),
        ],
        [IN_VMEM] * 2,
        1000,
        [pltpu.VMEM((up_to(classes, LANES), own), F32)],
    )(w_branch, w_class_t)

    payload = call(
        functools.partial(last_kernel, plan, row_scale),
        jax.ShapeDtypeStruct((block + kept + 16, local * width), BF16),
        [IN_SMEM] + [IN_VMEM] * 9,
        hop_flops + forward_flops,
        [ext],
    )(
        small, current, from_lower, from_upper, tile_values,
        *logits, w_branch, w_class_t, batch_order, label_mine,
    )
    last_all = lax.all_gather(payload, "shuf")
    loss_parts = lax.dynamic_slice(
        last_all, (0, block + kept, mine * share), (shuf, 3, share)
    ).astype(F32)
    loss_rows = (loss_parts[:, 0] + loss_parts[:, 1] + loss_parts[:, 2]).reshape(nodes)

    chunks = own_class // LANES
    height = kept + width
    grad_flops = 2 * shuf * nodes * own_class * (3 * width + 2 * kept)
    grad_ins = (*gathered, last_all, w_branch, wt_own, wct_own)
    outs = [
        jax.ShapeDtypeStruct((branches, width, own), F32),
        jax.ShapeDtypeStruct((classes, own_class), F32),
    ]
    chunks_f32 = pltpu.VMEM((chunks, height, LANES), F32)
    if chunks == dom and dom % 2 == 0 and dom & (dom - 1) == 0:
        half = dom // 2
        one_f32 = jax.ShapeDtypeStruct((height, LANES), F32)
        one_b16 = jax.ShapeDtypeStruct((height, LANES), BF16)
        made = call(
            functools.partial(grad_kernel, kept),
            [one_f32] * half + [one_b16] * half,
            [IN_VMEM] * 7,
            grad_flops,
            [chunks_f32],
        )(*grad_ins)
        order = list(range(1, half)) + [0]
        arrived = {step: swapped(made[half + step], 1) for step in order}
        total = {step: made[step] + arrived[step].astype(F32) for step in order}
        far = [swapped(total[step].astype(BF16), 2 * step) for step in range(1, half)]
        summed = total[0]
        for value in far:
            summed = summed + value.astype(F32)
        near = [summed.astype(BF16)]
        for step in range(1, half):
            near.append(swapped(near[0], 2 * step))
        other = [swapped(value, 1) for value in near]
        grad_branch, grad_class_t = call(
            functools.partial(out_kernel, kept), outs, [IN_VMEM] * dom, 1000
        )(*near, *other)
    else:
        grads = call(
            functools.partial(all_chunks, kept),
            jax.ShapeDtypeStruct((chunks, height, LANES), F32),
            [IN_VMEM] * 7,
            grad_flops,
        )(*grad_ins)
        grad_branch, grad_class_t = call(
            functools.partial(plain_out_kernel, kept), outs, [IN_VMEM], 1000
        )(lax.psum(grads, "dom"))
    return (loss_rows, grad_branch, grad_class_t.T)


def solution(mesh):
    return jax.shard_map(
        body,
        mesh=mesh,
        in_specs=(
            P(("dom", "shuf"), None),
            P(("dom", "shuf"), None, None),
            P(("dom", "shuf")),
            P(("dom", "shuf")),
            P(("dom", "shuf")),
            P(("dom", "shuf")),
            P(("dom", "shuf")),
            P(("dom", "shuf"), None),
            P(("dom", "shuf"), None),
            P(("dom", "shuf")),
            P(),
            P(),
        ),
        out_specs=(P(("dom", "shuf")), P(None, None, "shuf"), P("shuf", None)),
        check_vma=False,
    )
```

```python
import functools
import math

import jax
import jax.numpy as jnp
from jax import lax
from jax.experimental import pallas as pl
from jax.experimental.pallas import tpu as pltpu
from jax.sharding import PartitionSpec as P

HOPS = 3
LANES = 128
VMEM_LIMIT = 24 * 1024 * 1024

IN_VMEM = pl.BlockSpec(memory_space=pltpu.VMEM)
IN_SMEM = pl.BlockSpec(memory_space=pltpu.SMEM)
BF16 = jnp.bfloat16
F32 = jnp.float32


def up_to(value, multiple):
    return -(-value // multiple) * multiple


def passed_along(value, axis, steps):
    count = lax.axis_size(axis)
    pairs = [(source, (source + steps) % count) for source in range(count)]
    return lax.ppermute(value, axis, pairs)


def matmul(left, right, dims=((1,), (0,)), precision=None):
    return lax.dot_general(
        left, right, (dims, ((), ())), precision=precision, preferred_element_type=F32
    )


def call(kernel, out_shape, in_specs, flops, scratch=()):
    many = isinstance(out_shape, (list, tuple))
    outs = out_shape if many else [out_shape]
    moved = sum(math.prod(one.shape) * one.dtype.itemsize for one in outs)
    return pl.pallas_call(
        kernel,
        out_shape=out_shape,
        in_specs=in_specs,
        out_specs=[IN_VMEM] * len(outs) if many else IN_VMEM,
        scratch_shapes=list(scratch),
        compiler_params=pltpu.CompilerParams(vmem_limit_bytes=VMEM_LIMIT),
        cost_estimate=pl.CostEstimate(
            flops=flops, bytes_accessed=3 * moved, transcendentals=0
        ),
    )


class Plan:
    def __init__(self, tiles, slots):
        self.tiles = tiles
        self.slots = slots
        self.dst = 0
        self.src = tiles
        self.count = 2 * tiles
        self.left = 2 * tiles + 1
        self.right = self.left + slots
        self.sent = self.right + slots


def write_sends(plan, plan_ref, blocks, left_ref, right_ref):
    for slot in range(plan.slots):
        for out_ref, ids, side in ((left_ref, plan.left, 0), (right_ref, plan.right, 1)):
            index = plan_ref[ids + slot]
            picked = blocks[0]
            for number in range(1, len(blocks)):
                picked = jnp.where(index == number, blocks[number], picked)
            out_ref[slot] = jnp.where(slot < plan_ref[plan.sent + side], picked, 0.0)


def first_kernel(plan, plan_ref, feat_ref, left_ref, right_ref, held_ref, sem):
    copy = pltpu.make_async_copy(feat_ref, held_ref, sem)
    copy.start()
    copy.wait()
    blocks = [held_ref[number] for number in range(held_ref.shape[0])]
    write_sends(plan, plan_ref, blocks, left_ref, right_ref)


def next_blocks(plan, plan_ref, cur_ref, low_ref, high_ref, tiles_ref, ext_ref):
    local = cur_ref.shape[0]
    slots = low_ref.shape[0]
    ext_ref[:local] = cur_ref[...]
    ext_ref[local : local + slots] = low_ref[...]
    ext_ref[local + slots :] = high_ref[...]
    totals = [jnp.zeros(cur_ref.shape[1:], F32) for _ in range(local)]
    live = plan_ref[plan.count]
    for tile in range(plan.tiles):
        product = matmul(
            tiles_ref[tile],
            ext_ref[plan_ref[plan.src + tile]],
            precision=lax.Precision.HIGHEST,
        )
        wanted = jnp.where(tile < live, plan_ref[plan.dst + tile], -1)
        for number in range(local):
            totals[number] = totals[number] + jnp.where(wanted == number, product, 0.0)
    return totals


def hop_kernel(
    plan, plan_ref, cur_ref, low_ref, high_ref, tiles_ref,
    next_ref, left_ref, right_ref, ext_ref,
):
    blocks = next_blocks(plan, plan_ref, cur_ref, low_ref, high_ref, tiles_ref, ext_ref)
    write_sends(plan, plan_ref, blocks, left_ref, right_ref)
    for number, block in enumerate(blocks):
        next_ref[number] = block


def branch_logits(branch, rows, w_ref, wc_ref):
    hidden = jnp.maximum(matmul(rows, w_ref[branch]), 0.0).astype(BF16)
    hid = hidden.shape[1]
    return matmul(wc_ref[:, branch * hid : (branch + 1) * hid], hidden, ((1,), (1,)))


def forward_kernel(branch, cur_ref, w_ref, wc_ref, *refs):
    rows = cur_ref[...].reshape(-1, cur_ref.shape[2]).astype(BF16)
    part = branch_logits(branch, rows, w_ref, wc_ref)
    if len(refs) == 3:
        part = refs[0][...] + part
    refs[-2][...] = part
    refs[-1][...] = rows


def forward_first_kernel(cur_ref, w_ref, wc_ref, label_ref, tiles_ref, part_ref, b_ref):
    nodes = label_ref.shape[1]
    forward_kernel(0, cur_ref, w_ref, wc_ref, part_ref, b_ref.at[:nodes])
    width = b_ref.shape[1]
    per_piece = nodes // width
    place = lax.broadcasted_iota(jnp.int32, (16, width), 0)
    packed = jnp.zeros((16, width), F32)
    for piece in range(2):
        value = label_ref[...] & 255 if piece == 0 else label_ref[...] >> 8
        value = value.astype(F32)
        for part in range(per_piece):
            packed = jnp.where(
                place == piece * per_piece + part,
                value[:, part * width : (part + 1) * width],
                packed,
            )
    b_ref[nodes:] = packed.astype(BF16)


def places(order_ref):
    nodes = order_ref.shape[1]
    rows = lax.broadcasted_iota(jnp.int32, (nodes, nodes), 0)
    return (order_ref[...] == rows).astype(F32).astype(BF16)


def label_kernel(order_ref, *refs):
    nodes = order_ref.shape[1]
    group = len(refs) - 1
    share = nodes // group
    mine = lax.axis_index("shuf")
    width = refs[0].shape[1]
    per_piece = nodes // width
    ordered = [jnp.zeros((1, nodes), F32) for _ in range(2)]
    for step in range(group):
        tail = refs[step][nodes:]
        away = ((mine ^ step) - mine) * share
        for part in range(per_piece):
            source = lax.broadcasted_iota(jnp.int32, (width, nodes), 0) + part * width
            target = lax.broadcasted_iota(jnp.int32, (width, nodes), 1)
            first = mine * share
            wanted = (target == source + away) & (source >= first) & (source < first + share)
            moved = matmul(tail, wanted.astype(F32).astype(BF16))
            for piece in range(2):
                row = piece * per_piece + part
                ordered[piece] = ordered[piece] + moved[row : row + 1]
    number = lax.broadcasted_iota(jnp.int32, (16, nodes), 0)
    packed = jnp.where(number == 0, ordered[0], jnp.where(number == 1, ordered[1], 0.0))
    pieces = matmul(packed.astype(BF16), places(order_ref), ((1,), (1,)))
    refs[-1][...] = (pieces[0:1] + 256.0 * pieces[1:2]).astype(jnp.int32)


def last_kernel(
    plan, row_scale, plan_ref,
    cur_ref, low_ref, high_ref, tiles_ref, before_ref, w_ref, wc_ref, order_ref, label_ref,
    out_ref, ext_ref,
):
    blocks = next_blocks(plan, plan_ref, cur_ref, low_ref, high_ref, tiles_ref, ext_ref)
    halves = [block.astype(BF16) for block in blocks]
    rows_b = jnp.concatenate(halves, axis=0)
    size, width = halves[0].shape
    for number, half in enumerate(halves):
        out_ref[:size, number * width : (number + 1) * width] = half
    logits = before_ref[...] + branch_logits(w_ref.shape[0] - 1, rows_b, w_ref, wc_ref)
    classes, rows = logits.shape
    kept = up_to(classes, 16)
    hit = lax.broadcasted_iota(jnp.int32, (classes, rows), 0) == label_ref[...]
    top = jnp.max(logits, axis=0, keepdims=True)
    log_total = top + jnp.log(jnp.sum(jnp.exp(logits - top), axis=0, keepdims=True))
    loss = log_total - jnp.sum(jnp.where(hit, logits, 0.0), axis=0, keepdims=True)
    dlogits = (jnp.exp(logits - log_total) - jnp.where(hit, 1.0, 0.0)) * row_scale
    out_ref[size + kept - 16 : size + kept] = jnp.zeros((16, rows), BF16)
    out_ref[size : size + classes] = dlogits.astype(BF16)
    number = lax.broadcasted_iota(jnp.int32, (16, rows), 0)
    packed = jnp.zeros((16, rows), F32)
    rest = loss
    for piece in range(3):
        part = rest.astype(BF16).astype(F32)
        packed = jnp.where(number == piece, part, packed)
        rest = rest - part
    out_ref[size + kept :] = matmul(packed.astype(BF16), places(order_ref)).astype(BF16)


def weights_kernel(w_ref, wc_ref, wt_ref, wct_ref, pad_ref):
    branches, own, kept = wct_ref.shape
    classes = wc_ref.shape[0]
    hid = w_ref.shape[2]
    first = lax.axis_index("shuf") * own
    pad_ref[...] = jnp.zeros_like(pad_ref)
    for branch in range(branches):
        columns = w_ref[branch, :, pl.ds(pl.multiple_of(first, LANES), own)]
        wt_ref[branch] = columns.astype(F32).T.astype(BF16)
        columns = wc_ref[:, pl.ds(pl.multiple_of(branch * hid + first, LANES), own)]
        pad_ref[:classes] = columns.astype(F32)
        wct_ref[branch] = pad_ref[...].T[:, :kept].astype(BF16)


def all_chunks(kept, row_refs, last_ref, w_ref, wt_ref, wct_ref, chunks_ref):
    group = last_ref.shape[0]
    branches, own, width = wt_ref.shape
    nodes = row_refs[-1].shape[0]
    hid = w_ref.shape[2]
    parts = last_ref.shape[2] // width
    size = nodes // parts
    mine = lax.axis_index("shuf")
    all_rows = []
    for branch in range(branches - 1):
        ours = row_refs[branch * group : (branch + 1) * group]
        all_rows.append(jnp.concatenate([ref[:nodes] for ref in ours], axis=0))
    last_rows = []
    for step in range(group):
        for part in range(parts):
            last_rows.append(last_ref[mine ^ step, :size, part * width : (part + 1) * width])
    all_rows.append(jnp.concatenate(last_rows, axis=0))
    dlogits_t = jnp.concatenate(
        [last_ref[mine ^ step, size : size + kept] for step in range(group)], axis=1
    )
    own_class = branches * own
    first = lax.axis_index("shuf") * own_class
    which = first // hid
    columns = pl.ds(pl.multiple_of(first - which * hid, LANES), own_class)
    chosen = all_rows[0]
    for branch in range(1, branches):
        chosen = jnp.where(which == branch, all_rows[branch], chosen)
    hidden = jnp.maximum(matmul(chosen, w_ref[which, :, columns]), 0.0).astype(BF16)
    class_t = matmul(dlogits_t, hidden)
    for chunk in range(chunks_ref.shape[0]):
        chunks_ref[chunk, :kept] = class_t[:, chunk * LANES : (chunk + 1) * LANES]
    per_branch = chunks_ref.shape[0] // branches
    for branch, rows in enumerate(all_rows):
        live = matmul(wt_ref[branch], rows, ((1,), (1,))) > 0.0
        dhidden_t = jnp.where(live, matmul(wct_ref[branch], dlogits_t), 0.0).astype(BF16)
        branch_t = matmul(dhidden_t, rows)
        for part in range(per_branch):
            chunks_ref[branch * per_branch + part, kept:] = branch_t[
                part * LANES : (part + 1) * LANES
            ]


def grad_kernel(kept, row_count, half, *refs):
    outs = refs[row_count + 4 : -1]
    chunks_ref = refs[-1]
    all_chunks(kept, refs[:row_count], *refs[row_count : row_count + 4], chunks_ref)
    dom = lax.axis_index("dom")
    for step in range(half):
        stays = dom ^ (2 * step)
        outs[step][...] = chunks_ref[stays]
        outs[half + step // 2][step % 2] = chunks_ref[stays ^ 1].astype(BF16)


def plain_grad_kernel(kept, row_count, *refs):
    all_chunks(kept, refs[:row_count], *refs[row_count:])


def write_chunk(kept, chunk, value, branch_ref, class_ref):
    per_branch = branch_ref.shape[2] // LANES
    start = pl.multiple_of(chunk * LANES, LANES)
    class_ref[:, pl.ds(start, LANES)] = value[: class_ref.shape[0]]
    branch = chunk // per_branch
    start = pl.multiple_of((chunk - branch * per_branch) * LANES, LANES)
    branch_ref[branch, :, pl.ds(start, LANES)] = value[kept:].T


def out_kernel(kept, *refs):
    ins, branch_ref, class_ref = refs[:-2], refs[-2], refs[-1]
    dom = lax.axis_index("dom")
    half = len(ins) // 2
    for step in range(half):
        for side in range(2):
            value = ins[side * half + step][...].astype(F32)
            write_chunk(kept, dom ^ (2 * step + side), value, branch_ref, class_ref)


def plain_out_kernel(kept, in_ref, branch_ref, class_ref):
    for chunk in range(in_ref.shape[0]):
        write_chunk(kept, chunk, in_ref[chunk], branch_ref, class_ref)


def swapped(value, distance, axis="dom"):
    pairs = [(source, source ^ distance) for source in range(lax.axis_size(axis))]
    return lax.ppermute(value, axis, pairs)


def in_group(value):
    members = [value]
    distance = lax.axis_size("shuf") // 2
    while distance:
        members += [swapped(member, distance, "shuf") for member in members]
        distance //= 2
    count = len(members)
    steps = [0]
    distance = count // 2
    while distance:
        steps += [step + distance for step in steps]
        distance //= 2
    return [members[steps.index(step)] for step in range(count)]


def body(
    features, tile_values, tile_dst, tile_src, tile_count, send_left, send_right,
    send_count, batch_order, labels, w_branch, w_class,
):
    block = tile_values.shape[1]
    nodes, width = features.shape
    local = nodes // block
    slots = send_left.shape[0]
    tiles = tile_values.shape[0]
    branches, _, hid = w_branch.shape
    cat, classes = w_class.shape
    dom = lax.axis_size("dom")
    shuf = lax.axis_size("shuf")
    mine = lax.axis_index("shuf")
    share = nodes // shuf
    own = hid // shuf
    own_class = cat // shuf
    kept = up_to(classes, 16)
    row_scale = 1.0 / math.sqrt(float(nodes * dom * shuf))
    plan = Plan(tiles, slots)
    small = jnp.concatenate(
        [tile_dst, tile_src, tile_count, send_left, send_right, send_count.reshape(-1)]
    )
    blocks_f32 = jax.ShapeDtypeStruct((local, block, width), F32)
    slots_f32 = jax.ShapeDtypeStruct((slots, block, width), F32)
    rows_b16 = jax.ShapeDtypeStruct((nodes, width), BF16)
    first_b16 = jax.ShapeDtypeStruct((nodes + 16, width), BF16)
    logits_f32 = jax.ShapeDtypeStruct((classes, nodes), F32)
    w_class_t = w_class.T

    current = features.reshape(local, block, width)
    to_left, to_right = call(
        functools.partial(first_kernel, plan),
        [slots_f32, slots_f32],
        [IN_SMEM, pl.BlockSpec(memory_space=pl.ANY)],
        1000,
        [pltpu.VMEM((local, block, width), F32), pltpu.SemaphoreType.DMA],
    )(small, current)
    gathered = []
    logits = None
    hop_flops = 12 * tiles * block * block * width
    forward_flops = 2 * nodes * hid * (width + classes)
    ext = pltpu.VMEM((local + 2 * slots, block, width), F32)
    for hop in range(HOPS):
        from_lower = passed_along(to_right, "dom", 1)
        from_upper = passed_along(to_left, "dom", -1)
        if hop == 0:
            logits, rows = call(
                forward_first_kernel, [logits_f32, first_b16], [IN_VMEM] * 5, forward_flops
            )(current, w_branch, w_class_t, labels.reshape(1, nodes), tile_values)
        else:
            logits, rows = call(
                functools.partial(forward_kernel, hop),
                [logits_f32, rows_b16],
                [IN_VMEM] * 4,
                forward_flops,
            )(current, w_branch, w_class_t, logits)
        gathered += in_group(rows)
        if hop < HOPS - 1:
            current, to_left, to_right = call(
                functools.partial(hop_kernel, plan),
                [blocks_f32, slots_f32, slots_f32],
                [IN_SMEM] + [IN_VMEM] * 4,
                hop_flops,
                [ext],
            )(small, current, from_lower, from_upper, tile_values)

    label_mine = call(
        label_kernel,
        jax.ShapeDtypeStruct((1, nodes), jnp.int32),
        [IN_VMEM] * (1 + shuf),
        1000,
    )(batch_order, *gathered[:shuf])

    wt_own, wct_own = call(
        weights_kernel,
        [
            jax.ShapeDtypeStruct((branches, own, width), BF16),
            jax.ShapeDtypeStruct((branches, own, kept), BF16),
        ],
        [IN_VMEM] * 2,
        1000,
        [pltpu.VMEM((up_to(classes, LANES), own), F32)],
    )(w_branch, w_class_t)

    payload = call(
        functools.partial(last_kernel, plan, row_scale),
        jax.ShapeDtypeStruct((block + kept + 16, local * width), BF16),
        [IN_SMEM] + [IN_VMEM] * 9,
        hop_flops + forward_flops,
        [ext],
    )(
        small, current, from_lower, from_upper, tile_values,
        logits, w_branch, w_class_t, batch_order, label_mine,
    )
    last_all = lax.all_gather(payload, "shuf")
    loss_parts = lax.dynamic_slice(
        last_all, (0, block + kept, mine * share), (shuf, 3, share)
    ).astype(F32)
    loss_rows = (loss_parts[:, 0] + loss_parts[:, 1] + loss_parts[:, 2]).reshape(nodes)

    chunks = own_class // LANES
    height = kept + width
    grad_flops = 2 * shuf * nodes * own_class * (3 * width + 2 * kept)
    grad_ins = (*gathered, last_all, w_branch, wt_own, wct_own)
    outs = [
        jax.ShapeDtypeStruct((branches, width, own), F32),
        jax.ShapeDtypeStruct((classes, own_class), F32),
    ]
    chunks_f32 = pltpu.VMEM((chunks, height, LANES), F32)
    if chunks == dom and dom % 4 == 0 and dom & (dom - 1) == 0:
        half = dom // 2
        one_f32 = jax.ShapeDtypeStruct((height, LANES), F32)
        two_b16 = jax.ShapeDtypeStruct((2, height, LANES), BF16)
        made = call(
            functools.partial(grad_kernel, kept, len(gathered), half),
            [one_f32] * half + [two_b16] * (half // 2),
            [IN_VMEM] * len(grad_ins),
            grad_flops,
            [chunks_f32],
        )(*grad_ins)
        order = list(range(half - 1, -1, -1))
        arrived = {pair: swapped(made[half + pair], 1) for pair in range(half // 2 - 1, -1, -1)}
        total = {
            step: made[step] + arrived[step // 2][step % 2].astype(F32) for step in order
        }
        far = [swapped(total[step].astype(BF16), 2 * step) for step in order[:-1]]
        summed = total[0]
        for value in far:
            summed = summed + value.astype(F32)
        near = {0: summed.astype(BF16)}
        other = {0: swapped(near[0], 1)}
        for step in order[:-1]:
            near[step] = swapped(near[0], 2 * step)
        for step in range(1, half):
            other[step] = swapped(near[step], 1)
        near = [near[step] for step in range(half)]
        other = [other[step] for step in range(half)]
        grad_branch, grad_class_t = call(
            functools.partial(out_kernel, kept), outs, [IN_VMEM] * dom, 1000
        )(*near, *other)
    else:
        grads = call(
            functools.partial(plain_grad_kernel, kept, len(gathered)),
            jax.ShapeDtypeStruct((chunks, height, LANES), F32),
            [IN_VMEM] * len(grad_ins),
            grad_flops,
        )(*grad_ins)
        grad_branch, grad_class_t = call(
            functools.partial(plain_out_kernel, kept), outs, [IN_VMEM], 1000
        )(lax.psum(grads, "dom"))
    return (loss_rows, grad_branch, grad_class_t.T)


def solution(mesh):
    return jax.shard_map(
        body,
        mesh=mesh,
        in_specs=(
            P(("dom", "shuf"), None),
            P(("dom", "shuf"), None, None),
            P(("dom", "shuf")),
            P(("dom", "shuf")),
            P(("dom", "shuf")),
            P(("dom", "shuf")),
            P(("dom", "shuf")),
            P(("dom", "shuf"), None),
            P(("dom", "shuf"), None),
            P(("dom", "shuf")),
            P(),
            P(),
        ),
        out_specs=(P(("dom", "shuf")), P(None, None, "shuf"), P("shuf", None)),
        check_vma=False,
    )
```

```python
import functools
import math

import jax
import jax.numpy as jnp
from jax import lax
from jax.experimental import pallas as pl
from jax.experimental.pallas import tpu as pltpu
from jax.sharding import PartitionSpec as P

HOPS = 3
LANES = 128
VMEM_LIMIT = 24 * 1024 * 1024

IN_VMEM = pl.BlockSpec(memory_space=pltpu.VMEM)
IN_SMEM = pl.BlockSpec(memory_space=pltpu.SMEM)
BF16 = jnp.bfloat16
F32 = jnp.float32


def up_to(value, multiple):
    return -(-value // multiple) * multiple


def passed_along(value, axis, steps):
    count = lax.axis_size(axis)
    pairs = [(source, (source + steps) % count) for source in range(count)]
    return lax.ppermute(value, axis, pairs)


def matmul(left, right, dims=((1,), (0,)), precision=None):
    return lax.dot_general(
        left, right, (dims, ((), ())), precision=precision, preferred_element_type=F32
    )


def call(kernel, out_shape, in_specs, flops, scratch=(), after=()):
    many = isinstance(out_shape, (list, tuple))
    outs = out_shape if many else [out_shape]
    moved = sum(math.prod(one.shape) * one.dtype.itemsize for one in outs)
    waited = len(after)

    def run(*refs):
        kernel(*refs[waited:])

    made = pl.pallas_call(
        run,
        out_shape=out_shape,
        in_specs=[pl.BlockSpec(memory_space=pl.ANY)] * waited + in_specs,
        out_specs=[IN_VMEM] * len(outs) if many else IN_VMEM,
        scratch_shapes=list(scratch),
        compiler_params=pltpu.CompilerParams(vmem_limit_bytes=VMEM_LIMIT),
        cost_estimate=pl.CostEstimate(
            flops=flops, bytes_accessed=3 * moved, transcendentals=0
        ),
    )
    return functools.partial(made, *after)


class Plan:
    def __init__(self, tiles, slots):
        self.tiles = tiles
        self.slots = slots
        self.dst = 0
        self.src = tiles
        self.count = 2 * tiles
        self.left = 2 * tiles + 1
        self.right = self.left + slots
        self.sent = self.right + slots


def write_sends(plan, plan_ref, blocks, left_ref, right_ref):
    for slot in range(plan.slots):
        for out_ref, ids, side in ((left_ref, plan.left, 0), (right_ref, plan.right, 1)):
            index = plan_ref[ids + slot]
            picked = blocks[0]
            for number in range(1, len(blocks)):
                picked = jnp.where(index == number, blocks[number], picked)
            out_ref[slot] = jnp.where(slot < plan_ref[plan.sent + side], picked, 0.0)


def next_blocks(plan, plan_ref, cur_ref, tiles_ref, ext_ref):
    local = cur_ref.shape[0]
    ext_ref[:local] = cur_ref[...]
    totals = [jnp.zeros(cur_ref.shape[1:], F32) for _ in range(local)]
    live = plan_ref[plan.count]
    for tile in range(plan.tiles):
        product = matmul(
            tiles_ref[tile],
            ext_ref[plan_ref[plan.src + tile]],
            precision=lax.Precision.HIGHEST,
        )
        wanted = jnp.where(tile < live, plan_ref[plan.dst + tile], -1)
        for number in range(local):
            totals[number] = totals[number] + jnp.where(wanted == number, product, 0.0)
    return totals


def extend(cur_ref, low_ref, high_ref, ext_ref):
    local = cur_ref.shape[0]
    slots = low_ref.shape[0]
    ext_ref[local : local + slots] = low_ref[...]
    ext_ref[local + slots :] = high_ref[...]


def write_hop(plan, plan_ref, cur_ref, tiles_ref, next_ref, left_ref, right_ref, ext_ref):
    blocks = next_blocks(plan, plan_ref, cur_ref, tiles_ref, ext_ref)
    write_sends(plan, plan_ref, blocks, left_ref, right_ref)
    for number, block in enumerate(blocks):
        next_ref[number] = block


def first_hop_kernel(
    plan, plan_ref, low_plan_ref, high_plan_ref, cur_ref, low_ref, high_ref, tiles_ref,
    next_ref, left_ref, right_ref, ext_ref,
):
    local = cur_ref.shape[0]
    for slot in range(plan.slots):
        low = low_ref[low_plan_ref[plan.right + slot]]
        high = high_ref[high_plan_ref[plan.left + slot]]
        live_low = slot < low_plan_ref[plan.sent + 1]
        live_high = slot < high_plan_ref[plan.sent]
        ext_ref[local + slot] = jnp.where(live_low, low, 0.0)
        ext_ref[local + plan.slots + slot] = jnp.where(live_high, high, 0.0)
    write_hop(plan, plan_ref, cur_ref, tiles_ref, next_ref, left_ref, right_ref, ext_ref)


def hop_kernel(
    plan, plan_ref, cur_ref, low_ref, high_ref, tiles_ref,
    next_ref, left_ref, right_ref, ext_ref,
):
    extend(cur_ref, low_ref, high_ref, ext_ref)
    write_hop(plan, plan_ref, cur_ref, tiles_ref, next_ref, left_ref, right_ref, ext_ref)


def branch_logits(branch, rows, w_ref, wc_ref):
    hidden = jnp.maximum(matmul(rows, w_ref[branch]), 0.0).astype(BF16)
    hid = hidden.shape[1]
    return matmul(wc_ref[:, branch * hid : (branch + 1) * hid], hidden, ((1,), (1,)))


def forward_kernel(branch, cur_ref, w_ref, wc_ref, *refs):
    rows = cur_ref[...].reshape(-1, cur_ref.shape[2]).astype(BF16)
    part = branch_logits(branch, rows, w_ref, wc_ref)
    if len(refs) == 3:
        part = refs[0][...] + part
    refs[-2][...] = part
    refs[-1][...] = rows


def forward_first_kernel(cur_ref, w_ref, wc_ref, label_ref, tiles_ref, part_ref, b_ref):
    nodes = label_ref.shape[1]
    forward_kernel(0, cur_ref, w_ref, wc_ref, part_ref, b_ref.at[:nodes])
    width = b_ref.shape[1]
    per_piece = nodes // width
    place = lax.broadcasted_iota(jnp.int32, (16, width), 0)
    packed = jnp.zeros((16, width), F32)
    for piece in range(2):
        value = label_ref[...] & 255 if piece == 0 else label_ref[...] >> 8
        value = value.astype(F32)
        for part in range(per_piece):
            packed = jnp.where(
                place == piece * per_piece + part,
                value[:, part * width : (part + 1) * width],
                packed,
            )
    b_ref[nodes:] = packed.astype(BF16)


def places(order_ref):
    nodes = order_ref.shape[1]
    rows = lax.broadcasted_iota(jnp.int32, (nodes, nodes), 0)
    return (order_ref[...] == rows).astype(F32).astype(BF16)


def wanted_places(nodes, group, step, offset, count):
    share = nodes // group
    mine = lax.axis_index("shuf")
    first = mine * share
    source = lax.broadcasted_iota(jnp.int32, (count, nodes), 0) + offset
    target = lax.broadcasted_iota(jnp.int32, (count, nodes), 1)
    moved = source + ((mine ^ step) - mine) * share
    wanted = (target == moved) & (source >= first) & (source < first + share)
    return wanted.astype(F32).astype(BF16)


def label_kernel(order_ref, *refs):
    nodes = order_ref.shape[1]
    group = len(refs) - 1
    width = refs[0].shape[1]
    per_piece = nodes // width
    ordered = [jnp.zeros((1, nodes), F32) for _ in range(2)]
    for step in range(group):
        tail = refs[step][nodes:]
        for part in range(per_piece):
            moved = matmul(tail, wanted_places(nodes, group, step, part * width, width))
            for piece in range(2):
                row = piece * per_piece + part
                ordered[piece] = ordered[piece] + moved[row : row + 1]
    number = lax.broadcasted_iota(jnp.int32, (16, nodes), 0)
    packed = jnp.where(number == 0, ordered[0], jnp.where(number == 1, ordered[1], 0.0))
    pieces = matmul(packed.astype(BF16), places(order_ref), ((1,), (1,)))
    refs[-1][...] = (pieces[0:1] + 256.0 * pieces[1:2]).astype(jnp.int32)


def loss_kernel(*refs):
    group = len(refs) - 1
    height, nodes = refs[0].shape
    total = jnp.zeros((16, nodes), F32)
    for step in range(group):
        wanted = wanted_places(nodes, group, step, 0, nodes)
        total = total + matmul(refs[step][height - 16 :], wanted)
    refs[-1][...] = total[0:1] + total[1:2] + total[2:3]


def last_kernel(
    plan, row_scale, plan_ref,
    cur_ref, low_ref, high_ref, tiles_ref, before_ref, w_ref, wc_ref, order_ref, label_ref,
    out_ref, ext_ref,
):
    extend(cur_ref, low_ref, high_ref, ext_ref)
    blocks = next_blocks(plan, plan_ref, cur_ref, tiles_ref, ext_ref)
    halves = [block.astype(BF16) for block in blocks]
    rows_b = jnp.concatenate(halves, axis=0)
    size, width = halves[0].shape
    for number, half in enumerate(halves):
        out_ref[:size, number * width : (number + 1) * width] = half
    logits = before_ref[...] + branch_logits(w_ref.shape[0] - 1, rows_b, w_ref, wc_ref)
    classes, rows = logits.shape
    kept = up_to(classes, 16)
    hit = lax.broadcasted_iota(jnp.int32, (classes, rows), 0) == label_ref[...]
    top = jnp.max(logits, axis=0, keepdims=True)
    log_total = top + jnp.log(jnp.sum(jnp.exp(logits - top), axis=0, keepdims=True))
    loss = log_total - jnp.sum(jnp.where(hit, logits, 0.0), axis=0, keepdims=True)
    dlogits = (jnp.exp(logits - log_total) - jnp.where(hit, 1.0, 0.0)) * row_scale
    out_ref[size + kept - 16 : size + kept] = jnp.zeros((16, rows), BF16)
    out_ref[size : size + classes] = dlogits.astype(BF16)
    number = lax.broadcasted_iota(jnp.int32, (16, rows), 0)
    packed = jnp.zeros((16, rows), F32)
    rest = loss
    for piece in range(3):
        part = rest.astype(BF16).astype(F32)
        packed = jnp.where(number == piece, part, packed)
        rest = rest - part
    out_ref[size + kept :] = matmul(packed.astype(BF16), places(order_ref)).astype(BF16)


def weights_kernel(w_ref, wc_ref, wt_ref, wct_ref, pad_ref):
    branches, own, kept = wct_ref.shape
    classes = wc_ref.shape[0]
    hid = w_ref.shape[2]
    first = lax.axis_index("shuf") * own
    pad_ref[...] = jnp.zeros_like(pad_ref)
    for branch in range(branches):
        columns = w_ref[branch, :, pl.ds(pl.multiple_of(first, LANES), own)]
        wt_ref[branch] = columns.astype(F32).T.astype(BF16)
        columns = wc_ref[:, pl.ds(pl.multiple_of(branch * hid + first, LANES), own)]
        pad_ref[:classes] = columns.astype(F32)
        wct_ref[branch] = pad_ref[...].T[:, :kept].astype(BF16)


def all_chunks(kept, row_refs, last_refs, w_ref, wt_ref, wct_ref, chunks_ref):
    group = len(last_refs)
    branches, own, width = wt_ref.shape
    nodes = row_refs[-1].shape[0]
    hid = w_ref.shape[2]
    parts = last_refs[0].shape[1] // width
    size = nodes // parts
    all_rows = []
    for branch in range(branches - 1):
        ours = row_refs[branch * group : (branch + 1) * group]
        all_rows.append(jnp.concatenate([ref[:nodes] for ref in ours], axis=0))
    last_rows = []
    for ref in last_refs:
        for part in range(parts):
            last_rows.append(ref[:size, part * width : (part + 1) * width])
    all_rows.append(jnp.concatenate(last_rows, axis=0))
    dlogits_t = jnp.concatenate([ref[size : size + kept] for ref in last_refs], axis=1)
    own_class = branches * own
    first = lax.axis_index("shuf") * own_class
    which = first // hid
    columns = pl.ds(pl.multiple_of(first - which * hid, LANES), own_class)
    chosen = all_rows[0]
    for branch in range(1, branches):
        chosen = jnp.where(which == branch, all_rows[branch], chosen)
    hidden = jnp.maximum(matmul(chosen, w_ref[which, :, columns]), 0.0).astype(BF16)
    class_t = matmul(dlogits_t, hidden)
    for chunk in range(chunks_ref.shape[0]):
        chunks_ref[chunk, :kept] = class_t[:, chunk * LANES : (chunk + 1) * LANES]
    per_branch = chunks_ref.shape[0] // branches
    for branch, rows in enumerate(all_rows):
        live = matmul(wt_ref[branch], rows, ((1,), (1,))) > 0.0
        dhidden_t = jnp.where(live, matmul(wct_ref[branch], dlogits_t), 0.0).astype(BF16)
        branch_t = matmul(dhidden_t, rows)
        for part in range(per_branch):
            chunks_ref[branch * per_branch + part, kept:] = branch_t[
                part * LANES : (part + 1) * LANES
            ]


def grad_kernel(kept, group, row_count, half, *refs):
    ins = row_count + group + 3
    outs = refs[ins:-1]
    chunks_ref = refs[-1]
    plain_grad_kernel(kept, group, row_count, *refs[:ins], chunks_ref)
    dom = lax.axis_index("dom")
    for step in range(half):
        stays = dom ^ (2 * step)
        outs[step][...] = chunks_ref[stays]
        outs[half + step // 2][step % 2] = chunks_ref[stays ^ 1].astype(BF16)


def plain_grad_kernel(kept, group, row_count, *refs):
    last = row_count + group
    all_chunks(kept, refs[:row_count], refs[row_count:last], *refs[last:])


def write_chunk(kept, chunk, value, branch_ref, class_ref):
    per_branch = branch_ref.shape[2] // LANES
    start = pl.multiple_of(chunk * LANES, LANES)
    class_ref[:, pl.ds(start, LANES)] = value[: class_ref.shape[0]]
    branch = chunk // per_branch
    start = pl.multiple_of((chunk - branch * per_branch) * LANES, LANES)
    branch_ref[branch, :, pl.ds(start, LANES)] = value[kept:].T


def out_kernel(kept, *refs):
    ins, branch_ref, class_ref = refs[:-2], refs[-2], refs[-1]
    dom = lax.axis_index("dom")
    half = len(ins) // 2
    for step in range(half):
        for side in range(2):
            value = ins[side * half + step][...].astype(F32)
            write_chunk(kept, dom ^ (2 * step + side), value, branch_ref, class_ref)


def plain_out_kernel(kept, in_ref, branch_ref, class_ref):
    for chunk in range(in_ref.shape[0]):
        write_chunk(kept, chunk, in_ref[chunk], branch_ref, class_ref)


def swapped(value, distance, axis="dom"):
    pairs = [(source, source ^ distance) for source in range(lax.axis_size(axis))]
    return lax.ppermute(value, axis, pairs)


def in_group(value):
    members = [value]
    distance = lax.axis_size("shuf") // 2
    while distance:
        members += [swapped(member, distance, "shuf") for member in members]
        distance //= 2
    count = len(members)
    steps = [0]
    distance = count // 2
    while distance:
        steps += [step + distance for step in steps]
        distance //= 2
    return [members[steps.index(step)] for step in range(count)]


def body(
    features, tile_values, tile_dst, tile_src, tile_count, send_left, send_right,
    send_count, batch_order, labels, w_branch, w_class,
):
    block = tile_values.shape[1]
    nodes, width = features.shape
    local = nodes // block
    slots = send_left.shape[0]
    tiles = tile_values.shape[0]
    branches, _, hid = w_branch.shape
    cat, classes = w_class.shape
    dom = lax.axis_size("dom")
    shuf = lax.axis_size("shuf")
    mine = lax.axis_index("shuf")
    share = nodes // shuf
    own = hid // shuf
    own_class = cat // shuf
    kept = up_to(classes, 16)
    row_scale = 1.0 / math.sqrt(float(nodes * dom * shuf))
    plan = Plan(tiles, slots)
    small = jnp.concatenate(
        [tile_dst, tile_src, tile_count, send_left, send_right, send_count.reshape(-1)]
    )
    blocks_f32 = jax.ShapeDtypeStruct((local, block, width), F32)
    slots_f32 = jax.ShapeDtypeStruct((slots, block, width), F32)
    rows_b16 = jax.ShapeDtypeStruct((nodes, width), BF16)
    first_b16 = jax.ShapeDtypeStruct((nodes + 16, width), BF16)
    logits_f32 = jax.ShapeDtypeStruct((classes, nodes), F32)
    w_class_t = w_class.T

    current = features.reshape(local, block, width)
    gathered = []
    logits = None
    hop_flops = 12 * tiles * block * block * width
    forward_flops = 2 * nodes * hid * (width + classes)
    ext = pltpu.VMEM((local + 2 * slots, block, width), F32)
    to_left = to_right = current
    for hop in range(HOPS):
        from_lower = passed_along(to_right, "dom", 1)
        from_upper = passed_along(to_left, "dom", -1)
        if hop == 0:
            logits, rows = call(
                forward_first_kernel, [logits_f32, first_b16], [IN_VMEM] * 5, forward_flops
            )(current, w_branch, w_class_t, labels.reshape(1, nodes), tile_values)
        else:
            logits, rows = call(
                functools.partial(forward_kernel, hop),
                [logits_f32, rows_b16],
                [IN_VMEM] * 4,
                forward_flops,
            )(current, w_branch, w_class_t, logits)
        gathered.append(in_group(rows))
        if hop < HOPS - 1:
            out_shape = [blocks_f32, slots_f32, slots_f32]
            if hop == 0:
                kernel = first_hop_kernel
                plans = (small, passed_along(small, "dom", 1), passed_along(small, "dom", -1))
            else:
                kernel = hop_kernel
                plans = (small,)
            current, to_left, to_right = call(
                functools.partial(kernel, plan),
                out_shape,
                [IN_SMEM] * len(plans) + [IN_VMEM] * 4,
                hop_flops,
                [ext],
                [logits] + [members[shuf // 2] for members in gathered[:hop]],
            )(*plans, current, from_lower, from_upper, tile_values)

    label_mine = call(
        label_kernel,
        jax.ShapeDtypeStruct((1, nodes), jnp.int32),
        [IN_VMEM] * (1 + shuf),
        1000,
    )(batch_order, *gathered[0])

    wt_own, wct_own = call(
        weights_kernel,
        [
            jax.ShapeDtypeStruct((branches, own, width), BF16),
            jax.ShapeDtypeStruct((branches, own, kept), BF16),
        ],
        [IN_VMEM] * 2,
        1000,
        [pltpu.VMEM((up_to(classes, LANES), own), F32)],
    )(w_branch, w_class_t)

    payload = call(
        functools.partial(last_kernel, plan, row_scale),
        jax.ShapeDtypeStruct((block + kept + 16, local * width), BF16),
        [IN_SMEM] + [IN_VMEM] * 9,
        hop_flops + forward_flops,
        [ext],
        [*gathered[1][1:], gathered[2][shuf // 2]],
    )(
        small, current, from_lower, from_upper, tile_values,
        logits, w_branch, w_class_t, batch_order, label_mine,
    )
    gathered = [member for members in gathered for member in members]
    last_all = in_group(payload)
    loss_rows = call(
        loss_kernel, jax.ShapeDtypeStruct((1, nodes), F32), [IN_VMEM] * shuf, 1000
    )(*last_all).reshape(nodes)

    chunks = own_class // LANES
    height = kept + width
    grad_flops = 2 * shuf * nodes * own_class * (3 * width + 2 * kept)
    grad_ins = (*gathered, *last_all, w_branch, wt_own, wct_own)
    outs = [
        jax.ShapeDtypeStruct((branches, width, own), F32),
        jax.ShapeDtypeStruct((classes, own_class), F32),
    ]
    chunks_f32 = pltpu.VMEM((chunks, height, LANES), F32)
    if chunks == dom and dom % 4 == 0 and dom & (dom - 1) == 0:
        half = dom // 2
        one_f32 = jax.ShapeDtypeStruct((height, LANES), F32)
        two_b16 = jax.ShapeDtypeStruct((2, height, LANES), BF16)
        made = call(
            functools.partial(grad_kernel, kept, shuf, len(gathered), half),
            [one_f32] * half + [two_b16] * (half // 2),
            [IN_VMEM] * len(grad_ins),
            grad_flops,
            [chunks_f32],
        )(*grad_ins)
        order = list(range(half - 1, -1, -1))
        arrived = {pair: swapped(made[half + pair], 1) for pair in range(half // 2 - 1, -1, -1)}
        total = {
            step: made[step] + arrived[step // 2][step % 2].astype(F32) for step in order
        }
        far = [swapped(total[step].astype(BF16), 2 * step) for step in order[:-1]]
        summed = total[0]
        for value in far:
            summed = summed + value.astype(F32)
        near = {0: summed.astype(BF16)}
        other = {0: swapped(near[0], 1)}
        for step in order[:-1]:
            near[step] = swapped(near[0], 2 * step)
        for step in range(1, half):
            other[step] = swapped(near[step], 1)
        near = [near[step] for step in range(half)]
        other = [other[step] for step in range(half)]
        grad_branch, grad_class_t = call(
            functools.partial(out_kernel, kept), outs, [IN_VMEM] * dom, 1000
        )(*near, *other)
    else:
        grads = call(
            functools.partial(plain_grad_kernel, kept, shuf, len(gathered)),
            jax.ShapeDtypeStruct((chunks, height, LANES), F32),
            [IN_VMEM] * len(grad_ins),
            grad_flops,
        )(*grad_ins)
        grad_branch, grad_class_t = call(
            functools.partial(plain_out_kernel, kept), outs, [IN_VMEM], 1000
        )(lax.psum(grads, "dom"))
    return (loss_rows, grad_branch, grad_class_t.T)


def solution(mesh):
    return jax.shard_map(
        body,
        mesh=mesh,
        in_specs=(
            P(("dom", "shuf"), None),
            P(("dom", "shuf"), None, None),
            P(("dom", "shuf")),
            P(("dom", "shuf")),
            P(("dom", "shuf")),
            P(("dom", "shuf")),
            P(("dom", "shuf")),
            P(("dom", "shuf"), None),
            P(("dom", "shuf"), None),
            P(("dom", "shuf")),
            P(),
            P(),
        ),
        out_specs=(P(("dom", "shuf")), P(None, None, "shuf"), P("shuf", None)),
        check_vma=False,
    )
```

```python
import functools
import math

import jax
import jax.numpy as jnp
from jax import lax
from jax.experimental import pallas as pl
from jax.experimental.pallas import tpu as pltpu
from jax.sharding import PartitionSpec as P

HOPS = 3
LANES = 128
VMEM_LIMIT = 24 * 1024 * 1024
VMEM_ALL = 56 * 1024 * 1024

IN_VMEM = pl.BlockSpec(memory_space=pltpu.VMEM)
IN_SMEM = pl.BlockSpec(memory_space=pltpu.SMEM)
ANYWHERE = pl.BlockSpec(memory_space=pl.ANY)
BF16 = jnp.bfloat16
F32 = jnp.float32


def up_to(value, multiple):
    return -(-value // multiple) * multiple


def passed_along(value, axis, steps):
    count = lax.axis_size(axis)
    pairs = [(source, (source + steps) % count) for source in range(count)]
    return lax.ppermute(value, axis, pairs)


def matmul(left, right, dims=((1,), (0,)), precision=None):
    return lax.dot_general(
        left, right, (dims, ((), ())), precision=precision, preferred_element_type=F32
    )


def call(kernel, out_shape, in_specs, flops, scratch=(), after=(), limit=VMEM_LIMIT):
    many = isinstance(out_shape, (list, tuple))
    outs = out_shape if many else [out_shape]
    moved = sum(math.prod(one.shape) * one.dtype.itemsize for one in outs)
    waited = len(after)

    def run(*refs):
        kernel(*refs[waited:])

    made = pl.pallas_call(
        run,
        out_shape=out_shape,
        in_specs=[ANYWHERE] * waited + in_specs,
        out_specs=[IN_VMEM] * len(outs) if many else IN_VMEM,
        scratch_shapes=list(scratch),
        compiler_params=pltpu.CompilerParams(vmem_limit_bytes=limit),
        cost_estimate=pl.CostEstimate(
            flops=flops, bytes_accessed=3 * moved, transcendentals=0
        ),
    )
    return functools.partial(made, *after)


class Plan:
    def __init__(self, tiles, slots):
        self.tiles = tiles
        self.slots = slots
        self.dst = 0
        self.src = tiles
        self.count = 2 * tiles
        self.left = 2 * tiles + 1
        self.right = self.left + slots
        self.sent = self.right + slots


def write_sends(blocks, left_ref, right_ref, left_ids, right_ids, counts):
    for slot in range(left_ref.shape[0]):
        for out_ref, ids, side in ((left_ref, left_ids, 0), (right_ref, right_ids, 1)):
            index = ids(slot)
            picked = blocks[0]
            for number in range(1, len(blocks)):
                picked = jnp.where(index == number, blocks[number], picked)
            out_ref[slot] = jnp.where(slot < counts(side), picked, 0.0)


def copied(sources, targets, sems):
    copies = [
        pltpu.make_async_copy(source, target, sems.at[number])
        for number, (source, target) in enumerate(zip(sources, targets))
    ]
    for copy in copies:
        copy.start()
    for copy in copies:
        copy.wait()


def first_kernel(
    sl_ref, sr_ref, sc_ref, feat_ref, left_ref, right_ref, held_ref,
    sl_here, sr_here, sc_here, sems,
):
    copied(
        (sl_ref, sr_ref, sc_ref, feat_ref), (sl_here, sr_here, sc_here, held_ref), sems
    )
    write_sends(
        [held_ref[number] for number in range(held_ref.shape[0])],
        left_ref,
        right_ref,
        lambda slot: sl_here[slot],
        lambda slot: sr_here[slot],
        lambda side: sc_here[0, side],
    )


def next_blocks(plan, plan_ref, cur_ref, tiles_ref, ext_ref):
    local = cur_ref.shape[0]
    ext_ref[:local] = cur_ref[...]
    totals = [jnp.zeros(cur_ref.shape[1:], F32) for _ in range(local)]
    live = plan_ref[plan.count]
    for tile in range(plan.tiles):
        product = matmul(
            tiles_ref[tile],
            ext_ref[plan_ref[plan.src + tile]],
            precision=lax.Precision.HIGHEST,
        )
        wanted = jnp.where(tile < live, plan_ref[plan.dst + tile], -1)
        for number in range(local):
            totals[number] = totals[number] + jnp.where(wanted == number, product, 0.0)
    return totals


def extend(cur_ref, low_ref, high_ref, ext_ref):
    local = cur_ref.shape[0]
    slots = low_ref.shape[0]
    ext_ref[local : local + slots] = low_ref[...]
    ext_ref[local + slots :] = high_ref[...]


def write_hop(plan, plan_ref, cur_ref, tiles_ref, next_ref, left_ref, right_ref, ext_ref):
    blocks = next_blocks(plan, plan_ref, cur_ref, tiles_ref, ext_ref)
    write_sends(
        blocks,
        left_ref,
        right_ref,
        lambda slot: plan_ref[plan.left + slot],
        lambda slot: plan_ref[plan.right + slot],
        lambda side: plan_ref[plan.sent + side],
    )
    for number, block in enumerate(blocks):
        next_ref[number] = block


def hop_kernel(
    plan, plan_ref, cur_ref, low_ref, high_ref, tiles_ref,
    next_ref, left_ref, right_ref, ext_ref,
):
    extend(cur_ref, low_ref, high_ref, ext_ref)
    write_hop(plan, plan_ref, cur_ref, tiles_ref, next_ref, left_ref, right_ref, ext_ref)


def branch_logits(branch, rows, w_ref, wc_ref):
    hidden = jnp.maximum(matmul(rows, w_ref[branch]), 0.0).astype(BF16)
    hid = hidden.shape[1]
    return matmul(wc_ref[:, branch * hid : (branch + 1) * hid], hidden, ((1,), (1,)))


def forward_kernel(branch, cur_ref, w_ref, wc_ref, *refs):
    rows = cur_ref[...].reshape(-1, cur_ref.shape[2]).astype(BF16)
    part = branch_logits(branch, rows, w_ref, wc_ref)
    if len(refs) == 3:
        part = refs[0][...] + part
    refs[-2][...] = part
    refs[-1][...] = rows


def forward_first_kernel(cur_ref, w_ref, wc_ref, tiles_ref, label_ref, part_ref, b_ref):
    nodes = label_ref.shape[1]
    forward_kernel(0, cur_ref, w_ref, wc_ref, part_ref, b_ref.at[:nodes])
    width = b_ref.shape[1]
    per_piece = nodes // width
    place = lax.broadcasted_iota(jnp.int32, (16, width), 0)
    packed = jnp.zeros((16, width), F32)
    for piece in range(2):
        value = label_ref[...] & 255 if piece == 0 else label_ref[...] >> 8
        value = value.astype(F32)
        for part in range(per_piece):
            packed = jnp.where(
                place == piece * per_piece + part,
                value[:, part * width : (part + 1) * width],
                packed,
            )
    b_ref[nodes:] = packed.astype(BF16)


def places(order_ref):
    nodes = order_ref.shape[1]
    rows = lax.broadcasted_iota(jnp.int32, (nodes, nodes), 0)
    return (order_ref[...] == rows).astype(F32).astype(BF16)


def wanted_places(nodes, group, step, offset, count):
    share = nodes // group
    mine = lax.axis_index("shuf")
    first = mine * share
    source = lax.broadcasted_iota(jnp.int32, (count, nodes), 0) + offset
    target = lax.broadcasted_iota(jnp.int32, (count, nodes), 1)
    moved = source + ((mine ^ step) - mine) * share
    wanted = (target == moved) & (source >= first) & (source < first + share)
    return wanted.astype(F32).astype(BF16)


def label_kernel(order_ref, *refs):
    nodes = order_ref.shape[1]
    group = len(refs) - 1
    width = refs[0].shape[1]
    per_piece = nodes // width
    ordered = [jnp.zeros((1, nodes), F32) for _ in range(2)]
    for step in range(group):
        tail = refs[step][nodes:]
        for part in range(per_piece):
            moved = matmul(tail, wanted_places(nodes, group, step, part * width, width))
            for piece in range(2):
                row = piece * per_piece + part
                ordered[piece] = ordered[piece] + moved[row : row + 1]
    number = lax.broadcasted_iota(jnp.int32, (16, nodes), 0)
    packed = jnp.where(number == 0, ordered[0], jnp.where(number == 1, ordered[1], 0.0))
    pieces = matmul(packed.astype(BF16), places(order_ref), ((1,), (1,)))
    refs[-1][...] = (pieces[0:1] + 256.0 * pieces[1:2]).astype(jnp.int32)


def loss_kernel(*refs):
    group = len(refs) - 1
    height, nodes = refs[0].shape
    total = jnp.zeros((16, nodes), F32)
    for step in range(group):
        wanted = wanted_places(nodes, group, step, 0, nodes)
        total = total + matmul(refs[step][height - 16 :], wanted)
    refs[-1][...] = total[0:1] + total[1:2] + total[2:3]


def last_kernel(
    plan, row_scale, plan_ref,
    cur_ref, low_ref, high_ref, tiles_ref, before_ref, w_ref, wc_ref, order_ref, label_ref,
    out_ref, ext_ref,
):
    extend(cur_ref, low_ref, high_ref, ext_ref)
    blocks = next_blocks(plan, plan_ref, cur_ref, tiles_ref, ext_ref)
    halves = [block.astype(BF16) for block in blocks]
    rows_b = jnp.concatenate(halves, axis=0)
    size, width = halves[0].shape
    for number, half in enumerate(halves):
        columns = slice(number * width, (number + 1) * width)
        out_ref[:size, columns] = half
        out_ref[size : 2 * size, columns] = cur_ref[number].astype(BF16)
    size = 2 * size
    logits = before_ref[...] + branch_logits(w_ref.shape[0] - 1, rows_b, w_ref, wc_ref)
    classes, rows = logits.shape
    kept = up_to(classes, 16)
    hit = lax.broadcasted_iota(jnp.int32, (classes, rows), 0) == label_ref[...]
    top = jnp.max(logits, axis=0, keepdims=True)
    log_total = top + jnp.log(jnp.sum(jnp.exp(logits - top), axis=0, keepdims=True))
    loss = log_total - jnp.sum(jnp.where(hit, logits, 0.0), axis=0, keepdims=True)
    dlogits = (jnp.exp(logits - log_total) - jnp.where(hit, 1.0, 0.0)) * row_scale
    out_ref[size + kept - 16 : size + kept] = jnp.zeros((16, rows), BF16)
    out_ref[size : size + classes] = dlogits.astype(BF16)
    number = lax.broadcasted_iota(jnp.int32, (16, rows), 0)
    packed = jnp.zeros((16, rows), F32)
    rest = loss
    for piece in range(3):
        part = rest.astype(BF16).astype(F32)
        packed = jnp.where(number == piece, part, packed)
        rest = rest - part
    out_ref[size + kept :] = matmul(packed.astype(BF16), places(order_ref)).astype(BF16)


def weights_kernel(w_ref, wc_ref, wt_ref, wct_ref, pad_ref):
    branches, own, kept = wct_ref.shape
    classes = wc_ref.shape[0]
    hid = w_ref.shape[2]
    first = lax.axis_index("shuf") * own
    pad_ref[...] = jnp.zeros_like(pad_ref)
    for branch in range(branches):
        columns = w_ref[branch, :, pl.ds(pl.multiple_of(first, LANES), own)]
        wt_ref[branch] = columns.astype(F32).T.astype(BF16)
        columns = wc_ref[:, pl.ds(pl.multiple_of(branch * hid + first, LANES), own)]
        pad_ref[:classes] = columns.astype(F32)
        wct_ref[branch] = pad_ref[...].T[:, :kept].astype(BF16)


def all_chunks(kept, row_refs, last_refs, w_ref, wt_ref, wct_ref, chunks_ref):
    group = len(last_refs)
    branches, own, width = wt_ref.shape
    nodes = last_refs[0].shape[1]
    hid = w_ref.shape[2]
    parts = last_refs[0].shape[1] // width
    size = nodes // parts
    all_rows = []
    for branch in range(branches - 2):
        ours = row_refs[branch * group : (branch + 1) * group]
        all_rows.append(jnp.concatenate([ref[:nodes] for ref in ours], axis=0))
    for place in (1, 0):
        last_rows = []
        for ref in last_refs:
            for part in range(parts):
                columns = slice(part * width, (part + 1) * width)
                last_rows.append(ref[place * size : (place + 1) * size, columns])
        all_rows.append(jnp.concatenate(last_rows, axis=0))
    size = 2 * size
    dlogits_t = jnp.concatenate([ref[size : size + kept] for ref in last_refs], axis=1)
    own_class = branches * own
    first = lax.axis_index("shuf") * own_class
    which = first // hid
    columns = pl.ds(pl.multiple_of(first - which * hid, LANES), own_class)
    chosen = all_rows[0]
    for branch in range(1, branches):
        chosen = jnp.where(which == branch, all_rows[branch], chosen)
    hidden = jnp.maximum(matmul(chosen, w_ref[which, :, columns]), 0.0).astype(BF16)
    class_t = matmul(dlogits_t, hidden)
    for chunk in range(chunks_ref.shape[0]):
        chunks_ref[chunk, :kept] = class_t[:, chunk * LANES : (chunk + 1) * LANES]
    per_branch = chunks_ref.shape[0] // branches
    for branch, rows in enumerate(all_rows):
        live = matmul(wt_ref[branch], rows, ((1,), (1,))) > 0.0
        dhidden_t = jnp.where(live, matmul(wct_ref[branch], dlogits_t), 0.0).astype(BF16)
        branch_t = matmul(dhidden_t, rows)
        for part in range(per_branch):
            chunks_ref[branch * per_branch + part, kept:] = branch_t[
                part * LANES : (part + 1) * LANES
            ]


def grad_kernel(kept, group, row_count, half, *refs):
    ins = row_count + group + 3
    outs = refs[ins:-1]
    chunks_ref = refs[-1]
    plain_grad_kernel(kept, group, row_count, *refs[:ins], chunks_ref)
    dom = lax.axis_index("dom")
    for step in range(half):
        stays = dom ^ (2 * step)
        outs[step][...] = chunks_ref[stays]
        outs[half + step // 2][step % 2] = chunks_ref[stays ^ 1].astype(BF16)


def plain_grad_kernel(kept, group, row_count, *refs):
    last = row_count + group
    all_chunks(kept, refs[:row_count], refs[row_count:last], *refs[last:])


def write_chunk(kept, chunk, value, branch_ref, class_ref):
    per_branch = branch_ref.shape[2] // LANES
    start = pl.multiple_of(chunk * LANES, LANES)
    class_ref[:, pl.ds(start, LANES)] = value[: class_ref.shape[0]]
    branch = chunk // per_branch
    start = pl.multiple_of((chunk - branch * per_branch) * LANES, LANES)
    branch_ref[branch, :, pl.ds(start, LANES)] = value[kept:].T


def out_kernel(kept, *refs):
    ins, branch_ref, class_ref = refs[:-2], refs[-2], refs[-1]
    dom = lax.axis_index("dom")
    half = len(ins) // 2
    for step in range(half):
        for side in range(2):
            value = ins[side * half + step][...].astype(F32)
            write_chunk(kept, dom ^ (2 * step + side), value, branch_ref, class_ref)


def plain_out_kernel(kept, in_ref, branch_ref, class_ref):
    for chunk in range(in_ref.shape[0]):
        write_chunk(kept, chunk, in_ref[chunk], branch_ref, class_ref)


def swapped(value, distance, axis="dom"):
    pairs = [(source, source ^ distance) for source in range(lax.axis_size(axis))]
    return lax.ppermute(value, axis, pairs)


def in_group(value):
    members = [value]
    distance = lax.axis_size("shuf") // 2
    while distance:
        members += [swapped(member, distance, "shuf") for member in members]
        distance //= 2
    count = len(members)
    steps = [0]
    distance = count // 2
    while distance:
        steps += [step + distance for step in steps]
        distance //= 2
    return [members[steps.index(step)] for step in range(count)]


def body(
    features, tile_values, tile_dst, tile_src, tile_count, send_left, send_right,
    send_count, batch_order, labels, w_branch, w_class,
):
    block = tile_values.shape[1]
    nodes, width = features.shape
    local = nodes // block
    slots = send_left.shape[0]
    tiles = tile_values.shape[0]
    branches, _, hid = w_branch.shape
    cat, classes = w_class.shape
    dom = lax.axis_size("dom")
    shuf = lax.axis_size("shuf")
    mine = lax.axis_index("shuf")
    share = nodes // shuf
    own = hid // shuf
    own_class = cat // shuf
    kept = up_to(classes, 16)
    row_scale = 1.0 / math.sqrt(float(nodes * dom * shuf))
    plan = Plan(tiles, slots)
    small = jnp.concatenate(
        [tile_dst, tile_src, tile_count, send_left, send_right, send_count.reshape(-1)]
    )
    blocks_f32 = jax.ShapeDtypeStruct((local, block, width), F32)
    slots_f32 = jax.ShapeDtypeStruct((slots, block, width), F32)
    rows_b16 = jax.ShapeDtypeStruct((nodes, width), BF16)
    first_b16 = jax.ShapeDtypeStruct((nodes + 16, width), BF16)
    logits_f32 = jax.ShapeDtypeStruct((classes, nodes), F32)
    w_class_t = w_class.T

    current = features.reshape(local, block, width)
    gathered = []
    logits = None
    hop_flops = 12 * tiles * block * block * width
    forward_flops = 2 * nodes * hid * (width + classes)
    ext = pltpu.VMEM((local + 2 * slots, block, width), F32)
    to_left, to_right, current = call(
        first_kernel,
        [slots_f32, slots_f32, blocks_f32],
        [ANYWHERE] * 4,
        1000,
        [
            pltpu.SMEM((slots,), jnp.int32),
            pltpu.SMEM((slots,), jnp.int32),
            pltpu.SMEM((1, 2), jnp.int32),
            pltpu.SemaphoreType.DMA((4,)),
        ],
        limit=VMEM_ALL,
    )(send_left, send_right, send_count, current)
    for hop in range(HOPS):
        from_lower = passed_along(to_right, "dom", 1)
        from_upper = passed_along(to_left, "dom", -1)
        if hop == 0:
            logits, rows = call(
                forward_first_kernel, [logits_f32, first_b16], [IN_VMEM] * 5, forward_flops
            )(current, w_branch, w_class_t, tile_values, labels.reshape(1, nodes))
            gathered.append(in_group(rows))
        else:
            logits, rows = call(
                functools.partial(forward_kernel, hop),
                [logits_f32, rows_b16],
                [IN_VMEM] * 4,
                forward_flops,
                (),
                [members[shuf // 2] for members in gathered] if hop == 2 else [],
            )(current, w_branch, w_class_t, logits)
            if hop < HOPS - 1:
                gathered.append(in_group(rows))
        if hop < HOPS - 1:
            current, to_left, to_right = call(
                functools.partial(hop_kernel, plan),
                [blocks_f32, slots_f32, slots_f32],
                [IN_SMEM] + [IN_VMEM] * 4,
                hop_flops,
                [ext],
                [logits],
            )(small, current, from_lower, from_upper, tile_values)

    label_mine = call(
        label_kernel,
        jax.ShapeDtypeStruct((1, nodes), jnp.int32),
        [IN_VMEM] * (1 + shuf),
        1000,
    )(batch_order, *gathered[0])

    wt_own, wct_own = call(
        weights_kernel,
        [
            jax.ShapeDtypeStruct((branches, own, width), BF16),
            jax.ShapeDtypeStruct((branches, own, kept), BF16),
        ],
        [IN_VMEM] * 2,
        1000,
        [pltpu.VMEM((up_to(classes, LANES), own), F32)],
    )(w_branch, w_class_t)

    payload = call(
        functools.partial(last_kernel, plan, row_scale),
        jax.ShapeDtypeStruct((2 * block + kept + 16, local * width), BF16),
        [IN_SMEM] + [IN_VMEM] * 9,
        hop_flops + forward_flops,
        [ext],
        gathered[1][1:],
    )(
        small, current, from_lower, from_upper, tile_values,
        logits, w_branch, w_class_t, batch_order, label_mine,
    )
    gathered = [member for members in gathered for member in members]
    last_all = in_group(payload)
    loss_rows = call(
        loss_kernel, jax.ShapeDtypeStruct((1, nodes), F32), [IN_VMEM] * shuf, 1000
    )(*last_all).reshape(nodes)

    chunks = own_class // LANES
    height = kept + width
    grad_flops = 2 * shuf * nodes * own_class * (3 * width + 2 * kept)
    grad_ins = (*gathered, *last_all, w_branch, wt_own, wct_own)
    outs = [
        jax.ShapeDtypeStruct((branches, width, own), F32),
        jax.ShapeDtypeStruct((classes, own_class), F32),
    ]
    chunks_f32 = pltpu.VMEM((chunks, height, LANES), F32)
    if chunks == dom and dom % 4 == 0 and dom & (dom - 1) == 0:
        half = dom // 2
        one_f32 = jax.ShapeDtypeStruct((height, LANES), F32)
        two_b16 = jax.ShapeDtypeStruct((2, height, LANES), BF16)
        made = call(
            functools.partial(grad_kernel, kept, shuf, len(gathered), half),
            [one_f32] * half + [two_b16] * (half // 2),
            [IN_VMEM] * len(grad_ins),
            grad_flops,
            [chunks_f32],
        )(*grad_ins)
        order = list(range(half - 1, -1, -1))
        arrived = {pair: swapped(made[half + pair], 1) for pair in range(half // 2 - 1, -1, -1)}
        total = {
            step: made[step] + arrived[step // 2][step % 2].astype(F32) for step in order
        }
        far = [swapped(total[step].astype(BF16), 2 * step) for step in order[:-1]]
        summed = total[0]
        for value in far:
            summed = summed + value.astype(F32)
        near = {0: summed.astype(BF16)}
        other = {0: swapped(near[0], 1)}
        for step in order[:-1]:
            near[step] = swapped(near[0], 2 * step)
        for step in range(1, half):
            other[step] = swapped(near[step], 1)
        near = [near[step] for step in range(half)]
        other = [other[step] for step in range(half)]
        grad_branch, grad_class_t = call(
            functools.partial(out_kernel, kept), outs, [IN_VMEM] * dom, 1000
        )(*near, *other)
    else:
        grads = call(
            functools.partial(plain_grad_kernel, kept, shuf, len(gathered)),
            jax.ShapeDtypeStruct((chunks, height, LANES), F32),
            [IN_VMEM] * len(grad_ins),
            grad_flops,
        )(*grad_ins)
        grad_branch, grad_class_t = call(
            functools.partial(plain_out_kernel, kept), outs, [IN_VMEM], 1000
        )(lax.psum(grads, "dom"))
    return (loss_rows, grad_branch, grad_class_t.T)


def solution(mesh):
    return jax.shard_map(
        body,
        mesh=mesh,
        in_specs=(
            P(("dom", "shuf"), None),
            P(("dom", "shuf"), None, None),
            P(("dom", "shuf")),
            P(("dom", "shuf")),
            P(("dom", "shuf")),
            P(("dom", "shuf")),
            P(("dom", "shuf")),
            P(("dom", "shuf"), None),
            P(("dom", "shuf"), None),
            P(("dom", "shuf")),
            P(),
            P(),
        ),
        out_specs=(P(("dom", "shuf")), P(None, None, "shuf"), P("shuf", None)),
        check_vma=False,
    )
```

```python
import functools
import math

import jax
import jax.numpy as jnp
from jax import lax
from jax.experimental import pallas as pl
from jax.experimental.pallas import tpu as pltpu
from jax.sharding import PartitionSpec as P

HOPS = 3
LANES = 128
VMEM_LIMIT = 24 * 1024 * 1024
VMEM_ALL = 56 * 1024 * 1024

IN_VMEM = pl.BlockSpec(memory_space=pltpu.VMEM)
IN_SMEM = pl.BlockSpec(memory_space=pltpu.SMEM)
ANYWHERE = pl.BlockSpec(memory_space=pl.ANY)
BF16 = jnp.bfloat16
F32 = jnp.float32


def up_to(value, multiple):
    return -(-value // multiple) * multiple


def near_pairs(value):
    return swapped(value, 1)


def far_pairs(value):
    count = lax.axis_size("dom")
    pairs = [(d, (d + 1 if d % 2 else d - 1) % count) for d in range(count)]
    return lax.ppermute(value, "dom", pairs)


def swapped(value, distance, axis="dom"):
    pairs = [(source, source ^ distance) for source in range(lax.axis_size(axis))]
    return lax.ppermute(value, axis, pairs)


def matmul(left, right, dims=((1,), (0,)), precision=None):
    return lax.dot_general(
        left, right, (dims, ((), ())), precision=precision, preferred_element_type=F32
    )


def call(kernel, out_shape, in_specs, flops, scratch=(), after=(), limit=VMEM_LIMIT):
    many = isinstance(out_shape, (list, tuple))
    outs = out_shape if many else [out_shape]
    moved = sum(math.prod(one.shape) * one.dtype.itemsize for one in outs)
    waited = len(after)

    def run(*refs):
        kernel(*refs[waited:])

    made = pl.pallas_call(
        run,
        out_shape=out_shape,
        in_specs=[ANYWHERE] * waited + in_specs,
        out_specs=[IN_VMEM] * len(outs) if many else IN_VMEM,
        scratch_shapes=list(scratch),
        compiler_params=pltpu.CompilerParams(vmem_limit_bytes=limit),
        cost_estimate=pl.CostEstimate(
            flops=flops, bytes_accessed=3 * moved, transcendentals=0
        ),
    )
    return functools.partial(made, *after)


class Plan:
    def __init__(self, tiles, slots):
        self.tiles = tiles
        self.slots = slots
        self.dst = 0
        self.src = tiles
        self.count = 2 * tiles
        self.left = 2 * tiles + 1
        self.right = self.left + slots
        self.sent = self.right + slots


def write_sends(blocks, far_ref, near_ref, ids, counts):
    odd = lax.axis_index("dom") % 2
    for slot in range(far_ref.shape[0]):
        for out_ref, side in ((far_ref, odd), (near_ref, 1 - odd)):
            index = ids(side, slot)
            picked = blocks[0]
            for number in range(1, len(blocks)):
                picked = jnp.where(index == number, blocks[number], picked)
            out_ref[slot] = jnp.where(slot < counts(side), picked, 0.0)


def copied(sources, targets, sems):
    copies = [
        pltpu.make_async_copy(source, target, sems.at[number])
        for number, (source, target) in enumerate(zip(sources, targets))
    ]
    for copy in copies:
        copy.start()
    for copy in copies:
        copy.wait()


def first_kernel(
    sl_ref, sr_ref, sc_ref, feat_ref, label_from,
    far_ref, near_ref, held_ref, b_ref,
    sl_here, sr_here, sc_here, label_ref, sems,
):
    copied(
        (sl_ref, sr_ref, sc_ref, feat_ref, label_from),
        (sl_here, sr_here, sc_here, held_ref, label_ref),
        sems,
    )
    blocks = [held_ref[number] for number in range(held_ref.shape[0])]
    write_sends(
        blocks,
        far_ref,
        near_ref,
        lambda side, slot: jnp.where(side == 0, sl_here[slot], sr_here[slot]),
        lambda side: sc_here[0, side],
    )
    write_rows(blocks, b_ref)
    nodes = label_ref.shape[1]
    width = b_ref.shape[1]
    per_piece = nodes // width
    place = lax.broadcasted_iota(jnp.int32, (16, width), 0)
    packed = jnp.zeros((16, width), F32)
    for piece in range(2):
        value = label_ref[...] & 255 if piece == 0 else label_ref[...] >> 8
        value = value.astype(F32)
        for part in range(per_piece):
            packed = jnp.where(
                place == piece * per_piece + part,
                value[:, part * width : (part + 1) * width],
                packed,
            )
    b_ref[nodes:] = packed.astype(BF16)


def write_rows(blocks, b_ref):
    for number, block in enumerate(blocks):
        size = block.shape[0]
        b_ref[number * size : (number + 1) * size] = block.astype(BF16)


def next_blocks(plan, plan_ref, cur_ref, tiles_ref, ext_ref):
    local = cur_ref.shape[0]
    ext_ref[:local] = cur_ref[...]
    totals = [jnp.zeros(cur_ref.shape[1:], F32) for _ in range(local)]
    live = plan_ref[plan.count]
    for tile in range(plan.tiles):
        product = matmul(
            tiles_ref[tile],
            ext_ref[plan_ref[plan.src + tile]],
            precision=lax.Precision.HIGHEST,
        )
        wanted = jnp.where(tile < live, plan_ref[plan.dst + tile], -1)
        for number in range(local):
            totals[number] = totals[number] + jnp.where(wanted == number, product, 0.0)
    return totals


def extend(cur_ref, far_ref, near_ref, ext_ref):
    local = cur_ref.shape[0]
    slots = far_ref.shape[0]
    odd = lax.axis_index("dom") % 2
    ext_ref[pl.ds(local + odd * slots, slots)] = far_ref[...]
    ext_ref[pl.ds(local + (1 - odd) * slots, slots)] = near_ref[...]


def hop_kernel(
    plan, plan_ref, cur_ref, far_in_ref, near_in_ref, tiles_ref,
    next_ref, far_ref, near_ref, b_ref, ext_ref,
):
    extend(cur_ref, far_in_ref, near_in_ref, ext_ref)
    blocks = next_blocks(plan, plan_ref, cur_ref, tiles_ref, ext_ref)
    write_sends(
        blocks,
        far_ref,
        near_ref,
        lambda side, slot: plan_ref[plan.left + side * plan.slots + slot],
        lambda side: plan_ref[plan.sent + side],
    )
    for number, block in enumerate(blocks):
        next_ref[number] = block
    write_rows(blocks, b_ref)


def ready_kernel(cur_ref, tiles_ref, cur_out, tiles_out):
    cur_out[...] = cur_ref[...]
    tiles_out[...] = tiles_ref[...]


def branch_logits(branch, rows, w_ref, wc_ref):
    hidden = jnp.maximum(matmul(rows, w_ref[branch]), 0.0).astype(BF16)
    hid = hidden.shape[1]
    return matmul(wc_ref[:, branch * hid : (branch + 1) * hid], hidden, ((1,), (1,)))


def forward_kernel(branch, cur_ref, w_ref, wc_ref, *refs):
    rows = cur_ref[...].reshape(-1, cur_ref.shape[2]).astype(BF16)
    part = branch_logits(branch, rows, w_ref, wc_ref)
    if len(refs) == 2:
        part = refs[0][...] + part
    refs[-1][...] = part


def places(order_ref):
    nodes = order_ref.shape[1]
    rows = lax.broadcasted_iota(jnp.int32, (nodes, nodes), 0)
    return (order_ref[...] == rows).astype(F32).astype(BF16)


def wanted_places(nodes, group, step, offset, count):
    share = nodes // group
    mine = lax.axis_index("shuf")
    first = mine * share
    source = lax.broadcasted_iota(jnp.int32, (count, nodes), 0) + offset
    target = lax.broadcasted_iota(jnp.int32, (count, nodes), 1)
    moved = source + ((mine ^ step) - mine) * share
    wanted = (target == moved) & (source >= first) & (source < first + share)
    return wanted.astype(F32).astype(BF16)


def label_kernel(order_ref, *refs):
    nodes = order_ref.shape[1]
    group = len(refs) - 1
    width = refs[0].shape[1]
    per_piece = nodes // width
    ordered = [jnp.zeros((1, nodes), F32) for _ in range(2)]
    for step in range(group):
        tail = refs[step][nodes:]
        for part in range(per_piece):
            moved = matmul(tail, wanted_places(nodes, group, step, part * width, width))
            for piece in range(2):
                row = piece * per_piece + part
                ordered[piece] = ordered[piece] + moved[row : row + 1]
    number = lax.broadcasted_iota(jnp.int32, (16, nodes), 0)
    packed = jnp.where(number == 0, ordered[0], jnp.where(number == 1, ordered[1], 0.0))
    pieces = matmul(packed.astype(BF16), places(order_ref), ((1,), (1,)))
    refs[-1][...] = (pieces[0:1] + 256.0 * pieces[1:2]).astype(jnp.int32)


def loss_kernel(*refs):
    group = len(refs) - 1
    height, nodes = refs[0].shape
    total = jnp.zeros((16, nodes), F32)
    for step in range(group):
        wanted = wanted_places(nodes, group, step, 0, nodes)
        total = total + matmul(refs[step][height - 16 :], wanted)
    refs[-1][...] = total[0:1] + total[1:2] + total[2:3]


def last_kernel(
    plan, row_scale, plan_ref,
    cur_ref, far_ref, near_ref, tiles_ref, before_ref, w_ref, wc_ref, order_ref, label_ref,
    out_ref, ext_ref,
):
    extend(cur_ref, far_ref, near_ref, ext_ref)
    blocks = next_blocks(plan, plan_ref, cur_ref, tiles_ref, ext_ref)
    halves = [block.astype(BF16) for block in blocks]
    rows_b = jnp.concatenate(halves, axis=0)
    size, width = halves[0].shape
    for number, half in enumerate(halves):
        columns = slice(number * width, (number + 1) * width)
        out_ref[:size, columns] = half
        out_ref[size : 2 * size, columns] = cur_ref[number].astype(BF16)
    size = 2 * size
    logits = before_ref[...] + branch_logits(w_ref.shape[0] - 1, rows_b, w_ref, wc_ref)
    classes, rows = logits.shape
    kept = up_to(classes, 16)
    hit = lax.broadcasted_iota(jnp.int32, (classes, rows), 0) == label_ref[...]
    top = jnp.max(logits, axis=0, keepdims=True)
    log_total = top + jnp.log(jnp.sum(jnp.exp(logits - top), axis=0, keepdims=True))
    loss = log_total - jnp.sum(jnp.where(hit, logits, 0.0), axis=0, keepdims=True)
    dlogits = (jnp.exp(logits - log_total) - jnp.where(hit, 1.0, 0.0)) * row_scale
    out_ref[size + kept - 16 : size + kept] = jnp.zeros((16, rows), BF16)
    out_ref[size : size + classes] = dlogits.astype(BF16)
    number = lax.broadcasted_iota(jnp.int32, (16, rows), 0)
    packed = jnp.zeros((16, rows), F32)
    rest = loss
    for piece in range(3):
        part = rest.astype(BF16).astype(F32)
        packed = jnp.where(number == piece, part, packed)
        rest = rest - part
    out_ref[size + kept :] = matmul(packed.astype(BF16), places(order_ref)).astype(BF16)


def weights_kernel(w_ref, wc_ref, wt_ref, wct_ref, pad_ref):
    branches, own, kept = wct_ref.shape
    classes = wc_ref.shape[0]
    hid = w_ref.shape[2]
    first = lax.axis_index("shuf") * own
    pad_ref[...] = jnp.zeros_like(pad_ref)
    for branch in range(branches):
        columns = w_ref[branch, :, pl.ds(pl.multiple_of(first, LANES), own)]
        wt_ref[branch] = columns.astype(F32).T.astype(BF16)
        columns = wc_ref[:, pl.ds(pl.multiple_of(branch * hid + first, LANES), own)]
        pad_ref[:classes] = columns.astype(F32)
        wct_ref[branch] = pad_ref[...].T[:, :kept].astype(BF16)


def add_chunks(kept, more, row_refs, last_refs, w_ref, wt_ref, wct_ref, chunks_ref):
    members = len(last_refs)
    branches, own, width = wt_ref.shape
    nodes = last_refs[0].shape[1]
    hid = w_ref.shape[2]
    parts = last_refs[0].shape[1] // width
    size = nodes // parts
    all_rows = []
    for branch in range(branches - 2):
        ours = row_refs[branch * members : (branch + 1) * members]
        all_rows.append(jnp.concatenate([ref[:nodes] for ref in ours], axis=0))
    for place in (1, 0):
        last_rows = []
        for ref in last_refs:
            for part in range(parts):
                columns = slice(part * width, (part + 1) * width)
                last_rows.append(ref[place * size : (place + 1) * size, columns])
        all_rows.append(jnp.concatenate(last_rows, axis=0))
    size = 2 * size
    dlogits_t = jnp.concatenate([ref[size : size + kept] for ref in last_refs], axis=1)
    own_class = branches * own
    first = lax.axis_index("shuf") * own_class
    which = first // hid
    columns = pl.ds(pl.multiple_of(first - which * hid, LANES), own_class)
    chosen = all_rows[0]
    for branch in range(1, branches):
        chosen = jnp.where(which == branch, all_rows[branch], chosen)

    def put(chunk, rows, value):
        chunks_ref[chunk, rows] = chunks_ref[chunk, rows] + value if more else value

    hidden = jnp.maximum(matmul(chosen, w_ref[which, :, columns]), 0.0).astype(BF16)
    class_t = matmul(dlogits_t, hidden)
    for chunk in range(chunks_ref.shape[0]):
        put(chunk, slice(0, kept), class_t[:, chunk * LANES : (chunk + 1) * LANES])
    per_branch = chunks_ref.shape[0] // branches
    for branch, rows in enumerate(all_rows):
        live = matmul(wt_ref[branch], rows, ((1,), (1,))) > 0.0
        dhidden_t = jnp.where(live, matmul(wct_ref[branch], dlogits_t), 0.0).astype(BF16)
        branch_t = matmul(dhidden_t, rows)
        for part in range(per_branch):
            put(
                branch * per_branch + part,
                slice(kept, kept + width),
                branch_t[part * LANES : (part + 1) * LANES],
            )


def early_kernel(kept, members, *refs):
    last = len(refs) - 4 - members
    add_chunks(kept, False, refs[:last], refs[last : last + members], *refs[last + members :])


def late_chunks(kept, members, early_ref, refs, chunks_ref):
    last = len(refs) - 3 - members
    chunks_ref[...] = early_ref[...]
    add_chunks(
        kept, True, refs[:last], refs[last : last + members], *refs[last + members :], chunks_ref
    )


def late_kernel(kept, members, half, early_ref, *refs):
    ins = len(refs) - 1 - half - half // 2
    outs = refs[ins:-1]
    chunks_ref = refs[-1]
    late_chunks(kept, members, early_ref, refs[:ins], chunks_ref)
    dom = lax.axis_index("dom")
    for step in range(half):
        stays = dom ^ (2 * step)
        outs[step][...] = chunks_ref[stays]
        outs[half + step // 2][step % 2] = chunks_ref[stays ^ 1].astype(BF16)


def plain_late_kernel(kept, members, early_ref, *refs):
    late_chunks(kept, members, early_ref, refs[:-1], refs[-1])


def write_chunk(kept, chunk, value, branch_ref, class_ref):
    per_branch = branch_ref.shape[2] // LANES
    start = pl.multiple_of(chunk * LANES, LANES)
    class_ref[:, pl.ds(start, LANES)] = value[: class_ref.shape[0]]
    branch = chunk // per_branch
    start = pl.multiple_of((chunk - branch * per_branch) * LANES, LANES)
    branch_ref[branch, :, pl.ds(start, LANES)] = value[kept:].T


def out_kernel(kept, *refs):
    ins, branch_ref, class_ref = refs[:-2], refs[-2], refs[-1]
    dom = lax.axis_index("dom")
    half = len(ins) // 2
    for step in range(half):
        for side in range(2):
            value = ins[side * half + step][...].astype(F32)
            write_chunk(kept, dom ^ (2 * step + side), value, branch_ref, class_ref)


def plain_out_kernel(kept, in_ref, branch_ref, class_ref):
    for chunk in range(in_ref.shape[0]):
        write_chunk(kept, chunk, in_ref[chunk], branch_ref, class_ref)


def in_group(value, distance=None):
    members = [value]
    steps = [0]
    distance = lax.axis_size("shuf") // 2 if distance is None else distance
    while distance:
        members += [swapped(member, distance, "shuf") for member in members]
        steps += [step + distance for step in steps]
        distance //= 2
    return [members[steps.index(step)] for step in range(len(steps))]


def body(
    features, tile_values, tile_dst, tile_src, tile_count, send_left, send_right,
    send_count, batch_order, labels, w_branch, w_class,
):
    block = tile_values.shape[1]
    nodes, width = features.shape
    local = nodes // block
    slots = send_left.shape[0]
    tiles = tile_values.shape[0]
    branches, _, hid = w_branch.shape
    cat, classes = w_class.shape
    dom = lax.axis_size("dom")
    shuf = lax.axis_size("shuf")
    mine = lax.axis_index("shuf")
    share = nodes // shuf
    own = hid // shuf
    own_class = cat // shuf
    kept = up_to(classes, 16)
    row_scale = 1.0 / math.sqrt(float(nodes * dom * shuf))
    plan = Plan(tiles, slots)
    small = jnp.concatenate(
        [tile_dst, tile_src, tile_count, send_left, send_right, send_count.reshape(-1)]
    )
    blocks_f32 = jax.ShapeDtypeStruct((local, block, width), F32)
    slots_f32 = jax.ShapeDtypeStruct((slots, block, width), F32)
    rows_b16 = jax.ShapeDtypeStruct((nodes, width), BF16)
    first_b16 = jax.ShapeDtypeStruct((nodes + 16, width), BF16)
    logits_f32 = jax.ShapeDtypeStruct((classes, nodes), F32)
    w_class_t = w_class.T

    current = features.reshape(local, block, width)
    gathered = []
    logits = None
    hop_flops = 12 * tiles * block * block * width
    forward_flops = 2 * nodes * hid * (width + classes)
    ext = pltpu.VMEM((local + 2 * slots, block, width), F32)
    to_far, to_near, current, rows = call(
        first_kernel,
        [slots_f32, slots_f32, blocks_f32, first_b16],
        [ANYWHERE] * 5,
        1000,
        [
            pltpu.SMEM((slots,), jnp.int32),
            pltpu.SMEM((slots,), jnp.int32),
            pltpu.SMEM((1, 2), jnp.int32),
            pltpu.VMEM((1, nodes), jnp.int32),
            pltpu.SemaphoreType.DMA((5,)),
        ],
        limit=VMEM_ALL,
    )(send_left, send_right, send_count, current, labels.reshape(1, nodes))
    current, tile_values = call(
        ready_kernel,
        [blocks_f32, jax.ShapeDtypeStruct(tile_values.shape, F32)],
        [IN_VMEM] * 2,
        1000,
    )(current, tile_values)
    for hop in range(HOPS):
        from_far = far_pairs(to_far)
        from_near = near_pairs(to_near)
        if hop < HOPS - 1:
            gathered.append(in_group(rows))
        before = [] if logits is None else [logits]
        logits = call(
            functools.partial(forward_kernel, hop),
            logits_f32,
            [IN_VMEM] * (3 + len(before)),
            forward_flops,
            after=[members[shuf // 2] for members in gathered] if hop == HOPS - 1 else [],
        )(current, w_branch, w_class_t, *before)
        if hop == 0:
            first_logits = logits
            after = []
        else:
            after = [first_logits]
        if hop < HOPS - 1:
            current, to_far, to_near, rows = call(
                functools.partial(hop_kernel, plan),
                [blocks_f32, slots_f32, slots_f32, rows_b16],
                [IN_SMEM] + [IN_VMEM] * 4,
                hop_flops,
                [ext],
                after,
            )(small, current, from_far, from_near, tile_values)

    label_mine = call(
        label_kernel,
        jax.ShapeDtypeStruct((1, nodes), jnp.int32),
        [IN_VMEM] * (1 + shuf),
        1000,
    )(batch_order, *gathered[0])

    wt_own, wct_own = call(
        weights_kernel,
        [
            jax.ShapeDtypeStruct((branches, own, width), BF16),
            jax.ShapeDtypeStruct((branches, own, kept), BF16),
        ],
        [IN_VMEM] * 2,
        1000,
        [pltpu.VMEM((up_to(classes, LANES), own), F32)],
    )(w_branch, w_class_t)

    payload = call(
        functools.partial(last_kernel, plan, row_scale),
        jax.ShapeDtypeStruct((2 * block + kept + 16, local * width), BF16),
        [IN_SMEM] + [IN_VMEM] * 9,
        hop_flops + forward_flops,
        [ext],
        gathered[1][1:],
    )(
        small, current, from_far, from_near, tile_values,
        logits, w_branch, w_class_t, batch_order, label_mine,
    )
    chunks = own_class // LANES
    height = kept + width
    ahead = shuf // 2
    chunks_f32 = jax.ShapeDtypeStruct((chunks, height, LANES), F32)
    grad_flops = shuf * nodes * own_class * (3 * width + 2 * kept)
    weights = (w_branch, wt_own, wct_own)
    across = swapped(payload, ahead, "shuf")
    close = in_group(payload, ahead // 2)
    early = call(
        functools.partial(early_kernel, kept, ahead),
        chunks_f32,
        [IN_VMEM] * (3 * ahead + 3),
        grad_flops,
    )(*[member for members in gathered for member in members[:ahead]], *close, *weights)
    across, early = lax.optimization_barrier((across, early))
    distant = in_group(across, ahead // 2)
    late_ins = (
        early, *[member for members in gathered for member in members[ahead:]], *distant, *weights
    )
    last_all = close + distant
    loss_rows = call(
        loss_kernel, jax.ShapeDtypeStruct((1, nodes), F32), [IN_VMEM] * shuf, 1000
    )(*last_all).reshape(nodes)

    outs = [
        jax.ShapeDtypeStruct((branches, width, own), F32),
        jax.ShapeDtypeStruct((classes, own_class), F32),
    ]
    if chunks == dom and dom % 4 == 0 and dom & (dom - 1) == 0:
        half = dom // 2
        one_f32 = jax.ShapeDtypeStruct((height, LANES), F32)
        two_b16 = jax.ShapeDtypeStruct((2, height, LANES), BF16)
        made = call(
            functools.partial(late_kernel, kept, ahead, half),
            [one_f32] * half + [two_b16] * (half // 2),
            [IN_VMEM] * len(late_ins),
            grad_flops,
            [pltpu.VMEM(chunks_f32.shape, F32)],
        )(*late_ins)
        order = list(range(half - 1, -1, -1))
        arrived = {pair: swapped(made[half + pair], 1) for pair in range(half // 2 - 1, -1, -1)}
        total = {
            step: made[step] + arrived[step // 2][step % 2].astype(F32) for step in order
        }
        far = [swapped(total[step].astype(BF16), 2 * step) for step in order[:-1]]
        summed = total[0]
        for value in far:
            summed = summed + value.astype(F32)
        near = {0: summed.astype(BF16)}
        other = {0: swapped(near[0], 1)}
        for step in order[:-1]:
            near[step] = swapped(near[0], 2 * step)
        for step in range(1, half):
            other[step] = swapped(near[step], 1)
        near = [near[step] for step in range(half)]
        other = [other[step] for step in range(half)]
        grad_branch, grad_class_t = call(
            functools.partial(out_kernel, kept), outs, [IN_VMEM] * dom, 1000
        )(*near, *other)
    else:
        grads = call(
            functools.partial(plain_late_kernel, kept, ahead),
            chunks_f32,
            [IN_VMEM] * len(late_ins),
            grad_flops,
        )(*late_ins)
        grad_branch, grad_class_t = call(
            functools.partial(plain_out_kernel, kept), outs, [IN_VMEM], 1000
        )(lax.psum(grads, "dom"))
    return (loss_rows, grad_branch, grad_class_t.T)


def solution(mesh):
    return jax.shard_map(
        body,
        mesh=mesh,
        in_specs=(
            P(("dom", "shuf"), None),
            P(("dom", "shuf"), None, None),
            P(("dom", "shuf")),
            P(("dom", "shuf")),
            P(("dom", "shuf")),
            P(("dom", "shuf")),
            P(("dom", "shuf")),
            P(("dom", "shuf"), None),
            P(("dom", "shuf"), None),
            P(("dom", "shuf")),
            P(),
            P(),
        ),
        out_specs=(P(("dom", "shuf")), P(None, None, "shuf"), P("shuf", None)),
        check_vma=False,
    )
```

```python
import functools
import math

import jax
import jax.numpy as jnp
from jax import lax
from jax.experimental import pallas as pl
from jax.experimental.pallas import tpu as pltpu
from jax.sharding import PartitionSpec as P

HOPS = 3
LANES = 128
VMEM_LIMIT = 24 * 1024 * 1024
VMEM_ALL = 56 * 1024 * 1024

IN_VMEM = pl.BlockSpec(memory_space=pltpu.VMEM)
IN_SMEM = pl.BlockSpec(memory_space=pltpu.SMEM)
ANYWHERE = pl.BlockSpec(memory_space=pl.ANY)
BF16 = jnp.bfloat16
F32 = jnp.float32


def up_to(value, multiple):
    return -(-value // multiple) * multiple


def passed_along(value, axis, steps):
    count = lax.axis_size(axis)
    pairs = [(source, (source + steps) % count) for source in range(count)]
    return lax.ppermute(value, axis, pairs)


def swapped(value, distance, axis="dom"):
    pairs = [(source, source ^ distance) for source in range(lax.axis_size(axis))]
    return lax.ppermute(value, axis, pairs)


def matmul(left, right, dims=((1,), (0,)), precision=None):
    return lax.dot_general(
        left, right, (dims, ((), ())), precision=precision, preferred_element_type=F32
    )


def call(kernel, out_shape, in_specs, flops, scratch=(), after=(), limit=VMEM_LIMIT):
    many = isinstance(out_shape, (list, tuple))
    outs = out_shape if many else [out_shape]
    moved = sum(math.prod(one.shape) * one.dtype.itemsize for one in outs)
    waited = len(after)

    def run(*refs):
        kernel(*refs[waited:])

    made = pl.pallas_call(
        run,
        out_shape=out_shape,
        in_specs=[ANYWHERE] * waited + in_specs,
        out_specs=[IN_VMEM] * len(outs) if many else IN_VMEM,
        scratch_shapes=list(scratch),
        compiler_params=pltpu.CompilerParams(vmem_limit_bytes=limit),
        cost_estimate=pl.CostEstimate(
            flops=flops, bytes_accessed=3 * moved, transcendentals=0
        ),
    )
    return functools.partial(made, *after)


class Plan:
    def __init__(self, tiles, slots):
        self.tiles = tiles
        self.slots = slots
        self.dst = 0
        self.src = tiles
        self.count = 2 * tiles
        self.left = 2 * tiles + 1
        self.right = self.left + slots
        self.sent = self.right + slots


def write_sends(blocks, left_ref, right_ref, ids, counts):
    for slot in range(left_ref.shape[0]):
        for side, out_ref in enumerate((left_ref, right_ref)):
            index = ids(side, slot)
            picked = blocks[0]
            for number in range(1, len(blocks)):
                picked = jnp.where(index == number, blocks[number], picked)
            out_ref[slot] = jnp.where(slot < counts(side), picked, 0.0)


def copied(sources, targets, sems):
    copies = [
        pltpu.make_async_copy(source, target, sems.at[number])
        for number, (source, target) in enumerate(zip(sources, targets))
    ]
    for copy in copies:
        copy.start()
    for copy in copies:
        copy.wait()


def first_kernel(
    sl_ref, sr_ref, sc_ref, feat_ref, label_from,
    left_ref, right_ref, held_ref, b_ref,
    sl_here, sr_here, sc_here, label_ref, sems,
):
    copied(
        (sl_ref, sr_ref, sc_ref, feat_ref, label_from),
        (sl_here, sr_here, sc_here, held_ref, label_ref),
        sems,
    )
    blocks = [held_ref[number] for number in range(held_ref.shape[0])]
    write_sends(
        blocks,
        left_ref,
        right_ref,
        lambda side, slot: (sl_here, sr_here)[side][slot],
        lambda side: sc_here[0, side],
    )
    write_rows(blocks, b_ref)
    nodes = label_ref.shape[1]
    width = b_ref.shape[1]
    per_piece = nodes // width
    place = lax.broadcasted_iota(jnp.int32, (16, width), 0)
    packed = jnp.zeros((16, width), F32)
    for piece in range(2):
        value = label_ref[...] & 255 if piece == 0 else label_ref[...] >> 8
        value = value.astype(F32)
        for part in range(per_piece):
            packed = jnp.where(
                place == piece * per_piece + part,
                value[:, part * width : (part + 1) * width],
                packed,
            )
    b_ref[nodes:] = packed.astype(BF16)


def write_rows(blocks, b_ref):
    for number, block in enumerate(blocks):
        size = block.shape[0]
        b_ref[number * size : (number + 1) * size] = block.astype(BF16)


def next_blocks(plan, plan_ref, cur_ref, tiles_ref, ext_ref):
    local = cur_ref.shape[0]
    ext_ref[:local] = cur_ref[...]
    totals = [jnp.zeros(cur_ref.shape[1:], F32) for _ in range(local)]
    live = plan_ref[plan.count]
    for tile in range(plan.tiles):
        product = matmul(
            tiles_ref[tile],
            ext_ref[plan_ref[plan.src + tile]],
            precision=lax.Precision.HIGHEST,
        )
        wanted = jnp.where(tile < live, plan_ref[plan.dst + tile], -1)
        for number in range(local):
            totals[number] = totals[number] + jnp.where(wanted == number, product, 0.0)
    return totals


def extend(cur_ref, low_ref, high_ref, ext_ref):
    local = cur_ref.shape[0]
    slots = low_ref.shape[0]
    ext_ref[local : local + slots] = low_ref[...]
    ext_ref[local + slots :] = high_ref[...]


def hop_kernel(
    plan, plan_ref, cur_ref, low_ref, high_ref, tiles_ref,
    next_ref, left_ref, right_ref, b_ref, ext_ref,
):
    extend(cur_ref, low_ref, high_ref, ext_ref)
    blocks = next_blocks(plan, plan_ref, cur_ref, tiles_ref, ext_ref)
    write_sends(
        blocks,
        left_ref,
        right_ref,
        lambda side, slot: plan_ref[(plan.left, plan.right)[side] + slot],
        lambda side: plan_ref[plan.sent + side],
    )
    for number, block in enumerate(blocks):
        next_ref[number] = block
    write_rows(blocks, b_ref)


def ready_kernel(cur_ref, tiles_ref, cur_out, tiles_out):
    cur_out[...] = cur_ref[...]
    tiles_out[...] = tiles_ref[...]


def branch_logits(branch, rows, w_ref, wc_ref):
    hidden = jnp.maximum(matmul(rows, w_ref[branch]), 0.0).astype(BF16)
    hid = hidden.shape[1]
    return matmul(wc_ref[:, branch * hid : (branch + 1) * hid], hidden, ((1,), (1,)))


def forward_kernel(branch, cur_ref, w_ref, wc_ref, *refs):
    rows = cur_ref[...].reshape(-1, cur_ref.shape[2]).astype(BF16)
    part = branch_logits(branch, rows, w_ref, wc_ref)
    if len(refs) == 2:
        part = refs[0][...] + part
    refs[-1][...] = part


def places(order_ref):
    nodes = order_ref.shape[1]
    rows = lax.broadcasted_iota(jnp.int32, (nodes, nodes), 0)
    return (order_ref[...] == rows).astype(F32).astype(BF16)


def wanted_places(nodes, group, step, offset, count):
    share = nodes // group
    mine = lax.axis_index("shuf")
    first = mine * share
    source = lax.broadcasted_iota(jnp.int32, (count, nodes), 0) + offset
    target = lax.broadcasted_iota(jnp.int32, (count, nodes), 1)
    moved = source + ((mine ^ step) - mine) * share
    wanted = (target == moved) & (source >= first) & (source < first + share)
    return wanted.astype(F32).astype(BF16)


def label_kernel(order_ref, *refs):
    nodes = order_ref.shape[1]
    group = len(refs) - 1
    width = refs[0].shape[1]
    per_piece = nodes // width
    ordered = [jnp.zeros((1, nodes), F32) for _ in range(2)]
    for step in range(group):
        tail = refs[step][nodes:]
        for part in range(per_piece):
            moved = matmul(tail, wanted_places(nodes, group, step, part * width, width))
            for piece in range(2):
                row = piece * per_piece + part
                ordered[piece] = ordered[piece] + moved[row : row + 1]
    number = lax.broadcasted_iota(jnp.int32, (16, nodes), 0)
    packed = jnp.where(number == 0, ordered[0], jnp.where(number == 1, ordered[1], 0.0))
    pieces = matmul(packed.astype(BF16), places(order_ref), ((1,), (1,)))
    refs[-1][...] = (pieces[0:1] + 256.0 * pieces[1:2]).astype(jnp.int32)


def loss_kernel(*refs):
    group = len(refs) - 1
    height, nodes = refs[0].shape
    total = jnp.zeros((16, nodes), F32)
    for step in range(group):
        wanted = wanted_places(nodes, group, step, 0, nodes)
        total = total + matmul(refs[step][height - 16 :], wanted)
    refs[-1][...] = total[0:1] + total[1:2] + total[2:3]


def last_hop_kernel(plan, plan_ref, cur_ref, low_ref, high_ref, tiles_ref, out_ref, ext_ref):
    extend(cur_ref, low_ref, high_ref, ext_ref)
    blocks = next_blocks(plan, plan_ref, cur_ref, tiles_ref, ext_ref)
    for number, block in enumerate(blocks):
        size, width = block.shape
        columns = slice(number * width, (number + 1) * width)
        out_ref[:size, columns] = block.astype(BF16)
        out_ref[size:, columns] = cur_ref[number].astype(BF16)


def stacked(ref, place, width):
    size = ref.shape[0] // 2
    parts = ref.shape[1] // width
    return [
        ref[place * size : (place + 1) * size, part * width : (part + 1) * width]
        for part in range(parts)
    ]


def loss_and_gradient_kernel(
    row_scale, rows_ref, before_ref, w_ref, wc_ref, order_ref, label_ref, out_ref
):
    rows_b = jnp.concatenate(stacked(rows_ref, 0, w_ref.shape[1]), axis=0)
    logits = before_ref[...] + branch_logits(w_ref.shape[0] - 1, rows_b, w_ref, wc_ref)
    classes, rows = logits.shape
    kept = up_to(classes, 16)
    hit = lax.broadcasted_iota(jnp.int32, (classes, rows), 0) == label_ref[...]
    top = jnp.max(logits, axis=0, keepdims=True)
    log_total = top + jnp.log(jnp.sum(jnp.exp(logits - top), axis=0, keepdims=True))
    loss = log_total - jnp.sum(jnp.where(hit, logits, 0.0), axis=0, keepdims=True)
    dlogits = (jnp.exp(logits - log_total) - jnp.where(hit, 1.0, 0.0)) * row_scale
    out_ref[kept - 16 : kept] = jnp.zeros((16, rows), BF16)
    out_ref[:classes] = dlogits.astype(BF16)
    number = lax.broadcasted_iota(jnp.int32, (16, rows), 0)
    packed = jnp.zeros((16, rows), F32)
    rest = loss
    for piece in range(3):
        part = rest.astype(BF16).astype(F32)
        packed = jnp.where(number == piece, part, packed)
        rest = rest - part
    out_ref[kept:] = matmul(packed.astype(BF16), places(order_ref)).astype(BF16)


def weights_kernel(w_ref, wc_ref, wt_ref, wct_ref, pad_ref):
    branches, own, kept = wct_ref.shape
    classes = wc_ref.shape[0]
    hid = w_ref.shape[2]
    first = lax.axis_index("shuf") * own
    pad_ref[...] = jnp.zeros_like(pad_ref)
    for branch in range(branches):
        columns = w_ref[branch, :, pl.ds(pl.multiple_of(first, LANES), own)]
        wt_ref[branch] = columns.astype(F32).T.astype(BF16)
        columns = wc_ref[:, pl.ds(pl.multiple_of(branch * hid + first, LANES), own)]
        pad_ref[:classes] = columns.astype(F32)
        wct_ref[branch] = pad_ref[...].T[:, :kept].astype(BF16)


def add_chunks(kept, more, row_refs, last_refs, dlogit_refs, w_ref, wt_ref, wct_ref, chunks_ref):
    members = len(last_refs)
    branches, own, width = wt_ref.shape
    nodes = last_refs[0].shape[1]
    hid = w_ref.shape[2]
    all_rows = []
    for branch in range(branches - 2):
        ours = row_refs[branch * members : (branch + 1) * members]
        all_rows.append(jnp.concatenate([ref[:nodes] for ref in ours], axis=0))
    for place in (1, 0):
        ours = [rows for ref in last_refs for rows in stacked(ref, place, width)]
        all_rows.append(jnp.concatenate(ours, axis=0))
    dlogits_t = jnp.concatenate([ref[:kept] for ref in dlogit_refs], axis=1)
    own_class = branches * own
    first = lax.axis_index("shuf") * own_class
    which = first // hid
    columns = pl.ds(pl.multiple_of(first - which * hid, LANES), own_class)
    chosen = all_rows[0]
    for branch in range(1, branches):
        chosen = jnp.where(which == branch, all_rows[branch], chosen)

    def put(chunk, rows, value):
        chunks_ref[chunk, rows] = chunks_ref[chunk, rows] + value if more else value

    hidden = jnp.maximum(matmul(chosen, w_ref[which, :, columns]), 0.0).astype(BF16)
    class_t = matmul(dlogits_t, hidden)
    for chunk in range(chunks_ref.shape[0]):
        put(chunk, slice(0, kept), class_t[:, chunk * LANES : (chunk + 1) * LANES])
    per_branch = chunks_ref.shape[0] // branches
    for branch, rows in enumerate(all_rows):
        live = matmul(wt_ref[branch], rows, ((1,), (1,))) > 0.0
        dhidden_t = jnp.where(live, matmul(wct_ref[branch], dlogits_t), 0.0).astype(BF16)
        branch_t = matmul(dhidden_t, rows)
        for part in range(per_branch):
            put(
                branch * per_branch + part,
                slice(kept, kept + width),
                branch_t[part * LANES : (part + 1) * LANES],
            )


def split_refs(members, refs):
    last = len(refs) - 3 - 2 * members
    return (
        refs[:last], refs[last : last + members], refs[last + members : last + 2 * members],
        *refs[last + 2 * members :],
    )


def early_kernel(kept, members, *refs):
    add_chunks(kept, False, *split_refs(members, refs[:-1]), refs[-1])


def late_chunks(kept, members, early_ref, refs, chunks_ref):
    chunks_ref[...] = early_ref[...]
    add_chunks(kept, True, *split_refs(members, refs), chunks_ref)


def late_kernel(kept, members, half, early_ref, *refs):
    ins = len(refs) - 1 - half - half // 2
    outs = refs[ins:-1]
    chunks_ref = refs[-1]
    late_chunks(kept, members, early_ref, refs[:ins], chunks_ref)
    dom = lax.axis_index("dom")
    for step in range(half):
        stays = dom ^ (2 * step)
        outs[step][...] = chunks_ref[stays]
        outs[half + step // 2][step % 2] = chunks_ref[stays ^ 1].astype(BF16)


def plain_late_kernel(kept, members, early_ref, *refs):
    late_chunks(kept, members, early_ref, refs[:-1], refs[-1])


def write_chunk(kept, chunk, value, branch_ref, class_ref):
    per_branch = branch_ref.shape[2] // LANES
    start = pl.multiple_of(chunk * LANES, LANES)
    class_ref[:, pl.ds(start, LANES)] = value[: class_ref.shape[0]]
    branch = chunk // per_branch
    start = pl.multiple_of((chunk - branch * per_branch) * LANES, LANES)
    branch_ref[branch, :, pl.ds(start, LANES)] = value[kept:].T


def out_kernel(kept, *refs):
    ins, branch_ref, class_ref = refs[:-2], refs[-2], refs[-1]
    dom = lax.axis_index("dom")
    half = len(ins) // 2
    for step in range(half):
        for side in range(2):
            value = ins[side * half + step][...].astype(F32)
            write_chunk(kept, dom ^ (2 * step + side), value, branch_ref, class_ref)


def plain_out_kernel(kept, in_ref, branch_ref, class_ref):
    for chunk in range(in_ref.shape[0]):
        write_chunk(kept, chunk, in_ref[chunk], branch_ref, class_ref)


def in_group(value, distance=None):
    members = [value]
    steps = [0]
    distance = lax.axis_size("shuf") // 2 if distance is None else distance
    while distance:
        members += [swapped(member, distance, "shuf") for member in members]
        steps += [step + distance for step in steps]
        distance //= 2
    return [members[steps.index(step)] for step in range(len(steps))]


def body(
    features, tile_values, tile_dst, tile_src, tile_count, send_left, send_right,
    send_count, batch_order, labels, w_branch, w_class,
):
    block = tile_values.shape[1]
    nodes, width = features.shape
    local = nodes // block
    slots = send_left.shape[0]
    tiles = tile_values.shape[0]
    branches, _, hid = w_branch.shape
    cat, classes = w_class.shape
    dom = lax.axis_size("dom")
    shuf = lax.axis_size("shuf")
    mine = lax.axis_index("shuf")
    share = nodes // shuf
    own = hid // shuf
    own_class = cat // shuf
    kept = up_to(classes, 16)
    row_scale = 1.0 / math.sqrt(float(nodes * dom * shuf))
    plan = Plan(tiles, slots)
    small = jnp.concatenate(
        [tile_dst, tile_src, tile_count, send_left, send_right, send_count.reshape(-1)]
    )
    blocks_f32 = jax.ShapeDtypeStruct((local, block, width), F32)
    slots_f32 = jax.ShapeDtypeStruct((slots, block, width), F32)
    rows_b16 = jax.ShapeDtypeStruct((nodes, width), BF16)
    first_b16 = jax.ShapeDtypeStruct((nodes + 16, width), BF16)
    logits_f32 = jax.ShapeDtypeStruct((classes, nodes), F32)
    w_class_t = w_class.T

    current = features.reshape(local, block, width)
    gathered = []
    logits = None
    hop_flops = 12 * tiles * block * block * width
    forward_flops = 2 * nodes * hid * (width + classes)
    ext = pltpu.VMEM((local + 2 * slots, block, width), F32)
    to_left, to_right, current, rows = call(
        first_kernel,
        [slots_f32, slots_f32, blocks_f32, first_b16],
        [ANYWHERE] * 5,
        1000,
        [
            pltpu.SMEM((slots,), jnp.int32),
            pltpu.SMEM((slots,), jnp.int32),
            pltpu.SMEM((1, 2), jnp.int32),
            pltpu.VMEM((1, nodes), jnp.int32),
            pltpu.SemaphoreType.DMA((5,)),
        ],
        limit=VMEM_ALL,
    )(send_left, send_right, send_count, current, labels.reshape(1, nodes))
    current, tile_values = call(
        ready_kernel,
        [blocks_f32, jax.ShapeDtypeStruct(tile_values.shape, F32)],
        [IN_VMEM] * 2,
        1000,
    )(current, tile_values)
    for hop in range(HOPS):
        from_lower = passed_along(to_right, "dom", 1)
        from_upper = passed_along(to_left, "dom", -1)
        if hop < HOPS - 1:
            gathered.append(in_group(rows))
        before = [] if logits is None else [logits]
        logits = call(
            functools.partial(forward_kernel, hop),
            logits_f32,
            [IN_VMEM] * (3 + len(before)),
            forward_flops,
            after=[members[shuf // 2] for members in gathered] if hop == HOPS - 1 else [],
        )(current, w_branch, w_class_t, *before)
        if hop == 0:
            first_logits = logits
            after = []
        else:
            after = [first_logits]
        if hop < HOPS - 1:
            current, to_left, to_right, rows = call(
                functools.partial(hop_kernel, plan),
                [blocks_f32, slots_f32, slots_f32, rows_b16],
                [IN_SMEM] + [IN_VMEM] * 4,
                hop_flops,
                [ext],
                after,
            )(small, current, from_lower, from_upper, tile_values)

    label_mine = call(
        label_kernel,
        jax.ShapeDtypeStruct((1, nodes), jnp.int32),
        [IN_VMEM] * (1 + shuf),
        1000,
    )(batch_order, *gathered[0])

    wt_own, wct_own = call(
        weights_kernel,
        [
            jax.ShapeDtypeStruct((branches, own, width), BF16),
            jax.ShapeDtypeStruct((branches, own, kept), BF16),
        ],
        [IN_VMEM] * 2,
        1000,
        [pltpu.VMEM((up_to(classes, LANES), own), F32)],
    )(w_branch, w_class_t)

    last_rows = call(
        functools.partial(last_hop_kernel, plan),
        jax.ShapeDtypeStruct((2 * block, local * width), BF16),
        [IN_SMEM] + [IN_VMEM] * 4,
        hop_flops,
        [ext],
        [logits, label_mine, *gathered[1][1:]],
    )(small, current, from_lower, from_upper, tile_values)
    dlogits = call(
        functools.partial(loss_and_gradient_kernel, row_scale),
        jax.ShapeDtypeStruct((kept + 16, nodes), BF16),
        [IN_VMEM] * 6,
        forward_flops,
    )(last_rows, logits, w_branch, w_class_t, batch_order, label_mine)
    chunks = own_class // LANES
    height = kept + width
    ahead = shuf // 2
    chunks_f32 = jax.ShapeDtypeStruct((chunks, height, LANES), F32)
    grad_flops = shuf * nodes * own_class * (3 * width + 2 * kept)
    weights = (w_branch, wt_own, wct_own)
    across_rows = swapped(last_rows, ahead, "shuf")
    across = swapped(dlogits, ahead, "shuf")
    close_rows = in_group(last_rows, ahead // 2)
    close = in_group(dlogits, ahead // 2)
    early = call(
        functools.partial(early_kernel, kept, ahead),
        chunks_f32,
        [IN_VMEM] * (4 * ahead + 3),
        grad_flops,
    )(
        *[member for members in gathered for member in members[:ahead]],
        *close_rows, *close, *weights,
    )
    across, across_rows, early = lax.optimization_barrier((across, across_rows, early))
    distant_rows = in_group(across_rows, ahead // 2)
    distant = in_group(across, ahead // 2)
    late_ins = (
        early, *[member for members in gathered for member in members[ahead:]],
        *distant_rows, *distant, *weights,
    )
    last_all = close + distant
    loss_rows = call(
        loss_kernel, jax.ShapeDtypeStruct((1, nodes), F32), [IN_VMEM] * shuf, 1000
    )(*last_all).reshape(nodes)

    outs = [
        jax.ShapeDtypeStruct((branches, width, own), F32),
        jax.ShapeDtypeStruct((classes, own_class), F32),
    ]
    if chunks == dom and dom % 4 == 0 and dom & (dom - 1) == 0:
        half = dom // 2
        one_f32 = jax.ShapeDtypeStruct((height, LANES), F32)
        two_b16 = jax.ShapeDtypeStruct((2, height, LANES), BF16)
        made = call(
            functools.partial(late_kernel, kept, ahead, half),
            [one_f32] * half + [two_b16] * (half // 2),
            [IN_VMEM] * len(late_ins),
            grad_flops,
            [pltpu.VMEM(chunks_f32.shape, F32)],
        )(*late_ins)
        order = list(range(half - 1, -1, -1))
        arrived = {}
        for pair in range(half // 2 - 1, -1, -1):
            going = made[half + pair]
            if arrived:
                arrived[pair + 1], going = lax.optimization_barrier((arrived[pair + 1], going))
            arrived[pair] = swapped(going, 1)
        total = {
            step: made[step] + arrived[step // 2][step % 2].astype(F32) for step in order
        }
        far = [swapped(total[step].astype(BF16), 2 * step) for step in order[:-1]]
        summed = total[0]
        for value in far:
            summed = summed + value.astype(F32)
        near = {0: summed.astype(BF16)}
        other = {0: swapped(near[0], 1)}
        for step in order[:-1]:
            near[step] = swapped(near[0], 2 * step)
        for step in range(1, half):
            other[step] = swapped(near[step], 1)
        near = [near[step] for step in range(half)]
        other = [other[step] for step in range(half)]
        grad_branch, grad_class_t = call(
            functools.partial(out_kernel, kept), outs, [IN_VMEM] * dom, 1000
        )(*near, *other)
    else:
        grads = call(
            functools.partial(plain_late_kernel, kept, ahead),
            chunks_f32,
            [IN_VMEM] * len(late_ins),
            grad_flops,
        )(*late_ins)
        grad_branch, grad_class_t = call(
            functools.partial(plain_out_kernel, kept), outs, [IN_VMEM], 1000
        )(lax.psum(grads, "dom"))
    return (loss_rows, grad_branch, grad_class_t.T)


def solution(mesh):
    return jax.shard_map(
        body,
        mesh=mesh,
        in_specs=(
            P(("dom", "shuf"), None),
            P(("dom", "shuf"), None, None),
            P(("dom", "shuf")),
            P(("dom", "shuf")),
            P(("dom", "shuf")),
            P(("dom", "shuf")),
            P(("dom", "shuf")),
            P(("dom", "shuf"), None),
            P(("dom", "shuf"), None),
            P(("dom", "shuf")),
            P(),
            P(),
        ),
        out_specs=(P(("dom", "shuf")), P(None, None, "shuf"), P("shuf", None)),
        check_vma=False,
    )
```

```python
import functools
import math

import jax
import jax.numpy as jnp
from jax import lax
from jax.experimental import pallas as pl
from jax.experimental.pallas import tpu as pltpu
from jax.sharding import PartitionSpec as P

HOPS = 3
LANES = 128
VMEM_LIMIT = 24 * 1024 * 1024
VMEM_ALL = 56 * 1024 * 1024

IN_VMEM = pl.BlockSpec(memory_space=pltpu.VMEM)
IN_SMEM = pl.BlockSpec(memory_space=pltpu.SMEM)
ANYWHERE = pl.BlockSpec(memory_space=pl.ANY)
BF16 = jnp.bfloat16
F32 = jnp.float32


def up_to(value, multiple):
    return -(-value // multiple) * multiple


def passed_along(value, axis, steps):
    count = lax.axis_size(axis)
    pairs = [(source, (source + steps) % count) for source in range(count)]
    return lax.ppermute(value, axis, pairs)


def swapped(value, distance, axis="dom"):
    pairs = [(source, source ^ distance) for source in range(lax.axis_size(axis))]
    return lax.ppermute(value, axis, pairs)


def matmul(left, right, dims=((1,), (0,)), precision=None):
    return lax.dot_general(
        left, right, (dims, ((), ())), precision=precision, preferred_element_type=F32
    )


def call(kernel, out_shape, in_specs, flops, scratch=(), after=(), limit=VMEM_LIMIT):
    many = isinstance(out_shape, (list, tuple))
    outs = out_shape if many else [out_shape]
    moved = sum(math.prod(one.shape) * one.dtype.itemsize for one in outs)
    waited = len(after)

    def run(*refs):
        kernel(*refs[waited:])

    made = pl.pallas_call(
        run,
        out_shape=out_shape,
        in_specs=[ANYWHERE] * waited + in_specs,
        out_specs=[IN_VMEM] * len(outs) if many else IN_VMEM,
        scratch_shapes=list(scratch),
        compiler_params=pltpu.CompilerParams(vmem_limit_bytes=limit),
        cost_estimate=pl.CostEstimate(
            flops=flops, bytes_accessed=3 * moved if flops > 1000 else 1000, transcendentals=0
        ),
    )
    return functools.partial(made, *after)


class Plan:
    def __init__(self, tiles, slots):
        self.tiles = tiles
        self.slots = slots
        self.dst = 0
        self.src = tiles
        self.count = 2 * tiles
        self.left = 2 * tiles + 1
        self.right = self.left + slots
        self.sent = self.right + slots


def write_sends(blocks, left_ref, right_ref, ids, counts):
    for slot in range(left_ref.shape[0]):
        for side, out_ref in enumerate((left_ref, right_ref)):
            index = ids(side, slot)
            picked = blocks[0]
            for number in range(1, len(blocks)):
                picked = jnp.where(index == number, blocks[number], picked)
            out_ref[slot] = jnp.where(slot < counts(side), picked, 0.0)


def copied(sources, targets, sems):
    copies = [
        pltpu.make_async_copy(source, target, sems.at[number])
        for number, (source, target) in enumerate(zip(sources, targets))
    ]
    for copy in copies:
        copy.start()
    for copy in copies:
        copy.wait()


def first_kernel(
    sl_ref, sr_ref, sc_ref, feat_ref, label_from,
    left_ref, right_ref, held_ref, b_ref,
    sl_here, sr_here, sc_here, label_ref, sems,
):
    copied(
        (sl_ref, sr_ref, sc_ref, feat_ref, label_from),
        (sl_here, sr_here, sc_here, held_ref, label_ref),
        sems,
    )
    blocks = [held_ref[number] for number in range(held_ref.shape[0])]
    write_sends(
        blocks,
        left_ref,
        right_ref,
        lambda side, slot: (sl_here, sr_here)[side][slot],
        lambda side: sc_here[0, side],
    )
    write_rows(blocks, b_ref)
    nodes = label_ref.shape[1]
    width = b_ref.shape[1]
    per_piece = nodes // width
    place = lax.broadcasted_iota(jnp.int32, (16, width), 0)
    packed = jnp.zeros((16, width), F32)
    for piece in range(2):
        value = label_ref[...] & 255 if piece == 0 else label_ref[...] >> 8
        value = value.astype(F32)
        for part in range(per_piece):
            packed = jnp.where(
                place == piece * per_piece + part,
                value[:, part * width : (part + 1) * width],
                packed,
            )
    b_ref[nodes:] = packed.astype(BF16)


def write_rows(blocks, b_ref):
    for number, block in enumerate(blocks):
        size = block.shape[0]
        b_ref[number * size : (number + 1) * size] = block.astype(BF16)


def next_blocks(plan, plan_ref, cur_ref, tiles_ref, ext_ref):
    local = cur_ref.shape[0]
    ext_ref[:local] = cur_ref[...]
    totals = [jnp.zeros(cur_ref.shape[1:], F32) for _ in range(local)]
    live = plan_ref[plan.count]
    for tile in range(plan.tiles):
        product = matmul(
            tiles_ref[tile],
            ext_ref[plan_ref[plan.src + tile]],
            precision=lax.Precision.HIGHEST,
        )
        wanted = jnp.where(tile < live, plan_ref[plan.dst + tile], -1)
        for number in range(local):
            totals[number] = totals[number] + jnp.where(wanted == number, product, 0.0)
    return totals


def extend(cur_ref, low_ref, high_ref, ext_ref):
    local = cur_ref.shape[0]
    slots = low_ref.shape[0]
    ext_ref[local : local + slots] = low_ref[...]
    ext_ref[local + slots :] = high_ref[...]


def hop_kernel(
    plan, plan_ref, cur_ref, low_ref, high_ref, tiles_ref, next_ref, left_ref, right_ref, *refs
):
    ext_ref = refs[-1]
    extend(cur_ref, low_ref, high_ref, ext_ref)
    blocks = next_blocks(plan, plan_ref, cur_ref, tiles_ref, ext_ref)
    write_sends(
        blocks,
        left_ref,
        right_ref,
        lambda side, slot: plan_ref[(plan.left, plan.right)[side] + slot],
        lambda side: plan_ref[plan.sent + side],
    )
    for number, block in enumerate(blocks):
        next_ref[number] = block
    for b_ref in refs[:-1]:
        write_rows(blocks, b_ref)


def ready_kernel(cur_ref, tiles_ref, wc_ref, cur_out, tiles_out, wc_out):
    cur_out[...] = cur_ref[...]
    tiles_out[...] = tiles_ref[...]
    wc_out[...] = wc_ref[...]


def branch_logits(branch, rows, w_ref, wc_ref):
    hidden = jnp.maximum(matmul(rows, w_ref[branch]), 0.0).astype(BF16)
    hid = hidden.shape[1]
    return matmul(wc_ref[:, branch * hid : (branch + 1) * hid], hidden, ((1,), (1,)))


def forward_kernel(branch, cur_ref, w_ref, wc_ref, *refs):
    rows = cur_ref[...].reshape(-1, cur_ref.shape[2]).astype(BF16)
    part = branch_logits(branch, rows, w_ref, wc_ref)
    if len(refs) == 2:
        part = refs[0][...] + part
    refs[-1][...] = part


def places(order_ref):
    nodes = order_ref.shape[1]
    rows = lax.broadcasted_iota(jnp.int32, (nodes, nodes), 0)
    return (order_ref[...] == rows).astype(F32).astype(BF16)


def wanted_places(nodes, group, step, offset, count):
    share = nodes // group
    mine = lax.axis_index("shuf")
    first = mine * share
    source = lax.broadcasted_iota(jnp.int32, (count, nodes), 0) + offset
    target = lax.broadcasted_iota(jnp.int32, (count, nodes), 1)
    moved = source + ((mine ^ step) - mine) * share
    wanted = (target == moved) & (source >= first) & (source < first + share)
    return wanted.astype(F32).astype(BF16)


def label_kernel(order_ref, *refs):
    nodes = order_ref.shape[1]
    group = len(refs) - 1
    width = refs[0].shape[1]
    per_piece = nodes // width
    ordered = [jnp.zeros((1, nodes), F32) for _ in range(2)]
    for step in range(group):
        tail = refs[step][nodes:]
        for part in range(per_piece):
            moved = matmul(tail, wanted_places(nodes, group, step, part * width, width))
            for piece in range(2):
                row = piece * per_piece + part
                ordered[piece] = ordered[piece] + moved[row : row + 1]
    number = lax.broadcasted_iota(jnp.int32, (16, nodes), 0)
    packed = jnp.where(number == 0, ordered[0], jnp.where(number == 1, ordered[1], 0.0))
    pieces = matmul(packed.astype(BF16), places(order_ref), ((1,), (1,)))
    refs[-1][...] = (pieces[0:1] + 256.0 * pieces[1:2]).astype(jnp.int32)


def loss_kernel(*refs):
    group = len(refs) - 1
    height, nodes = refs[0].shape
    total = jnp.zeros((16, nodes), F32)
    for step in range(group):
        wanted = wanted_places(nodes, group, step, 0, nodes)
        total = total + matmul(refs[step][height - 16 :], wanted)
    refs[-1][...] = total[0:1] + total[1:2] + total[2:3]


def last_hop_kernel(plan, plan_ref, cur_ref, low_ref, high_ref, tiles_ref, out_ref, ext_ref):
    extend(cur_ref, low_ref, high_ref, ext_ref)
    blocks = next_blocks(plan, plan_ref, cur_ref, tiles_ref, ext_ref)
    for number, block in enumerate(blocks):
        size, width = block.shape
        columns = slice(number * width, (number + 1) * width)
        out_ref[:size, columns] = block.astype(BF16)
        out_ref[size:, columns] = cur_ref[number].astype(BF16)


def stacked(ref, place, width):
    size = ref.shape[0] // 2
    parts = ref.shape[1] // width
    return [
        ref[place * size : (place + 1) * size, part * width : (part + 1) * width]
        for part in range(parts)
    ]


def loss_and_gradient_kernel(
    row_scale, rows_ref, before_ref, w_ref, wc_ref, order_ref, label_ref, out_ref
):
    rows_b = jnp.concatenate(stacked(rows_ref, 0, w_ref.shape[1]), axis=0)
    logits = before_ref[...] + branch_logits(w_ref.shape[0] - 1, rows_b, w_ref, wc_ref)
    classes, rows = logits.shape
    kept = up_to(classes, 16)
    hit = lax.broadcasted_iota(jnp.int32, (classes, rows), 0) == label_ref[...]
    top = jnp.max(logits, axis=0, keepdims=True)
    log_total = top + jnp.log(jnp.sum(jnp.exp(logits - top), axis=0, keepdims=True))
    loss = log_total - jnp.sum(jnp.where(hit, logits, 0.0), axis=0, keepdims=True)
    dlogits = (jnp.exp(logits - log_total) - jnp.where(hit, 1.0, 0.0)) * row_scale
    out_ref[kept - 16 : kept] = jnp.zeros((16, rows), BF16)
    out_ref[:classes] = dlogits.astype(BF16)
    number = lax.broadcasted_iota(jnp.int32, (16, rows), 0)
    packed = jnp.zeros((16, rows), F32)
    rest = loss
    for piece in range(3):
        part = rest.astype(BF16).astype(F32)
        packed = jnp.where(number == piece, part, packed)
        rest = rest - part
    out_ref[kept:] = matmul(packed.astype(BF16), places(order_ref)).astype(BF16)


def weights_kernel(w_ref, wc_ref, wt_ref, wct_ref, pad_ref):
    branches, own, kept = wct_ref.shape
    classes = wc_ref.shape[0]
    hid = w_ref.shape[2]
    first = lax.axis_index("shuf") * own
    pad_ref[...] = jnp.zeros_like(pad_ref)
    for branch in range(branches):
        columns = w_ref[branch, :, pl.ds(pl.multiple_of(first, LANES), own)]
        wt_ref[branch] = columns.astype(F32).T.astype(BF16)
        columns = wc_ref[:, pl.ds(pl.multiple_of(branch * hid + first, LANES), own)]
        pad_ref[:classes] = columns.astype(F32)
        wct_ref[branch] = pad_ref[...].T[:, :kept].astype(BF16)


def add_chunks(kept, more, row_refs, last_refs, dlogit_refs, w_ref, wt_ref, wct_ref, chunks_ref):
    members = len(last_refs)
    branches, own, width = wt_ref.shape
    nodes = last_refs[0].shape[1]
    hid = w_ref.shape[2]
    all_rows = []
    for branch in range(branches - 2):
        ours = row_refs[branch * members : (branch + 1) * members]
        all_rows.append(jnp.concatenate([ref[:nodes] for ref in ours], axis=0))
    for place in (1, 0):
        ours = [rows for ref in last_refs for rows in stacked(ref, place, width)]
        all_rows.append(jnp.concatenate(ours, axis=0))
    dlogits_t = jnp.concatenate([ref[:kept] for ref in dlogit_refs], axis=1)
    own_class = branches * own
    first = lax.axis_index("shuf") * own_class
    which = first // hid
    columns = pl.ds(pl.multiple_of(first - which * hid, LANES), own_class)
    chosen = all_rows[0]
    for branch in range(1, branches):
        chosen = jnp.where(which == branch, all_rows[branch], chosen)

    def put(chunk, rows, value):
        chunks_ref[chunk, rows] = chunks_ref[chunk, rows] + value if more else value

    hidden = jnp.maximum(matmul(chosen, w_ref[which, :, columns]), 0.0).astype(BF16)
    class_t = matmul(dlogits_t, hidden)
    for chunk in range(chunks_ref.shape[0]):
        put(chunk, slice(0, kept), class_t[:, chunk * LANES : (chunk + 1) * LANES])
    per_branch = chunks_ref.shape[0] // branches
    for branch, rows in enumerate(all_rows):
        live = matmul(wt_ref[branch], rows, ((1,), (1,))) > 0.0
        dhidden_t = jnp.where(live, matmul(wct_ref[branch], dlogits_t), 0.0).astype(BF16)
        branch_t = matmul(dhidden_t, rows)
        for part in range(per_branch):
            put(
                branch * per_branch + part,
                slice(kept, kept + width),
                branch_t[part * LANES : (part + 1) * LANES],
            )


def split_refs(members, refs):
    last = len(refs) - 3 - 2 * members
    return (
        refs[:last], refs[last : last + members], refs[last + members : last + 2 * members],
        *refs[last + 2 * members :],
    )


def early_kernel(kept, members, *refs):
    add_chunks(kept, False, *split_refs(members, refs[:-1]), refs[-1])


def late_chunks(kept, members, early_ref, refs, chunks_ref):
    chunks_ref[...] = early_ref[...]
    add_chunks(kept, True, *split_refs(members, refs), chunks_ref)


def late_kernel(kept, members, half, early_ref, *refs):
    ins = len(refs) - 2 - half
    outs = refs[ins:-1]
    chunks_ref = refs[-1]
    late_chunks(kept, members, early_ref, refs[:ins], chunks_ref)
    dom = lax.axis_index("dom")
    for step in range(half):
        stays = dom ^ (2 * step)
        outs[step][...] = chunks_ref[stays]
        outs[half][step] = chunks_ref[stays ^ 1].astype(BF16)


def plain_late_kernel(kept, members, early_ref, *refs):
    late_chunks(kept, members, early_ref, refs[:-1], refs[-1])


def write_chunk(kept, chunk, value, branch_ref, class_ref):
    per_branch = branch_ref.shape[2] // LANES
    start = pl.multiple_of(chunk * LANES, LANES)
    class_ref[:, pl.ds(start, LANES)] = value[: class_ref.shape[0]]
    branch = chunk // per_branch
    start = pl.multiple_of((chunk - branch * per_branch) * LANES, LANES)
    branch_ref[branch, :, pl.ds(start, LANES)] = value[kept:].T


def out_kernel(kept, *refs):
    ins, branch_ref, class_ref = refs[:-2], refs[-2], refs[-1]
    dom = lax.axis_index("dom")
    half = len(ins) // 2
    for step in range(half):
        for side in range(2):
            value = ins[side * half + step][...].astype(F32)
            write_chunk(kept, dom ^ (2 * step + side), value, branch_ref, class_ref)


def plain_out_kernel(kept, in_ref, branch_ref, class_ref):
    for chunk in range(in_ref.shape[0]):
        write_chunk(kept, chunk, in_ref[chunk], branch_ref, class_ref)


def in_group(value, distance=None):
    members = [value]
    steps = [0]
    distance = lax.axis_size("shuf") // 2 if distance is None else distance
    while distance:
        members += [swapped(member, distance, "shuf") for member in members]
        steps += [step + distance for step in steps]
        distance //= 2
    return [members[steps.index(step)] for step in range(len(steps))]


def body(
    features, tile_values, tile_dst, tile_src, tile_count, send_left, send_right,
    send_count, batch_order, labels, w_branch, w_class,
):
    block = tile_values.shape[1]
    nodes, width = features.shape
    local = nodes // block
    slots = send_left.shape[0]
    tiles = tile_values.shape[0]
    branches, _, hid = w_branch.shape
    cat, classes = w_class.shape
    dom = lax.axis_size("dom")
    shuf = lax.axis_size("shuf")
    mine = lax.axis_index("shuf")
    share = nodes // shuf
    own = hid // shuf
    own_class = cat // shuf
    kept = up_to(classes, 16)
    row_scale = 1.0 / math.sqrt(float(nodes * dom * shuf))
    plan = Plan(tiles, slots)
    small = jnp.concatenate(
        [tile_dst, tile_src, tile_count, send_left, send_right, send_count.reshape(-1)]
    )
    blocks_f32 = jax.ShapeDtypeStruct((local, block, width), F32)
    slots_f32 = jax.ShapeDtypeStruct((slots, block, width), F32)
    rows_b16 = jax.ShapeDtypeStruct((nodes, width), BF16)
    first_b16 = jax.ShapeDtypeStruct((nodes + 16, width), BF16)
    logits_f32 = jax.ShapeDtypeStruct((classes, nodes), F32)
    w_class_t = w_class.T

    current = features.reshape(local, block, width)
    gathered = []
    logits = None
    hop_flops = 12 * tiles * block * block * width
    forward_flops = 2 * nodes * hid * (width + classes)
    ext = pltpu.VMEM((local + 2 * slots, block, width), F32)
    to_left, to_right, current, *rows = call(
        first_kernel,
        [slots_f32, slots_f32, blocks_f32, first_b16],
        [ANYWHERE] * 5,
        1000,
        [
            pltpu.SMEM((slots,), jnp.int32),
            pltpu.SMEM((slots,), jnp.int32),
            pltpu.SMEM((1, 2), jnp.int32),
            pltpu.VMEM((1, nodes), jnp.int32),
            pltpu.SemaphoreType.DMA((5,)),
        ],
        limit=VMEM_ALL,
    )(send_left, send_right, send_count, current, labels.reshape(1, nodes))
    current, tile_values, w_class_t = call(
        ready_kernel,
        [
            blocks_f32,
            jax.ShapeDtypeStruct(tile_values.shape, F32),
            jax.ShapeDtypeStruct(w_class_t.shape, BF16),
        ],
        [IN_VMEM] * 3,
        1000,
    )(current, tile_values, w_class_t)
    for hop in range(HOPS):
        from_lower = passed_along(to_right, "dom", 1)
        from_upper = passed_along(to_left, "dom", -1)
        for value in rows:
            gathered.append(in_group(value))
        before = [] if logits is None else [logits]
        logits = call(
            functools.partial(forward_kernel, hop),
            logits_f32,
            [IN_VMEM] * (3 + len(before)),
            forward_flops,
            after=[members[shuf // 2] for members in gathered] if hop == HOPS - 1 else [],
        )(current, w_branch, w_class_t, *before)
        if hop == 0:
            first_logits = logits
            after = []
        else:
            after = [first_logits]
        if hop < HOPS - 1:
            current, to_left, to_right, *rows = call(
                functools.partial(hop_kernel, plan),
                [blocks_f32, slots_f32, slots_f32] + [rows_b16] * (hop < HOPS - 2),
                [IN_SMEM] + [IN_VMEM] * 4,
                hop_flops,
                [ext],
                after,
            )(small, current, from_lower, from_upper, tile_values)

    label_mine = call(
        label_kernel,
        jax.ShapeDtypeStruct((1, nodes), jnp.int32),
        [IN_VMEM] * (1 + shuf),
        1000,
    )(batch_order, *gathered[0])

    wt_own, wct_own = call(
        weights_kernel,
        [
            jax.ShapeDtypeStruct((branches, own, width), BF16),
            jax.ShapeDtypeStruct((branches, own, kept), BF16),
        ],
        [IN_VMEM] * 2,
        1000,
        [pltpu.VMEM((up_to(classes, LANES), own), F32)],
    )(w_branch, w_class_t)

    last_rows = call(
        functools.partial(last_hop_kernel, plan),
        jax.ShapeDtypeStruct((2 * block, local * width), BF16),
        [IN_SMEM] + [IN_VMEM] * 4,
        hop_flops,
        [ext],
        [logits, label_mine, *gathered[1][1:]],
    )(small, current, from_lower, from_upper, tile_values)
    dlogits = call(
        functools.partial(loss_and_gradient_kernel, row_scale),
        jax.ShapeDtypeStruct((kept + 16, nodes), BF16),
        [IN_VMEM] * 6,
        1000,
    )(last_rows, logits, w_branch, w_class_t, batch_order, label_mine)
    chunks = own_class // LANES
    height = kept + width
    ahead = shuf // 2
    chunks_f32 = jax.ShapeDtypeStruct((chunks, height, LANES), F32)
    grad_flops = shuf * nodes * own_class * (3 * width + 2 * kept)
    weights = (w_branch, wt_own, wct_own)
    across_rows = swapped(last_rows, ahead, "shuf")
    across = swapped(dlogits, ahead, "shuf")
    close_rows = in_group(last_rows, ahead // 2)
    close = in_group(dlogits, ahead // 2)
    early = call(
        functools.partial(early_kernel, kept, ahead),
        chunks_f32,
        [IN_VMEM] * (4 * ahead + 3),
        1000,
    )(
        *[member for members in gathered for member in members[:ahead]],
        *close_rows, *close, *weights,
    )
    across, across_rows, early = lax.optimization_barrier((across, across_rows, early))
    distant_rows = in_group(across_rows, ahead // 2)
    distant = in_group(across, ahead // 2)
    late_ins = (
        early, *[member for members in gathered for member in members[ahead:]],
        *distant_rows, *distant, *weights,
    )
    last_all = close + distant
    loss_rows = call(
        loss_kernel, jax.ShapeDtypeStruct((1, nodes), F32), [IN_VMEM] * shuf, 1000
    )(*last_all).reshape(nodes)

    outs = [
        jax.ShapeDtypeStruct((branches, width, own), F32),
        jax.ShapeDtypeStruct((classes, own_class), F32),
    ]
    if chunks == dom and dom % 2 == 0 and dom & (dom - 1) == 0:
        half = dom // 2
        one_f32 = jax.ShapeDtypeStruct((height, LANES), F32)
        made = call(
            functools.partial(late_kernel, kept, ahead, half),
            [one_f32] * half + [jax.ShapeDtypeStruct((half, height, LANES), BF16)],
            [IN_VMEM] * len(late_ins),
            grad_flops,
            [pltpu.VMEM(chunks_f32.shape, F32)],
        )(*late_ins)
        order = list(range(half - 1, -1, -1))
        arrived = swapped(made[half], 1)
        total = {step: made[step] + arrived[step].astype(F32) for step in order}
        far = [swapped(total[step].astype(BF16), 2 * step) for step in order[:-1]]
        summed = total[0]
        for value in far:
            summed = summed + value.astype(F32)
        near = {0: summed.astype(BF16)}
        other = {0: swapped(near[0], 1)}
        for step in order[:-1]:
            near[step] = swapped(near[0], 2 * step)
        for step in range(1, half):
            other[step] = swapped(near[step], 1)
        near = [near[step] for step in range(half)]
        other = [other[step] for step in range(half)]
        grad_branch, grad_class_t = call(
            functools.partial(out_kernel, kept), outs, [IN_VMEM] * dom, 1000
        )(*near, *other)
    else:
        grads = call(
            functools.partial(plain_late_kernel, kept, ahead),
            chunks_f32,
            [IN_VMEM] * len(late_ins),
            grad_flops,
        )(*late_ins)
        grad_branch, grad_class_t = call(
            functools.partial(plain_out_kernel, kept), outs, [IN_VMEM], 1000
        )(lax.psum(grads, "dom"))
    return (loss_rows, grad_branch, grad_class_t.T)


def solution(mesh):
    return jax.shard_map(
        body,
        mesh=mesh,
        in_specs=(
            P(("dom", "shuf"), None),
            P(("dom", "shuf"), None, None),
            P(("dom", "shuf")),
            P(("dom", "shuf")),
            P(("dom", "shuf")),
            P(("dom", "shuf")),
            P(("dom", "shuf")),
            P(("dom", "shuf"), None),
            P(("dom", "shuf"), None),
            P(("dom", "shuf")),
            P(),
            P(),
        ),
        out_specs=(P(("dom", "shuf")), P(None, None, "shuf"), P("shuf", None)),
        check_vma=False,
    )
```

```python
import functools
import math

import jax
import jax.numpy as jnp
from jax import lax
from jax.experimental import pallas as pl
from jax.experimental.pallas import tpu as pltpu
from jax.sharding import PartitionSpec as P

HOPS = 3
LANES = 128
VMEM_LIMIT = 24 * 1024 * 1024
VMEM_ALL = 56 * 1024 * 1024

IN_VMEM = pl.BlockSpec(memory_space=pltpu.VMEM)
IN_SMEM = pl.BlockSpec(memory_space=pltpu.SMEM)
ANYWHERE = pl.BlockSpec(memory_space=pl.ANY)
BF16 = jnp.bfloat16
F32 = jnp.float32


def up_to(value, multiple):
    return -(-value // multiple) * multiple


def passed_along(value, axis, steps):
    count = lax.axis_size(axis)
    pairs = [(source, (source + steps) % count) for source in range(count)]
    return lax.ppermute(value, axis, pairs)


def swapped(value, distance, axis="dom"):
    pairs = [(source, source ^ distance) for source in range(lax.axis_size(axis))]
    return lax.ppermute(value, axis, pairs)


def matmul(left, right, dims=((1,), (0,)), precision=None):
    return lax.dot_general(
        left, right, (dims, ((), ())), precision=precision, preferred_element_type=F32
    )


def call(kernel, out_shape, in_specs, flops, scratch=(), after=(), limit=VMEM_LIMIT):
    many = isinstance(out_shape, (list, tuple))
    outs = out_shape if many else [out_shape]
    moved = sum(math.prod(one.shape) * one.dtype.itemsize for one in outs)
    waited = len(after)

    def run(*refs):
        kernel(*refs[waited:])

    made = pl.pallas_call(
        run,
        out_shape=out_shape,
        in_specs=[ANYWHERE] * waited + in_specs,
        out_specs=[IN_VMEM] * len(outs) if many else IN_VMEM,
        scratch_shapes=list(scratch),
        compiler_params=pltpu.CompilerParams(vmem_limit_bytes=limit),
        cost_estimate=pl.CostEstimate(
            flops=flops, bytes_accessed=3 * moved if flops > 1000 else 1000, transcendentals=0
        ),
    )
    return functools.partial(made, *after)


class Plan:
    def __init__(self, tiles, slots):
        self.tiles = tiles
        self.slots = slots
        self.dst = 0
        self.src = tiles
        self.count = 2 * tiles
        self.left = 2 * tiles + 1
        self.right = self.left + slots
        self.sent = self.right + slots


def write_sends(blocks, left_ref, right_ref, ids, counts):
    for slot in range(left_ref.shape[0]):
        for side, out_ref in enumerate((left_ref, right_ref)):
            index = ids(side, slot)
            picked = blocks[0]
            for number in range(1, len(blocks)):
                picked = jnp.where(index == number, blocks[number], picked)
            out_ref[slot] = jnp.where(slot < counts(side), picked, 0.0)


def copied(sources, targets, sems):
    copies = [
        pltpu.make_async_copy(source, target, sems.at[number])
        for number, (source, target) in enumerate(zip(sources, targets))
    ]
    for copy in copies:
        copy.start()
    for copy in copies:
        copy.wait()


def first_kernel(
    sl_ref, sr_ref, sc_ref, feat_ref, label_from,
    left_ref, right_ref, held_ref, b_ref,
    sl_here, sr_here, sc_here, label_ref, sems,
):
    copied(
        (sl_ref, sr_ref, sc_ref, feat_ref, label_from),
        (sl_here, sr_here, sc_here, held_ref, label_ref),
        sems,
    )
    blocks = [held_ref[number] for number in range(held_ref.shape[0])]
    write_sends(
        blocks,
        left_ref,
        right_ref,
        lambda side, slot: (sl_here, sr_here)[side][slot],
        lambda side: sc_here[0, side],
    )
    write_rows(blocks, b_ref)
    nodes = label_ref.shape[1]
    width = b_ref.shape[1]
    per_piece = nodes // width
    place = lax.broadcasted_iota(jnp.int32, (16, width), 0)
    packed = jnp.zeros((16, width), F32)
    for piece in range(2):
        value = label_ref[...] & 255 if piece == 0 else label_ref[...] >> 8
        value = value.astype(F32)
        for part in range(per_piece):
            packed = jnp.where(
                place == piece * per_piece + part,
                value[:, part * width : (part + 1) * width],
                packed,
            )
    b_ref[nodes:] = packed.astype(BF16)


def write_rows(blocks, b_ref):
    for number, block in enumerate(blocks):
        size = block.shape[0]
        b_ref[number * size : (number + 1) * size] = block.astype(BF16)


def next_blocks(plan, plan_ref, cur_ref, tiles_ref, ext_ref):
    local = cur_ref.shape[0]
    ext_ref[:local] = cur_ref[...]
    totals = [jnp.zeros(cur_ref.shape[1:], F32) for _ in range(local)]
    live = plan_ref[plan.count]
    for tile in range(plan.tiles):
        product = matmul(
            tiles_ref[tile],
            ext_ref[plan_ref[plan.src + tile]],
            precision=lax.Precision.HIGHEST,
        )
        wanted = jnp.where(tile < live, plan_ref[plan.dst + tile], -1)
        for number in range(local):
            totals[number] = totals[number] + jnp.where(wanted == number, product, 0.0)
    return totals


def extend(cur_ref, low_ref, high_ref, ext_ref):
    local = cur_ref.shape[0]
    slots = low_ref.shape[0]
    ext_ref[local : local + slots] = low_ref[...]
    ext_ref[local + slots :] = high_ref[...]


def hop_kernel(
    plan, plan_ref, cur_ref, low_ref, high_ref, tiles_ref, next_ref, left_ref, right_ref, *refs
):
    ext_ref = refs[-1]
    extend(cur_ref, low_ref, high_ref, ext_ref)
    blocks = next_blocks(plan, plan_ref, cur_ref, tiles_ref, ext_ref)
    write_sends(
        blocks,
        left_ref,
        right_ref,
        lambda side, slot: plan_ref[(plan.left, plan.right)[side] + slot],
        lambda side: plan_ref[plan.sent + side],
    )
    for number, block in enumerate(blocks):
        next_ref[number] = block
    for b_ref in refs[:-1]:
        write_rows(blocks, b_ref)


def ready_kernel(cur_ref, tiles_ref, wc_ref, cur_out, tiles_out, wc_out):
    cur_out[...] = cur_ref[...]
    tiles_out[...] = tiles_ref[...]
    wc_out[...] = wc_ref[...]


def branch_logits(branch, rows, w_ref, wc_ref):
    hidden = jnp.maximum(matmul(rows, w_ref[branch]), 0.0).astype(BF16)
    hid = hidden.shape[1]
    return matmul(wc_ref[:, branch * hid : (branch + 1) * hid], hidden, ((1,), (1,)))


def forward_kernel(branch, cur_ref, w_ref, wc_ref, *refs):
    rows = cur_ref[...].reshape(-1, cur_ref.shape[2]).astype(BF16)
    part = branch_logits(branch, rows, w_ref, wc_ref)
    if len(refs) == 2:
        part = refs[0][...] + part
    refs[-1][...] = part


def places(order_ref):
    nodes = order_ref.shape[1]
    rows = lax.broadcasted_iota(jnp.int32, (nodes, nodes), 0)
    return (order_ref[...] == rows).astype(F32).astype(BF16)


def wanted_places(nodes, group, step, offset, count):
    share = nodes // group
    mine = lax.axis_index("shuf")
    first = mine * share
    source = lax.broadcasted_iota(jnp.int32, (count, nodes), 0) + offset
    target = lax.broadcasted_iota(jnp.int32, (count, nodes), 1)
    moved = source + ((mine ^ step) - mine) * share
    wanted = (target == moved) & (source >= first) & (source < first + share)
    return wanted.astype(F32).astype(BF16)


def label_kernel(order_ref, *refs):
    nodes = order_ref.shape[1]
    group = len(refs) - 1
    width = refs[0].shape[1]
    per_piece = nodes // width
    ordered = [jnp.zeros((1, nodes), F32) for _ in range(2)]
    for step in range(group):
        tail = refs[step][nodes:]
        for part in range(per_piece):
            moved = matmul(tail, wanted_places(nodes, group, step, part * width, width))
            for piece in range(2):
                row = piece * per_piece + part
                ordered[piece] = ordered[piece] + moved[row : row + 1]
    number = lax.broadcasted_iota(jnp.int32, (16, nodes), 0)
    packed = jnp.where(number == 0, ordered[0], jnp.where(number == 1, ordered[1], 0.0))
    pieces = matmul(packed.astype(BF16), places(order_ref), ((1,), (1,)))
    refs[-1][...] = (pieces[0:1] + 256.0 * pieces[1:2]).astype(jnp.int32)


def loss_kernel(*refs):
    group = len(refs) - 1
    height, nodes = refs[0].shape
    total = jnp.zeros((16, nodes), F32)
    for step in range(group):
        wanted = wanted_places(nodes, group, step, 0, nodes)
        total = total + matmul(refs[step][height - 16 :], wanted)
    refs[-1][...] = total[0:1] + total[1:2] + total[2:3]


def last_hop_kernel(plan, plan_ref, cur_ref, low_ref, high_ref, tiles_ref, out_ref, ext_ref):
    extend(cur_ref, low_ref, high_ref, ext_ref)
    blocks = next_blocks(plan, plan_ref, cur_ref, tiles_ref, ext_ref)
    for number, block in enumerate(blocks):
        size, width = block.shape
        columns = slice(number * width, (number + 1) * width)
        out_ref[:size, columns] = block.astype(BF16)
        out_ref[size:, columns] = cur_ref[number].astype(BF16)


def stacked(ref, place, width):
    size = ref.shape[0] // 2
    parts = ref.shape[1] // width
    return [
        ref[place * size : (place + 1) * size, part * width : (part + 1) * width]
        for part in range(parts)
    ]


def loss_and_gradient_kernel(
    row_scale, rows_ref, before_ref, w_ref, wc_ref, order_ref, label_ref, out_ref
):
    rows_b = jnp.concatenate(stacked(rows_ref, 0, w_ref.shape[1]), axis=0)
    logits = before_ref[...] + branch_logits(w_ref.shape[0] - 1, rows_b, w_ref, wc_ref)
    classes, rows = logits.shape
    kept = up_to(classes, 16)
    hit = lax.broadcasted_iota(jnp.int32, (classes, rows), 0) == label_ref[...]
    top = jnp.max(logits, axis=0, keepdims=True)
    log_total = top + jnp.log(jnp.sum(jnp.exp(logits - top), axis=0, keepdims=True))
    loss = log_total - jnp.sum(jnp.where(hit, logits, 0.0), axis=0, keepdims=True)
    dlogits = (jnp.exp(logits - log_total) - jnp.where(hit, 1.0, 0.0)) * row_scale
    out_ref[kept - 16 : kept] = jnp.zeros((16, rows), BF16)
    out_ref[:classes] = dlogits.astype(BF16)
    number = lax.broadcasted_iota(jnp.int32, (16, rows), 0)
    packed = jnp.zeros((16, rows), F32)
    rest = loss
    for piece in range(3):
        part = rest.astype(BF16).astype(F32)
        packed = jnp.where(number == piece, part, packed)
        rest = rest - part
    out_ref[kept:] = matmul(packed.astype(BF16), places(order_ref)).astype(BF16)


def weights_kernel(w_ref, wc_ref, wt_ref, wct_ref, pad_ref):
    branches, own, kept = wct_ref.shape
    classes = wc_ref.shape[0]
    hid = w_ref.shape[2]
    first = lax.axis_index("shuf") * own
    pad_ref[...] = jnp.zeros_like(pad_ref)
    for branch in range(branches):
        columns = w_ref[branch, :, pl.ds(pl.multiple_of(first, LANES), own)]
        wt_ref[branch] = columns.astype(F32).T.astype(BF16)
        columns = wc_ref[:, pl.ds(pl.multiple_of(branch * hid + first, LANES), own)]
        pad_ref[:classes] = columns.astype(F32)
        wct_ref[branch] = pad_ref[...].T[:, :kept].astype(BF16)


def add_chunks(kept, more, row_refs, last_refs, dlogit_refs, w_ref, wt_ref, wct_ref, chunks_ref):
    members = len(last_refs)
    branches, own, width = wt_ref.shape
    nodes = last_refs[0].shape[1]
    hid = w_ref.shape[2]
    all_rows = []
    for branch in range(branches - 2):
        ours = row_refs[branch * members : (branch + 1) * members]
        all_rows.append(jnp.concatenate([ref[:nodes] for ref in ours], axis=0))
    for place in (1, 0):
        ours = [rows for ref in last_refs for rows in stacked(ref, place, width)]
        all_rows.append(jnp.concatenate(ours, axis=0))
    dlogits_t = jnp.concatenate([ref[:kept] for ref in dlogit_refs], axis=1)
    own_class = branches * own
    first = lax.axis_index("shuf") * own_class
    which = first // hid
    columns = pl.ds(pl.multiple_of(first - which * hid, LANES), own_class)
    chosen = all_rows[0]
    for branch in range(1, branches):
        chosen = jnp.where(which == branch, all_rows[branch], chosen)

    def put(chunk, rows, value):
        chunks_ref[chunk, rows] = chunks_ref[chunk, rows] + value if more else value

    hidden = jnp.maximum(matmul(chosen, w_ref[which, :, columns]), 0.0).astype(BF16)
    class_t = matmul(dlogits_t, hidden)
    for chunk in range(chunks_ref.shape[0]):
        put(chunk, slice(0, kept), class_t[:, chunk * LANES : (chunk + 1) * LANES])
    per_branch = chunks_ref.shape[0] // branches
    for branch, rows in enumerate(all_rows):
        live = matmul(wt_ref[branch], rows, ((1,), (1,))) > 0.0
        dhidden_t = jnp.where(live, matmul(wct_ref[branch], dlogits_t), 0.0).astype(BF16)
        branch_t = matmul(dhidden_t, rows)
        for part in range(per_branch):
            put(
                branch * per_branch + part,
                slice(kept, kept + width),
                branch_t[part * LANES : (part + 1) * LANES],
            )


def split_refs(members, refs):
    last = len(refs) - 3 - 2 * members
    return (
        refs[:last], refs[last : last + members], refs[last + members : last + 2 * members],
        *refs[last + 2 * members :],
    )


def early_kernel(kept, members, *refs):
    add_chunks(kept, False, *split_refs(members, refs[:-1]), refs[-1])


def late_chunks(kept, members, early_ref, refs, chunks_ref):
    chunks_ref[...] = early_ref[...]
    add_chunks(kept, True, *split_refs(members, refs), chunks_ref)


def late_kernel(kept, members, half, early_ref, *refs):
    ins = len(refs) - 1 - 2 * half
    outs = refs[ins:-1]
    chunks_ref = refs[-1]
    late_chunks(kept, members, early_ref, refs[:ins], chunks_ref)
    dom = lax.axis_index("dom")
    for step in range(half):
        stays = dom ^ (2 * step)
        outs[step][...] = chunks_ref[stays]
        outs[half + step][...] = chunks_ref[stays ^ 1].astype(BF16)


def plain_late_kernel(kept, members, early_ref, *refs):
    late_chunks(kept, members, early_ref, refs[:-1], refs[-1])


def write_chunk(kept, chunk, value, branch_ref, class_ref):
    per_branch = branch_ref.shape[2] // LANES
    start = pl.multiple_of(chunk * LANES, LANES)
    class_ref[:, pl.ds(start, LANES)] = value[: class_ref.shape[0]]
    branch = chunk // per_branch
    start = pl.multiple_of((chunk - branch * per_branch) * LANES, LANES)
    branch_ref[branch, :, pl.ds(start, LANES)] = value[kept:].T


def out_kernel(kept, distances, *refs):
    count = len(distances)
    ins = refs[-5 - count : -5]
    branch_ref, class_ref, branch_here, class_here, sems = refs[-5:]
    dom = lax.axis_index("dom")
    per_branch = branch_ref.shape[2] // LANES
    copies = []
    for number, distance in enumerate(distances):
        chunk = dom ^ distance
        value = ins[number][...].astype(F32)
        class_here[number] = value[: class_ref.shape[0]]
        start = pl.multiple_of(chunk * LANES, LANES)
        copies.append(
            pltpu.make_async_copy(
                class_here.at[number], class_ref.at[:, pl.ds(start, LANES)], sems.at[2 * number]
            )
        )
        copies[-1].start()
        branch_here[number] = value[kept:].T
        branch = chunk // per_branch
        start = pl.multiple_of((chunk - branch * per_branch) * LANES, LANES)
        copies.append(
            pltpu.make_async_copy(
                branch_here.at[number],
                branch_ref.at[branch, :, pl.ds(start, LANES)],
                sems.at[2 * number + 1],
            )
        )
        copies[-1].start()
    for copy in copies:
        copy.wait()


def write_out(kept, distances, values, outs, before):
    count = len(distances)
    return pl.pallas_call(
        functools.partial(out_kernel, kept, distances),
        out_shape=outs,
        in_specs=[ANYWHERE] * len(before) + [IN_VMEM] * count,
        out_specs=[pl.BlockSpec(memory_space=pltpu.HBM)] * 2,
        scratch_shapes=[
            pltpu.VMEM((count, outs[0].shape[1], LANES), F32),
            pltpu.VMEM((count, outs[1].shape[0], LANES), F32),
            pltpu.SemaphoreType.DMA((2 * count,)),
        ],
        input_output_aliases={0: 0, 1: 1} if before else {},
        compiler_params=pltpu.CompilerParams(vmem_limit_bytes=VMEM_LIMIT),
        cost_estimate=pl.CostEstimate(flops=1000, bytes_accessed=1000, transcendentals=0),
    )(*before, *values)


def plain_out_kernel(kept, in_ref, branch_ref, class_ref):
    for chunk in range(in_ref.shape[0]):
        write_chunk(kept, chunk, in_ref[chunk], branch_ref, class_ref)


def in_group(value, distance=None):
    members = [value]
    steps = [0]
    distance = lax.axis_size("shuf") // 2 if distance is None else distance
    while distance:
        members += [swapped(member, distance, "shuf") for member in members]
        steps += [step + distance for step in steps]
        distance //= 2
    return [members[steps.index(step)] for step in range(len(steps))]


def body(
    features, tile_values, tile_dst, tile_src, tile_count, send_left, send_right,
    send_count, batch_order, labels, w_branch, w_class,
):
    block = tile_values.shape[1]
    nodes, width = features.shape
    local = nodes // block
    slots = send_left.shape[0]
    tiles = tile_values.shape[0]
    branches, _, hid = w_branch.shape
    cat, classes = w_class.shape
    dom = lax.axis_size("dom")
    shuf = lax.axis_size("shuf")
    mine = lax.axis_index("shuf")
    share = nodes // shuf
    own = hid // shuf
    own_class = cat // shuf
    kept = up_to(classes, 16)
    row_scale = 1.0 / math.sqrt(float(nodes * dom * shuf))
    plan = Plan(tiles, slots)
    small = jnp.concatenate(
        [tile_dst, tile_src, tile_count, send_left, send_right, send_count.reshape(-1)]
    )
    blocks_f32 = jax.ShapeDtypeStruct((local, block, width), F32)
    slots_f32 = jax.ShapeDtypeStruct((slots, block, width), F32)
    rows_b16 = jax.ShapeDtypeStruct((nodes, width), BF16)
    first_b16 = jax.ShapeDtypeStruct((nodes + 16, width), BF16)
    logits_f32 = jax.ShapeDtypeStruct((classes, nodes), F32)
    w_class_t = w_class.T

    current = features.reshape(local, block, width)
    gathered = []
    logits = None
    hop_flops = 12 * tiles * block * block * width
    forward_flops = 2 * nodes * hid * (width + classes)
    ext = pltpu.VMEM((local + 2 * slots, block, width), F32)
    to_left, to_right, current, *rows = call(
        first_kernel,
        [slots_f32, slots_f32, blocks_f32, first_b16],
        [ANYWHERE] * 5,
        1000,
        [
            pltpu.SMEM((slots,), jnp.int32),
            pltpu.SMEM((slots,), jnp.int32),
            pltpu.SMEM((1, 2), jnp.int32),
            pltpu.VMEM((1, nodes), jnp.int32),
            pltpu.SemaphoreType.DMA((5,)),
        ],
        limit=VMEM_ALL,
    )(send_left, send_right, send_count, current, labels.reshape(1, nodes))
    current, tile_values, w_class_t = call(
        ready_kernel,
        [
            blocks_f32,
            jax.ShapeDtypeStruct(tile_values.shape, F32),
            jax.ShapeDtypeStruct(w_class_t.shape, BF16),
        ],
        [IN_VMEM] * 3,
        1000,
    )(current, tile_values, w_class_t)
    for hop in range(HOPS):
        from_lower = passed_along(to_right, "dom", 1)
        from_upper = passed_along(to_left, "dom", -1)
        for value in rows:
            gathered.append(in_group(value))
        before = [] if logits is None else [logits]
        logits = call(
            functools.partial(forward_kernel, hop),
            logits_f32,
            [IN_VMEM] * (3 + len(before)),
            forward_flops,
            after=[members[shuf // 2] for members in gathered] if hop == HOPS - 1 else [],
        )(current, w_branch, w_class_t, *before)
        if hop == 0:
            first_logits = logits
            after = []
        else:
            after = [first_logits]
        if hop < HOPS - 1:
            current, to_left, to_right, *rows = call(
                functools.partial(hop_kernel, plan),
                [blocks_f32, slots_f32, slots_f32] + [rows_b16] * (hop < HOPS - 2),
                [IN_SMEM] + [IN_VMEM] * 4,
                hop_flops,
                [ext],
                after,
            )(small, current, from_lower, from_upper, tile_values)

    label_mine = call(
        label_kernel,
        jax.ShapeDtypeStruct((1, nodes), jnp.int32),
        [IN_VMEM] * (1 + shuf),
        1000,
    )(batch_order, *gathered[0])

    wt_own, wct_own = call(
        weights_kernel,
        [
            jax.ShapeDtypeStruct((branches, own, width), BF16),
            jax.ShapeDtypeStruct((branches, own, kept), BF16),
        ],
        [IN_VMEM] * 2,
        1000,
        [pltpu.VMEM((up_to(classes, LANES), own), F32)],
    )(w_branch, w_class_t)

    last_rows = call(
        functools.partial(last_hop_kernel, plan),
        jax.ShapeDtypeStruct((2 * block, local * width), BF16),
        [IN_SMEM] + [IN_VMEM] * 4,
        hop_flops,
        [ext],
        [logits, label_mine, *gathered[1][1:]],
    )(small, current, from_lower, from_upper, tile_values)
    dlogits = call(
        functools.partial(loss_and_gradient_kernel, row_scale),
        jax.ShapeDtypeStruct((kept + 16, nodes), BF16),
        [IN_VMEM] * 6,
        1000,
    )(last_rows, logits, w_branch, w_class_t, batch_order, label_mine)
    chunks = own_class // LANES
    height = kept + width
    ahead = shuf // 2
    chunks_f32 = jax.ShapeDtypeStruct((chunks, height, LANES), F32)
    grad_flops = shuf * nodes * own_class * (3 * width + 2 * kept)
    weights = (w_branch, wt_own, wct_own)
    across_rows = swapped(last_rows, ahead, "shuf")
    across = swapped(dlogits, ahead, "shuf")
    close_rows = in_group(last_rows, ahead // 2)
    close = in_group(dlogits, ahead // 2)
    early = call(
        functools.partial(early_kernel, kept, ahead),
        chunks_f32,
        [IN_VMEM] * (4 * ahead + 3),
        1000,
    )(
        *[member for members in gathered for member in members[:ahead]],
        *close_rows, *close, *weights,
    )
    across, across_rows, early = lax.optimization_barrier((across, across_rows, early))
    distant_rows = in_group(across_rows, ahead // 2)
    distant = in_group(across, ahead // 2)
    late_ins = (
        early, *[member for members in gathered for member in members[ahead:]],
        *distant_rows, *distant, *weights,
    )
    last_all = close + distant
    loss_rows = call(
        loss_kernel, jax.ShapeDtypeStruct((1, nodes), F32), [IN_VMEM] * shuf, 1000
    )(*last_all).reshape(nodes)

    outs = [
        jax.ShapeDtypeStruct((branches, width, own), F32),
        jax.ShapeDtypeStruct((classes, own_class), F32),
    ]
    if chunks == dom and dom % 2 == 0 and dom & (dom - 1) == 0:
        half = dom // 2
        one_f32 = jax.ShapeDtypeStruct((height, LANES), F32)
        made = call(
            functools.partial(late_kernel, kept, ahead, half),
            [one_f32] * half + [jax.ShapeDtypeStruct((height, LANES), BF16)] * half,
            [IN_VMEM] * len(late_ins),
            grad_flops,
            [pltpu.VMEM(chunks_f32.shape, F32)],
        )(*late_ins)
        order = list(range(half - 1, -1, -1))
        arrived = {step: swapped(made[half + step], 1) for step in order}
        total = {step: made[step] + arrived[step].astype(F32) for step in order}
        far = {step: swapped(total[step].astype(BF16), 2 * step) for step in order[:-1]}
        summed = total[0]
        for step in order[:-1]:
            summed = lax.optimization_barrier(summed + far[step].astype(F32))
        near = [summed.astype(BF16)]
        near += [swapped(near[0], 2 * step) for step in range(1, half)]
        other = [swapped(value, 1) for value in near]
        results = []
        for first in range(0, half, 2):
            results = write_out(
                kept, [2 * first, 2 * first + 2, 2 * first + 1, 2 * first + 3],
                near[first : first + 2] + other[first : first + 2], outs, results,
            )
        grad_branch, grad_class_t = results
    else:
        grads = call(
            functools.partial(plain_late_kernel, kept, ahead),
            chunks_f32,
            [IN_VMEM] * len(late_ins),
            grad_flops,
        )(*late_ins)
        grad_branch, grad_class_t = call(
            functools.partial(plain_out_kernel, kept), outs, [IN_VMEM], 1000
        )(lax.psum(grads, "dom"))
    return (loss_rows, grad_branch, grad_class_t.T)


def solution(mesh):
    return jax.shard_map(
        body,
        mesh=mesh,
        in_specs=(
            P(("dom", "shuf"), None),
            P(("dom", "shuf"), None, None),
            P(("dom", "shuf")),
            P(("dom", "shuf")),
            P(("dom", "shuf")),
            P(("dom", "shuf")),
            P(("dom", "shuf")),
            P(("dom", "shuf"), None),
            P(("dom", "shuf"), None),
            P(("dom", "shuf")),
            P(),
            P(),
        ),
        out_specs=(P(("dom", "shuf")), P(None, None, "shuf"), P("shuf", None)),
        check_vma=False,
    )
```

```python
import functools
import math

import jax
import jax.numpy as jnp
from jax import lax
from jax.experimental import pallas as pl
from jax.experimental.pallas import tpu as pltpu
from jax.sharding import PartitionSpec as P

HOPS = 3
LANES = 128
VMEM_LIMIT = 24 * 1024 * 1024
VMEM_ALL = 56 * 1024 * 1024

IN_VMEM = pl.BlockSpec(memory_space=pltpu.VMEM)
IN_SMEM = pl.BlockSpec(memory_space=pltpu.SMEM)
ANYWHERE = pl.BlockSpec(memory_space=pl.ANY)
BF16 = jnp.bfloat16
F32 = jnp.float32


def up_to(value, multiple):
    return -(-value // multiple) * multiple


def passed_along(value, axis, steps):
    count = lax.axis_size(axis)
    pairs = [(source, (source + steps) % count) for source in range(count)]
    return lax.ppermute(value, axis, pairs)


def swapped(value, distance, axis="dom"):
    pairs = [(source, source ^ distance) for source in range(lax.axis_size(axis))]
    return lax.ppermute(value, axis, pairs)


def matmul(left, right, dims=((1,), (0,)), precision=None):
    return lax.dot_general(
        left, right, (dims, ((), ())), precision=precision, preferred_element_type=F32
    )


def call(kernel, out_shape, in_specs, flops, scratch=(), after=(), limit=VMEM_LIMIT):
    many = isinstance(out_shape, (list, tuple))
    outs = out_shape if many else [out_shape]
    moved = sum(math.prod(one.shape) * one.dtype.itemsize for one in outs)
    waited = len(after)

    def run(*refs):
        kernel(*refs[waited:])

    made = pl.pallas_call(
        run,
        out_shape=out_shape,
        in_specs=[ANYWHERE] * waited + in_specs,
        out_specs=[IN_VMEM] * len(outs) if many else IN_VMEM,
        scratch_shapes=list(scratch),
        compiler_params=pltpu.CompilerParams(vmem_limit_bytes=limit),
        cost_estimate=pl.CostEstimate(
            flops=flops, bytes_accessed=3 * moved if flops > 1000 else 1000, transcendentals=0
        ),
    )
    return functools.partial(made, *after)


class Plan:
    def __init__(self, tiles, slots):
        self.tiles = tiles
        self.slots = slots
        self.dst = 0
        self.src = tiles
        self.count = 2 * tiles
        self.left = 2 * tiles + 1
        self.right = self.left + slots
        self.sent = self.right + slots


def write_sends(blocks, left_ref, right_ref, ids, counts):
    for slot in range(left_ref.shape[0]):
        for side, out_ref in enumerate((left_ref, right_ref)):
            index = ids(side, slot)
            picked = blocks[0]
            for number in range(1, len(blocks)):
                picked = jnp.where(index == number, blocks[number], picked)
            out_ref[slot] = jnp.where(slot < counts(side), picked, 0.0)


def copied(sources, targets, sems):
    copies = [
        pltpu.make_async_copy(source, target, sems.at[number])
        for number, (source, target) in enumerate(zip(sources, targets))
    ]
    for copy in copies:
        copy.start()
    for copy in copies:
        copy.wait()


def first_kernel(
    sl_ref, sr_ref, sc_ref, feat_ref, label_from,
    left_ref, right_ref, held_ref, b_ref,
    sl_here, sr_here, sc_here, label_ref, sems,
):
    copied(
        (sl_ref, sr_ref, sc_ref, feat_ref, label_from),
        (sl_here, sr_here, sc_here, held_ref, label_ref),
        sems,
    )
    blocks = [held_ref[number] for number in range(held_ref.shape[0])]
    write_sends(
        blocks,
        left_ref,
        right_ref,
        lambda side, slot: (sl_here, sr_here)[side][slot],
        lambda side: sc_here[0, side],
    )
    write_rows(blocks, b_ref)
    nodes = label_ref.shape[1]
    width = b_ref.shape[1]
    per_piece = nodes // width
    place = lax.broadcasted_iota(jnp.int32, (16, width), 0)
    packed = jnp.zeros((16, width), F32)
    for piece in range(2):
        value = label_ref[...] & 255 if piece == 0 else label_ref[...] >> 8
        value = value.astype(F32)
        for part in range(per_piece):
            packed = jnp.where(
                place == piece * per_piece + part,
                value[:, part * width : (part + 1) * width],
                packed,
            )
    b_ref[nodes:] = packed.astype(BF16)


def write_rows(blocks, b_ref):
    for number, block in enumerate(blocks):
        size = block.shape[0]
        b_ref[number * size : (number + 1) * size] = block.astype(BF16)


def next_blocks(plan, plan_ref, cur_ref, tiles_ref, ext_ref):
    local = cur_ref.shape[0]
    ext_ref[:local] = cur_ref[...]
    totals = [jnp.zeros(cur_ref.shape[1:], F32) for _ in range(local)]
    live = plan_ref[plan.count]
    for tile in range(plan.tiles):
        product = matmul(
            tiles_ref[tile],
            ext_ref[plan_ref[plan.src + tile]],
            precision=lax.Precision.HIGHEST,
        )
        wanted = jnp.where(tile < live, plan_ref[plan.dst + tile], -1)
        for number in range(local):
            totals[number] = totals[number] + jnp.where(wanted == number, product, 0.0)
    return totals


def extend(cur_ref, low_ref, high_ref, ext_ref):
    local = cur_ref.shape[0]
    slots = low_ref.shape[0]
    ext_ref[local : local + slots] = low_ref[...]
    ext_ref[local + slots :] = high_ref[...]


def hop_kernel(
    plan, plan_ref, cur_ref, low_ref, high_ref, tiles_ref, next_ref, left_ref, right_ref, *refs
):
    ext_ref = refs[-1]
    extend(cur_ref, low_ref, high_ref, ext_ref)
    blocks = next_blocks(plan, plan_ref, cur_ref, tiles_ref, ext_ref)
    write_sends(
        blocks,
        left_ref,
        right_ref,
        lambda side, slot: plan_ref[(plan.left, plan.right)[side] + slot],
        lambda side: plan_ref[plan.sent + side],
    )
    for number, block in enumerate(blocks):
        next_ref[number] = block
    for b_ref in refs[:-1]:
        write_rows(blocks, b_ref)


def ready_kernel(cur_ref, tiles_ref, wc_ref, cur_out, tiles_out, wc_out):
    cur_out[...] = cur_ref[...]
    tiles_out[...] = tiles_ref[...]
    wc_out[...] = wc_ref[...]


def branch_logits(branch, rows, w_ref, wc_ref):
    hidden = jnp.maximum(matmul(rows, w_ref[branch]), 0.0).astype(BF16)
    hid = hidden.shape[1]
    return matmul(wc_ref[:, branch * hid : (branch + 1) * hid], hidden, ((1,), (1,)))


def forward_kernel(branch, cur_ref, w_ref, wc_ref, *refs):
    rows = cur_ref[...].reshape(-1, cur_ref.shape[2]).astype(BF16)
    part = branch_logits(branch, rows, w_ref, wc_ref)
    if len(refs) == 2:
        part = refs[0][...] + part
    refs[-1][...] = part


def places(order_ref):
    nodes = order_ref.shape[1]
    rows = lax.broadcasted_iota(jnp.int32, (nodes, nodes), 0)
    return (order_ref[...] == rows).astype(F32).astype(BF16)


def wanted_places(nodes, group, step, offset, count):
    share = nodes // group
    mine = lax.axis_index("shuf")
    first = mine * share
    source = lax.broadcasted_iota(jnp.int32, (count, nodes), 0) + offset
    target = lax.broadcasted_iota(jnp.int32, (count, nodes), 1)
    moved = source + ((mine ^ step) - mine) * share
    wanted = (target == moved) & (source >= first) & (source < first + share)
    return wanted.astype(F32).astype(BF16)


def label_kernel(order_ref, *refs):
    nodes = order_ref.shape[1]
    group = len(refs) - 1
    width = refs[0].shape[1]
    per_piece = nodes // width
    ordered = [jnp.zeros((1, nodes), F32) for _ in range(2)]
    for step in range(group):
        tail = refs[step][nodes:]
        for part in range(per_piece):
            moved = matmul(tail, wanted_places(nodes, group, step, part * width, width))
            for piece in range(2):
                row = piece * per_piece + part
                ordered[piece] = ordered[piece] + moved[row : row + 1]
    number = lax.broadcasted_iota(jnp.int32, (16, nodes), 0)
    packed = jnp.where(number == 0, ordered[0], jnp.where(number == 1, ordered[1], 0.0))
    pieces = matmul(packed.astype(BF16), places(order_ref), ((1,), (1,)))
    refs[-1][...] = (pieces[0:1] + 256.0 * pieces[1:2]).astype(jnp.int32)


def loss_kernel(*refs):
    group = len(refs) - 1
    height, nodes = refs[0].shape
    total = jnp.zeros((16, nodes), F32)
    for step in range(group):
        wanted = wanted_places(nodes, group, step, 0, nodes)
        total = total + matmul(refs[step][height - 16 :], wanted)
    refs[-1][...] = total[0:1] + total[1:2] + total[2:3]


def last_hop_kernel(plan, plan_ref, cur_ref, low_ref, high_ref, tiles_ref, out_ref, ext_ref):
    extend(cur_ref, low_ref, high_ref, ext_ref)
    blocks = next_blocks(plan, plan_ref, cur_ref, tiles_ref, ext_ref)
    for number, block in enumerate(blocks):
        width = block.shape[1]
        columns = slice(number * width, (number + 1) * width)
        out_ref[:, columns] = block.astype(BF16)


def stacked(ref, width):
    parts = ref.shape[1] // width
    return [ref[:, part * width : (part + 1) * width] for part in range(parts)]


def loss_and_gradient_kernel(
    row_scale, rows_ref, before_ref, w_ref, wc_ref, order_ref, label_ref, out_ref
):
    rows_b = jnp.concatenate(stacked(rows_ref, w_ref.shape[1]), axis=0)
    logits = before_ref[...] + branch_logits(w_ref.shape[0] - 1, rows_b, w_ref, wc_ref)
    classes, rows = logits.shape
    kept = up_to(classes, 16)
    hit = lax.broadcasted_iota(jnp.int32, (classes, rows), 0) == label_ref[...]
    top = jnp.max(logits, axis=0, keepdims=True)
    log_total = top + jnp.log(jnp.sum(jnp.exp(logits - top), axis=0, keepdims=True))
    loss = log_total - jnp.sum(jnp.where(hit, logits, 0.0), axis=0, keepdims=True)
    dlogits = (jnp.exp(logits - log_total) - jnp.where(hit, 1.0, 0.0)) * row_scale
    out_ref[kept - 16 : kept] = jnp.zeros((16, rows), BF16)
    out_ref[:classes] = dlogits.astype(BF16)
    number = lax.broadcasted_iota(jnp.int32, (16, rows), 0)
    packed = jnp.zeros((16, rows), F32)
    rest = loss
    for piece in range(3):
        part = rest.astype(BF16).astype(F32)
        packed = jnp.where(number == piece, part, packed)
        rest = rest - part
    out_ref[kept:] = matmul(packed.astype(BF16), places(order_ref)).astype(BF16)


def weights_kernel(w_ref, wc_ref, wt_ref, wct_ref, pad_ref):
    branches, own, kept = wct_ref.shape
    classes = wc_ref.shape[0]
    hid = w_ref.shape[2]
    first = lax.axis_index("shuf") * own
    pad_ref[...] = jnp.zeros_like(pad_ref)
    for branch in range(branches):
        columns = w_ref[branch, :, pl.ds(pl.multiple_of(first, LANES), own)]
        wt_ref[branch] = columns.astype(F32).T.astype(BF16)
        columns = wc_ref[:, pl.ds(pl.multiple_of(branch * hid + first, LANES), own)]
        pad_ref[:classes] = columns.astype(F32)
        wct_ref[branch] = pad_ref[...].T[:, :kept].astype(BF16)


def add_chunks(kept, before_ref, row_refs, last_refs, dlogit_refs, w_ref, wt_ref, wct_ref, chunks_ref):
    members = len(last_refs)
    branches, own, width = wt_ref.shape
    nodes = last_refs[0].shape[1]
    hid = w_ref.shape[2]
    all_rows = []
    for branch in range(branches - 1):
        ours = row_refs[branch * members : (branch + 1) * members]
        all_rows.append(jnp.concatenate([ref[:nodes] for ref in ours], axis=0))
    ours = [rows for ref in last_refs for rows in stacked(ref, width)]
    all_rows.append(jnp.concatenate(ours, axis=0))
    dlogits_t = jnp.concatenate([ref[:kept] for ref in dlogit_refs], axis=1)
    own_class = branches * own
    first = lax.axis_index("shuf") * own_class
    which = first // hid
    columns = pl.ds(pl.multiple_of(first - which * hid, LANES), own_class)
    chosen = all_rows[0]
    for branch in range(1, branches):
        chosen = jnp.where(which == branch, all_rows[branch], chosen)

    def put(chunk, rows, value):
        chunks_ref[chunk, rows] = value if before_ref is None else before_ref[chunk, rows] + value

    hidden = jnp.maximum(matmul(chosen, w_ref[which, :, columns]), 0.0).astype(BF16)
    class_t = matmul(dlogits_t, hidden)
    for chunk in range(chunks_ref.shape[0]):
        put(chunk, slice(0, kept), class_t[:, chunk * LANES : (chunk + 1) * LANES])
    per_branch = chunks_ref.shape[0] // branches
    for branch, rows in enumerate(all_rows):
        live = matmul(wt_ref[branch], rows, ((1,), (1,))) > 0.0
        dhidden_t = jnp.where(live, matmul(wct_ref[branch], dlogits_t), 0.0).astype(BF16)
        branch_t = matmul(dhidden_t, rows)
        for part in range(per_branch):
            put(
                branch * per_branch + part,
                slice(kept, kept + width),
                branch_t[part * LANES : (part + 1) * LANES],
            )


def split_refs(members, refs):
    last = len(refs) - 3 - 2 * members
    return (
        refs[:last], refs[last : last + members], refs[last + members : last + 2 * members],
        *refs[last + 2 * members :],
    )


def early_kernel(kept, members, *refs):
    add_chunks(kept, None, *split_refs(members, refs[:-1]), refs[-1])


def late_chunks(kept, members, early_ref, refs, chunks_ref):
    add_chunks(kept, early_ref, *split_refs(members, refs), chunks_ref)


def late_kernel(kept, members, half, early_ref, *refs):
    ins = len(refs) - 1 - 2 * half
    outs = refs[ins:-1]
    chunks_ref = refs[-1]
    late_chunks(kept, members, early_ref, refs[:ins], chunks_ref)
    dom = lax.axis_index("dom")
    for step in range(half):
        stays = dom ^ (2 * step)
        outs[step][...] = chunks_ref[stays]
        outs[half + step][...] = chunks_ref[stays ^ 1].astype(BF16)


def plain_late_kernel(kept, members, early_ref, *refs):
    late_chunks(kept, members, early_ref, refs[:-1], refs[-1])


def write_chunk(kept, chunk, value, branch_ref, class_ref):
    per_branch = branch_ref.shape[2] // LANES
    start = pl.multiple_of(chunk * LANES, LANES)
    class_ref[:, pl.ds(start, LANES)] = value[: class_ref.shape[0]]
    branch = chunk // per_branch
    start = pl.multiple_of((chunk - branch * per_branch) * LANES, LANES)
    branch_ref[branch, :, pl.ds(start, LANES)] = value[kept:].T


def out_kernel(kept, distances, *refs):
    count = len(distances)
    ins = refs[-5 - count : -5]
    branch_ref, class_ref, branch_here, class_here, sems = refs[-5:]
    dom = lax.axis_index("dom")
    per_branch = branch_ref.shape[2] // LANES
    copies = []
    for number, distance in enumerate(distances):
        chunk = dom ^ distance
        value = ins[number][...].astype(F32)
        class_here[number] = value[: class_ref.shape[0]]
        start = pl.multiple_of(chunk * LANES, LANES)
        copies.append(
            pltpu.make_async_copy(
                class_here.at[number], class_ref.at[:, pl.ds(start, LANES)], sems.at[2 * number]
            )
        )
        copies[-1].start()
        branch_here[number] = value[kept:].T
        branch = chunk // per_branch
        start = pl.multiple_of((chunk - branch * per_branch) * LANES, LANES)
        copies.append(
            pltpu.make_async_copy(
                branch_here.at[number],
                branch_ref.at[branch, :, pl.ds(start, LANES)],
                sems.at[2 * number + 1],
            )
        )
        copies[-1].start()
    for copy in copies:
        copy.wait()


def write_out(kept, distances, values, outs, before):
    count = len(distances)
    return pl.pallas_call(
        functools.partial(out_kernel, kept, distances),
        out_shape=outs,
        in_specs=[ANYWHERE] * len(before) + [IN_VMEM] * count,
        out_specs=[pl.BlockSpec(memory_space=pltpu.HBM)] * 2,
        scratch_shapes=[
            pltpu.VMEM((count, outs[0].shape[1], LANES), F32),
            pltpu.VMEM((count, outs[1].shape[0], LANES), F32),
            pltpu.SemaphoreType.DMA((2 * count,)),
        ],
        input_output_aliases={0: 0, 1: 1} if before else {},
        compiler_params=pltpu.CompilerParams(vmem_limit_bytes=VMEM_LIMIT),
        cost_estimate=pl.CostEstimate(flops=1000, bytes_accessed=1000, transcendentals=0),
    )(*before, *values)


def plain_out_kernel(kept, in_ref, branch_ref, class_ref):
    for chunk in range(in_ref.shape[0]):
        write_chunk(kept, chunk, in_ref[chunk], branch_ref, class_ref)


def in_group(value, distance=None):
    members = [value]
    steps = [0]
    distance = lax.axis_size("shuf") // 2 if distance is None else distance
    while distance:
        members += [swapped(member, distance, "shuf") for member in members]
        steps += [step + distance for step in steps]
        distance //= 2
    return [members[steps.index(step)] for step in range(len(steps))]


def body(
    features, tile_values, tile_dst, tile_src, tile_count, send_left, send_right,
    send_count, batch_order, labels, w_branch, w_class,
):
    block = tile_values.shape[1]
    nodes, width = features.shape
    local = nodes // block
    slots = send_left.shape[0]
    tiles = tile_values.shape[0]
    branches, _, hid = w_branch.shape
    cat, classes = w_class.shape
    dom = lax.axis_size("dom")
    shuf = lax.axis_size("shuf")
    mine = lax.axis_index("shuf")
    share = nodes // shuf
    own = hid // shuf
    own_class = cat // shuf
    kept = up_to(classes, 16)
    row_scale = 1.0 / math.sqrt(float(nodes * dom * shuf))
    plan = Plan(tiles, slots)
    small = jnp.concatenate(
        [tile_dst, tile_src, tile_count, send_left, send_right, send_count.reshape(-1)]
    )
    blocks_f32 = jax.ShapeDtypeStruct((local, block, width), F32)
    slots_f32 = jax.ShapeDtypeStruct((slots, block, width), F32)
    rows_b16 = jax.ShapeDtypeStruct((nodes, width), BF16)
    first_b16 = jax.ShapeDtypeStruct((nodes + 16, width), BF16)
    logits_f32 = jax.ShapeDtypeStruct((classes, nodes), F32)
    w_class_t = w_class.T

    current = features.reshape(local, block, width)
    gathered = []
    logits = None
    hop_flops = 12 * tiles * block * block * width
    forward_flops = 2 * nodes * hid * (width + classes)
    ext = pltpu.VMEM((local + 2 * slots, block, width), F32)
    to_left, to_right, current, *rows = call(
        first_kernel,
        [slots_f32, slots_f32, blocks_f32, first_b16],
        [ANYWHERE] * 5,
        1000,
        [
            pltpu.SMEM((slots,), jnp.int32),
            pltpu.SMEM((slots,), jnp.int32),
            pltpu.SMEM((1, 2), jnp.int32),
            pltpu.VMEM((1, nodes), jnp.int32),
            pltpu.SemaphoreType.DMA((5,)),
        ],
        limit=VMEM_ALL,
    )(send_left, send_right, send_count, current, labels.reshape(1, nodes))
    current, tile_values, w_class_t = call(
        ready_kernel,
        [
            blocks_f32,
            jax.ShapeDtypeStruct(tile_values.shape, F32),
            jax.ShapeDtypeStruct(w_class_t.shape, BF16),
        ],
        [IN_VMEM] * 3,
        1000,
    )(current, tile_values, w_class_t)
    for hop in range(HOPS):
        from_lower = passed_along(to_right, "dom", 1)
        from_upper = passed_along(to_left, "dom", -1)
        for value in rows:
            gathered.append(in_group(value))
        before = [] if logits is None else [logits]
        logits = call(
            functools.partial(forward_kernel, hop),
            logits_f32,
            [IN_VMEM] * (3 + len(before)),
            forward_flops,
            after=[members[shuf // 2] for members in gathered[:2]] if hop == HOPS - 1 else [],
        )(current, w_branch, w_class_t, *before)
        if hop == 0:
            first_logits = logits
            after = []
        else:
            after = [first_logits]
        if hop < HOPS - 1:
            current, to_left, to_right, *rows = call(
                functools.partial(hop_kernel, plan),
                [blocks_f32, slots_f32, slots_f32, rows_b16],
                [IN_SMEM] + [IN_VMEM] * 4,
                hop_flops,
                [ext],
                after,
            )(small, current, from_lower, from_upper, tile_values)

    label_mine = call(
        label_kernel,
        jax.ShapeDtypeStruct((1, nodes), jnp.int32),
        [IN_VMEM] * (1 + shuf),
        1000,
    )(batch_order, *gathered[0])

    wt_own, wct_own = call(
        weights_kernel,
        [
            jax.ShapeDtypeStruct((branches, own, width), BF16),
            jax.ShapeDtypeStruct((branches, own, kept), BF16),
        ],
        [IN_VMEM] * 2,
        1000,
        [pltpu.VMEM((up_to(classes, LANES), own), F32)],
    )(w_branch, w_class_t)

    last_rows = call(
        functools.partial(last_hop_kernel, plan),
        jax.ShapeDtypeStruct((block, local * width), BF16),
        [IN_SMEM] + [IN_VMEM] * 4,
        hop_flops,
        [ext],
        [logits, label_mine, *gathered[1][1:]],
    )(small, current, from_lower, from_upper, tile_values)
    dlogits = call(
        functools.partial(loss_and_gradient_kernel, row_scale),
        jax.ShapeDtypeStruct((kept + 16, nodes), BF16),
        [IN_VMEM] * 6,
        1000,
        after=[gathered[2][shuf // 2]],
    )(last_rows, logits, w_branch, w_class_t, batch_order, label_mine)
    chunks = own_class // LANES
    height = kept + width
    ahead = shuf // 2
    chunks_f32 = jax.ShapeDtypeStruct((chunks, height, LANES), F32)
    grad_flops = shuf * nodes * own_class * (3 * width + 2 * kept)
    weights = (w_branch, wt_own, wct_own)
    across_rows = swapped(last_rows, ahead, "shuf")
    across = swapped(dlogits, ahead, "shuf")
    close_rows = in_group(last_rows, ahead // 2)
    close = in_group(dlogits, ahead // 2)
    early = call(
        functools.partial(early_kernel, kept, ahead),
        chunks_f32,
        [IN_VMEM] * (5 * ahead + 3),
        1000,
        after=[across_rows],
    )(
        *[member for members in gathered for member in members[:ahead]],
        *close_rows, *close, *weights,
    )
    across, across_rows, early = lax.optimization_barrier((across, across_rows, early))
    distant_rows = in_group(across_rows, ahead // 2)
    distant = in_group(across, ahead // 2)
    late_ins = (
        early, *[member for members in gathered for member in members[ahead:]],
        *distant_rows, *distant, *weights,
    )
    last_all = close + distant
    loss_rows = call(
        loss_kernel, jax.ShapeDtypeStruct((1, nodes), F32), [IN_VMEM] * shuf, 1000
    )(*last_all).reshape(nodes)

    outs = [
        jax.ShapeDtypeStruct((branches, width, own), F32),
        jax.ShapeDtypeStruct((classes, own_class), F32),
    ]
    if chunks == dom and dom % 2 == 0 and dom & (dom - 1) == 0:
        half = dom // 2
        one_f32 = jax.ShapeDtypeStruct((height, LANES), F32)
        made = call(
            functools.partial(late_kernel, kept, ahead, half),
            [one_f32] * half + [jax.ShapeDtypeStruct((height, LANES), BF16)] * half,
            [IN_VMEM] * len(late_ins),
            grad_flops,
            [pltpu.VMEM(chunks_f32.shape, F32)],
        )(*late_ins)
        order = sorted(range(half), key=lambda step: (step % 2 == 0, -step))
        arrived = {step: swapped(made[half + step], 1) for step in order}
        total = {step: made[step] + arrived[step].astype(F32) for step in order}
        distance = 1
        while distance < half:
            far = [step for step in total if step & distance]
            for step in far:
                came = swapped(total.pop(step).astype(BF16), 2 * distance)
                kept_step = step ^ distance
                total[kept_step] = lax.optimization_barrier(
                    total[kept_step] + came.astype(F32)
                )
            distance *= 2
        summed = total[0]
        near = [summed.astype(BF16)]
        near += [swapped(near[0], 2 * step) for step in range(1, half)]
        other = [swapped(value, 1) for value in near]
        results = []
        places = [2 * step for step in range(half)] + [2 * step + 1 for step in range(half)]
        for part in (slice(0, -half // 2), slice(-half // 2, None)):
            results = write_out(kept, places[part], (near + other)[part], outs, results)
        grad_branch, grad_class_t = results
    else:
        grads = call(
            functools.partial(plain_late_kernel, kept, ahead),
            chunks_f32,
            [IN_VMEM] * len(late_ins),
            grad_flops,
        )(*late_ins)
        grad_branch, grad_class_t = call(
            functools.partial(plain_out_kernel, kept), outs, [IN_VMEM], 1000
        )(lax.psum(grads, "dom"))
    return (loss_rows, grad_branch, grad_class_t.T)


def solution(mesh):
    return jax.shard_map(
        body,
        mesh=mesh,
        in_specs=(
            P(("dom", "shuf"), None),
            P(("dom", "shuf"), None, None),
            P(("dom", "shuf")),
            P(("dom", "shuf")),
            P(("dom", "shuf")),
            P(("dom", "shuf")),
            P(("dom", "shuf")),
            P(("dom", "shuf"), None),
            P(("dom", "shuf"), None),
            P(("dom", "shuf")),
            P(),
            P(),
        ),
        out_specs=(P(("dom", "shuf")), P(None, None, "shuf"), P("shuf", None)),
        check_vma=False,
    )
```

```python
import functools
import math

import jax
import jax.numpy as jnp
from jax import lax
from jax.experimental import pallas as pl
from jax.experimental.pallas import tpu as pltpu
from jax.sharding import PartitionSpec as P

HOPS = 3
LANES = 128
VMEM_LIMIT = 24 * 1024 * 1024
VMEM_ALL = 56 * 1024 * 1024

IN_VMEM = pl.BlockSpec(memory_space=pltpu.VMEM)
IN_SMEM = pl.BlockSpec(memory_space=pltpu.SMEM)
ANYWHERE = pl.BlockSpec(memory_space=pl.ANY)
BF16 = jnp.bfloat16
F32 = jnp.float32


def up_to(value, multiple):
    return -(-value // multiple) * multiple


def passed_along(value, axis, steps):
    count = lax.axis_size(axis)
    pairs = [(source, (source + steps) % count) for source in range(count)]
    return lax.ppermute(value, axis, pairs)


def swapped(value, distance, axis="dom"):
    pairs = [(source, source ^ distance) for source in range(lax.axis_size(axis))]
    return lax.ppermute(value, axis, pairs)


def matmul(left, right, dims=((1,), (0,)), precision=None):
    return lax.dot_general(
        left, right, (dims, ((), ())), precision=precision, preferred_element_type=F32
    )


def call(kernel, out_shape, in_specs, flops, scratch=(), after=(), limit=VMEM_LIMIT):
    many = isinstance(out_shape, (list, tuple))
    outs = out_shape if many else [out_shape]
    moved = sum(math.prod(one.shape) * one.dtype.itemsize for one in outs)
    waited = len(after)

    def run(*refs):
        kernel(*refs[waited:])

    made = pl.pallas_call(
        run,
        out_shape=out_shape,
        in_specs=[ANYWHERE] * waited + in_specs,
        out_specs=[IN_VMEM] * len(outs) if many else IN_VMEM,
        scratch_shapes=list(scratch),
        compiler_params=pltpu.CompilerParams(vmem_limit_bytes=limit),
        cost_estimate=pl.CostEstimate(
            flops=flops, bytes_accessed=3 * moved if flops > 1000 else 1000, transcendentals=0
        ),
    )
    return functools.partial(made, *after)


class Plan:
    def __init__(self, tiles, slots):
        self.tiles = tiles
        self.slots = slots
        self.dst = 0
        self.src = tiles
        self.count = 2 * tiles
        self.left = 2 * tiles + 1
        self.right = self.left + slots
        self.sent = self.right + slots


def write_sends(blocks, left_ref, right_ref, ids, counts):
    for slot in range(left_ref.shape[0]):
        for side, out_ref in enumerate((left_ref, right_ref)):
            index = ids(side, slot)
            picked = blocks[0]
            for number in range(1, len(blocks)):
                picked = jnp.where(index == number, blocks[number], picked)
            out_ref[slot] = jnp.where(slot < counts(side), picked, 0.0)


def copied(sources, targets, sems):
    copies = [
        pltpu.make_async_copy(source, target, sems.at[number])
        for number, (source, target) in enumerate(zip(sources, targets))
    ]
    for copy in copies:
        copy.start()
    for copy in copies:
        copy.wait()


def first_kernel(
    sl_ref, sr_ref, sc_ref, feat_ref, label_from,
    left_ref, right_ref, held_ref, b_ref,
    sl_here, sr_here, sc_here, label_ref, sems,
):
    copied(
        (sl_ref, sr_ref, sc_ref, feat_ref, label_from),
        (sl_here, sr_here, sc_here, held_ref, label_ref),
        sems,
    )
    blocks = [held_ref[number] for number in range(held_ref.shape[0])]
    write_sends(
        blocks,
        left_ref,
        right_ref,
        lambda side, slot: (sl_here, sr_here)[side][slot],
        lambda side: sc_here[0, side],
    )
    write_rows(blocks, b_ref)
    nodes = label_ref.shape[1]
    width = b_ref.shape[1]
    per_piece = nodes // width
    place = lax.broadcasted_iota(jnp.int32, (16, width), 0)
    packed = jnp.zeros((16, width), F32)
    for piece in range(2):
        value = label_ref[...] & 255 if piece == 0 else label_ref[...] >> 8
        value = value.astype(F32)
        for part in range(per_piece):
            packed = jnp.where(
                place == piece * per_piece + part,
                value[:, part * width : (part + 1) * width],
                packed,
            )
    b_ref[nodes:] = packed.astype(BF16)


def write_rows(blocks, b_ref):
    for number, block in enumerate(blocks):
        size = block.shape[0]
        b_ref[number * size : (number + 1) * size] = block.astype(BF16)


def next_blocks(plan, plan_ref, cur_ref, tiles_ref, ext_ref):
    local = cur_ref.shape[0]
    ext_ref[:local] = cur_ref[...]
    totals = [jnp.zeros(cur_ref.shape[1:], F32) for _ in range(local)]
    live = plan_ref[plan.count]
    for tile in range(plan.tiles):
        product = matmul(
            tiles_ref[tile],
            ext_ref[plan_ref[plan.src + tile]],
            precision=lax.Precision.HIGHEST,
        )
        wanted = jnp.where(tile < live, plan_ref[plan.dst + tile], -1)
        for number in range(local):
            totals[number] = totals[number] + jnp.where(wanted == number, product, 0.0)
    return totals


def extend(cur_ref, low_ref, high_ref, ext_ref):
    local = cur_ref.shape[0]
    slots = low_ref.shape[0]
    ext_ref[local : local + slots] = low_ref[...]
    ext_ref[local + slots :] = high_ref[...]


def hop_kernel(
    plan, plan_ref, cur_ref, low_ref, high_ref, tiles_ref, next_ref, left_ref, right_ref, *refs
):
    ext_ref = refs[-1]
    extend(cur_ref, low_ref, high_ref, ext_ref)
    blocks = next_blocks(plan, plan_ref, cur_ref, tiles_ref, ext_ref)
    write_sends(
        blocks,
        left_ref,
        right_ref,
        lambda side, slot: plan_ref[(plan.left, plan.right)[side] + slot],
        lambda side: plan_ref[plan.sent + side],
    )
    for number, block in enumerate(blocks):
        next_ref[number] = block
    for b_ref in refs[:-1]:
        write_rows(blocks, b_ref)


def ready_kernel(cur_ref, tiles_ref, wc_ref, cur_out, tiles_out, wc_out):
    cur_out[...] = cur_ref[...]
    tiles_out[...] = tiles_ref[...]
    wc_out[...] = wc_ref[...]


def branch_logits(branch, rows, w_ref, wc_ref):
    hidden = jnp.maximum(matmul(rows, w_ref[branch]), 0.0).astype(BF16)
    hid = hidden.shape[1]
    return matmul(wc_ref[:, branch * hid : (branch + 1) * hid], hidden, ((1,), (1,)))


def forward_kernel(branch, cur_ref, w_ref, wc_ref, *refs):
    rows = cur_ref[...].reshape(-1, cur_ref.shape[2]).astype(BF16)
    part = branch_logits(branch, rows, w_ref, wc_ref)
    if len(refs) == 2:
        part = refs[0][...] + part
    refs[-1][...] = part


def places(order_ref):
    nodes = order_ref.shape[1]
    rows = lax.broadcasted_iota(jnp.int32, (nodes, nodes), 0)
    return (order_ref[...] == rows).astype(F32).astype(BF16)


def wanted_places(nodes, group, step, offset, count):
    share = nodes // group
    mine = lax.axis_index("shuf")
    first = mine * share
    source = lax.broadcasted_iota(jnp.int32, (count, nodes), 0) + offset
    target = lax.broadcasted_iota(jnp.int32, (count, nodes), 1)
    moved = source + ((mine ^ step) - mine) * share
    wanted = (target == moved) & (source >= first) & (source < first + share)
    return wanted.astype(F32).astype(BF16)


def label_kernel(order_ref, *refs):
    nodes = order_ref.shape[1]
    group = len(refs) - 1
    width = refs[0].shape[1]
    per_piece = nodes // width
    ordered = [jnp.zeros((1, nodes), F32) for _ in range(2)]
    for step in range(group):
        tail = refs[step][nodes:]
        for part in range(per_piece):
            moved = matmul(tail, wanted_places(nodes, group, step, part * width, width))
            for piece in range(2):
                row = piece * per_piece + part
                ordered[piece] = ordered[piece] + moved[row : row + 1]
    number = lax.broadcasted_iota(jnp.int32, (16, nodes), 0)
    packed = jnp.where(number == 0, ordered[0], jnp.where(number == 1, ordered[1], 0.0))
    pieces = matmul(packed.astype(BF16), places(order_ref), ((1,), (1,)))
    refs[-1][...] = (pieces[0:1] + 256.0 * pieces[1:2]).astype(jnp.int32)


def loss_kernel(*refs):
    group = len(refs) - 1
    height, nodes = refs[0].shape
    total = jnp.zeros((16, nodes), F32)
    for step in range(group):
        wanted = wanted_places(nodes, group, step, 0, nodes)
        total = total + matmul(refs[step][height - 16 :], wanted)
    refs[-1][...] = total[0:1] + total[1:2] + total[2:3]


def last_hop_kernel(plan, plan_ref, cur_ref, low_ref, high_ref, tiles_ref, out_ref, ext_ref):
    extend(cur_ref, low_ref, high_ref, ext_ref)
    blocks = next_blocks(plan, plan_ref, cur_ref, tiles_ref, ext_ref)
    for number, block in enumerate(blocks):
        width = block.shape[1]
        columns = slice(number * width, (number + 1) * width)
        out_ref[:, columns] = block.astype(BF16)


def stacked(ref, width):
    parts = ref.shape[1] // width
    return [ref[:, part * width : (part + 1) * width] for part in range(parts)]


def loss_and_gradient_kernel(
    row_scale, rows_ref, before_ref, w_ref, wc_ref, order_ref, label_ref, out_ref
):
    rows_b = jnp.concatenate(stacked(rows_ref, w_ref.shape[1]), axis=0)
    logits = before_ref[...] + branch_logits(w_ref.shape[0] - 1, rows_b, w_ref, wc_ref)
    classes, rows = logits.shape
    kept = up_to(classes, 16)
    hit = lax.broadcasted_iota(jnp.int32, (classes, rows), 0) == label_ref[...]
    top = jnp.max(logits, axis=0, keepdims=True)
    log_total = top + jnp.log(jnp.sum(jnp.exp(logits - top), axis=0, keepdims=True))
    loss = log_total - jnp.sum(jnp.where(hit, logits, 0.0), axis=0, keepdims=True)
    dlogits = (jnp.exp(logits - log_total) - jnp.where(hit, 1.0, 0.0)) * row_scale
    out_ref[kept - 16 : kept] = jnp.zeros((16, rows), BF16)
    out_ref[:classes] = dlogits.astype(BF16)
    number = lax.broadcasted_iota(jnp.int32, (16, rows), 0)
    packed = jnp.zeros((16, rows), F32)
    rest = loss
    for piece in range(3):
        part = rest.astype(BF16).astype(F32)
        packed = jnp.where(number == piece, part, packed)
        rest = rest - part
    out_ref[kept:] = matmul(packed.astype(BF16), places(order_ref)).astype(BF16)


def weights_kernel(w_ref, wc_ref, wt_ref, wct_ref, pad_ref):
    branches, own, kept = wct_ref.shape
    classes = wc_ref.shape[0]
    hid = w_ref.shape[2]
    first = lax.axis_index("shuf") * own
    pad_ref[...] = jnp.zeros_like(pad_ref)
    for branch in range(branches):
        columns = w_ref[branch, :, pl.ds(pl.multiple_of(first, LANES), own)]
        wt_ref[branch] = columns.astype(F32).T.astype(BF16)
        columns = wc_ref[:, pl.ds(pl.multiple_of(branch * hid + first, LANES), own)]
        pad_ref[:classes] = columns.astype(F32)
        wct_ref[branch] = pad_ref[...].T[:, :kept].astype(BF16)


def add_chunks(kept, before_ref, row_refs, last_refs, dlogit_refs, w_ref, wt_ref, wct_ref, chunks_ref):
    members = len(last_refs)
    branches, own, width = wt_ref.shape
    nodes = last_refs[0].shape[1]
    hid = w_ref.shape[2]
    all_rows = []
    for branch in range(branches - 1):
        ours = row_refs[branch * members : (branch + 1) * members]
        all_rows.append(jnp.concatenate([ref[:nodes] for ref in ours], axis=0))
    ours = [rows for ref in last_refs for rows in stacked(ref, width)]
    all_rows.append(jnp.concatenate(ours, axis=0))
    dlogits_t = jnp.concatenate([ref[:kept] for ref in dlogit_refs], axis=1)
    own_class = branches * own
    first = lax.axis_index("shuf") * own_class
    which = first // hid
    columns = pl.ds(pl.multiple_of(first - which * hid, LANES), own_class)
    chosen = all_rows[0]
    for branch in range(1, branches):
        chosen = jnp.where(which == branch, all_rows[branch], chosen)

    def put(chunk, rows, value):
        chunks_ref[chunk, rows] = value if before_ref is None else before_ref[chunk, rows] + value

    hidden = jnp.maximum(matmul(chosen, w_ref[which, :, columns]), 0.0).astype(BF16)
    class_t = matmul(dlogits_t, hidden)
    for chunk in range(chunks_ref.shape[0]):
        put(chunk, slice(0, kept), class_t[:, chunk * LANES : (chunk + 1) * LANES])
    per_branch = chunks_ref.shape[0] // branches
    for branch, rows in enumerate(all_rows):
        live = matmul(wt_ref[branch], rows, ((1,), (1,))) > 0.0
        dhidden_t = jnp.where(live, matmul(wct_ref[branch], dlogits_t), 0.0).astype(BF16)
        branch_t = matmul(dhidden_t, rows)
        for part in range(per_branch):
            put(
                branch * per_branch + part,
                slice(kept, kept + width),
                branch_t[part * LANES : (part + 1) * LANES],
            )


def split_refs(members, refs):
    last = len(refs) - 3 - 2 * members
    return (
        refs[:last], refs[last : last + members], refs[last + members : last + 2 * members],
        *refs[last + 2 * members :],
    )


def early_kernel(kept, members, *refs):
    add_chunks(kept, None, *split_refs(members, refs[:-1]), refs[-1])


def late_chunks(kept, members, early_ref, refs, chunks_ref):
    add_chunks(kept, early_ref, *split_refs(members, refs), chunks_ref)


def late_kernel(kept, members, half, early_ref, *refs):
    ins = len(refs) - 1 - 2 * half
    outs = refs[ins:-1]
    chunks_ref = refs[-1]
    late_chunks(kept, members, early_ref, refs[:ins], chunks_ref)
    dom = lax.axis_index("dom")
    for step in range(half):
        stays = dom ^ (2 * step)
        outs[step][...] = chunks_ref[stays]
        outs[half + step][...] = chunks_ref[stays ^ 1].astype(BF16)


def plain_late_kernel(kept, members, early_ref, *refs):
    late_chunks(kept, members, early_ref, refs[:-1], refs[-1])


def write_chunk(kept, chunk, value, branch_ref, class_ref):
    per_branch = branch_ref.shape[2] // LANES
    start = pl.multiple_of(chunk * LANES, LANES)
    class_ref[:, pl.ds(start, LANES)] = value[: class_ref.shape[0]]
    branch = chunk // per_branch
    start = pl.multiple_of((chunk - branch * per_branch) * LANES, LANES)
    branch_ref[branch, :, pl.ds(start, LANES)] = value[kept:].T


def out_kernel(kept, distances, *refs):
    count = len(distances)
    ins = refs[-5 - count : -5]
    branch_ref, class_ref, branch_here, class_here, sems = refs[-5:]
    dom = lax.axis_index("dom")
    per_branch = branch_ref.shape[2] // LANES
    copies = []
    for number, distance in enumerate(distances):
        chunk = dom ^ distance
        value = ins[number][...].astype(F32)
        class_here[number] = value[: class_ref.shape[0]]
        start = pl.multiple_of(chunk * LANES, LANES)
        copies.append(
            pltpu.make_async_copy(
                class_here.at[number], class_ref.at[:, pl.ds(start, LANES)], sems.at[2 * number]
            )
        )
        copies[-1].start()
        branch_here[number] = value[kept:].T
        branch = chunk // per_branch
        start = pl.multiple_of((chunk - branch * per_branch) * LANES, LANES)
        copies.append(
            pltpu.make_async_copy(
                branch_here.at[number],
                branch_ref.at[branch, :, pl.ds(start, LANES)],
                sems.at[2 * number + 1],
            )
        )
        copies[-1].start()
    for copy in copies:
        copy.wait()


def write_out(kept, distances, values, outs, before):
    count = len(distances)
    return pl.pallas_call(
        functools.partial(out_kernel, kept, distances),
        out_shape=outs,
        in_specs=[ANYWHERE] * len(before) + [IN_VMEM] * count,
        out_specs=[pl.BlockSpec(memory_space=pltpu.HBM)] * 2,
        scratch_shapes=[
            pltpu.VMEM((count, outs[0].shape[1], LANES), F32),
            pltpu.VMEM((count, outs[1].shape[0], LANES), F32),
            pltpu.SemaphoreType.DMA((2 * count,)),
        ],
        input_output_aliases={0: 0, 1: 1} if before else {},
        compiler_params=pltpu.CompilerParams(vmem_limit_bytes=VMEM_LIMIT),
        cost_estimate=pl.CostEstimate(flops=1000, bytes_accessed=1000, transcendentals=0),
    )(*before, *values)


def plain_out_kernel(kept, in_ref, branch_ref, class_ref):
    for chunk in range(in_ref.shape[0]):
        write_chunk(kept, chunk, in_ref[chunk], branch_ref, class_ref)


def in_group(value, distance=None):
    members = [value]
    steps = [0]
    distance = lax.axis_size("shuf") // 2 if distance is None else distance
    while distance:
        members += [swapped(member, distance, "shuf") for member in members]
        steps += [step + distance for step in steps]
        distance //= 2
    return [members[steps.index(step)] for step in range(len(steps))]


def body(
    features, tile_values, tile_dst, tile_src, tile_count, send_left, send_right,
    send_count, batch_order, labels, w_branch, w_class,
):
    block = tile_values.shape[1]
    nodes, width = features.shape
    local = nodes // block
    slots = send_left.shape[0]
    tiles = tile_values.shape[0]
    branches, _, hid = w_branch.shape
    cat, classes = w_class.shape
    dom = lax.axis_size("dom")
    shuf = lax.axis_size("shuf")
    mine = lax.axis_index("shuf")
    share = nodes // shuf
    own = hid // shuf
    own_class = cat // shuf
    kept = up_to(classes, 16)
    row_scale = 1.0 / math.sqrt(float(nodes * dom * shuf))
    plan = Plan(tiles, slots)
    small = jnp.concatenate(
        [tile_dst, tile_src, tile_count, send_left, send_right, send_count.reshape(-1)]
    )
    blocks_f32 = jax.ShapeDtypeStruct((local, block, width), F32)
    slots_f32 = jax.ShapeDtypeStruct((slots, block, width), F32)
    rows_b16 = jax.ShapeDtypeStruct((nodes, width), BF16)
    first_b16 = jax.ShapeDtypeStruct((nodes + 16, width), BF16)
    logits_f32 = jax.ShapeDtypeStruct((classes, nodes), F32)
    w_class_t = w_class.T

    current = features.reshape(local, block, width)
    gathered = []
    logits = None
    hop_flops = 12 * tiles * block * block * width
    forward_flops = 2 * nodes * hid * (width + classes)
    ext = pltpu.VMEM((local + 2 * slots, block, width), F32)
    to_left, to_right, current, *rows = call(
        first_kernel,
        [slots_f32, slots_f32, blocks_f32, first_b16],
        [ANYWHERE] * 5,
        1000,
        [
            pltpu.SMEM((slots,), jnp.int32),
            pltpu.SMEM((slots,), jnp.int32),
            pltpu.SMEM((1, 2), jnp.int32),
            pltpu.VMEM((1, nodes), jnp.int32),
            pltpu.SemaphoreType.DMA((5,)),
        ],
        limit=VMEM_ALL,
    )(send_left, send_right, send_count, current, labels.reshape(1, nodes))
    current, tile_values, w_class_t = call(
        ready_kernel,
        [
            blocks_f32,
            jax.ShapeDtypeStruct(tile_values.shape, F32),
            jax.ShapeDtypeStruct(w_class_t.shape, BF16),
        ],
        [IN_VMEM] * 3,
        1000,
    )(current, tile_values, w_class_t)
    for hop in range(HOPS):
        from_lower = passed_along(to_right, "dom", 1)
        from_upper = passed_along(to_left, "dom", -1)
        for value in rows:
            gathered.append(in_group(value))
        before = [] if logits is None else [logits]
        logits = call(
            functools.partial(forward_kernel, hop),
            logits_f32,
            [IN_VMEM] * (3 + len(before)),
            forward_flops,
            after=[members[shuf // 2] for members in gathered[:2]] if hop == HOPS - 1 else [],
        )(current, w_branch, w_class_t, *before)
        if hop == 0:
            first_logits = logits
            after = []
        else:
            after = [first_logits]
        if hop < HOPS - 1:
            current, to_left, to_right, *rows = call(
                functools.partial(hop_kernel, plan),
                [blocks_f32, slots_f32, slots_f32, rows_b16],
                [IN_SMEM] + [IN_VMEM] * 4,
                hop_flops,
                [ext],
                after,
            )(small, current, from_lower, from_upper, tile_values)

    label_mine = call(
        label_kernel,
        jax.ShapeDtypeStruct((1, nodes), jnp.int32),
        [IN_VMEM] * (1 + shuf),
        1000,
    )(batch_order, *gathered[0])

    wt_own, wct_own = call(
        weights_kernel,
        [
            jax.ShapeDtypeStruct((branches, own, width), BF16),
            jax.ShapeDtypeStruct((branches, own, kept), BF16),
        ],
        [IN_VMEM] * 2,
        1000,
        [pltpu.VMEM((up_to(classes, LANES), own), F32)],
    )(w_branch, w_class_t)

    last_rows = call(
        functools.partial(last_hop_kernel, plan),
        jax.ShapeDtypeStruct((block, local * width), BF16),
        [IN_SMEM] + [IN_VMEM] * 4,
        hop_flops,
        [ext],
        [logits, label_mine, *gathered[1][1:]],
    )(small, current, from_lower, from_upper, tile_values)
    dlogits = call(
        functools.partial(loss_and_gradient_kernel, row_scale),
        jax.ShapeDtypeStruct((kept + 16, nodes), BF16),
        [IN_VMEM] * 6,
        1000,
        after=[gathered[2][shuf // 2]],
    )(last_rows, logits, w_branch, w_class_t, batch_order, label_mine)
    chunks = own_class // LANES
    height = kept + width
    ahead = shuf // 2
    chunks_f32 = jax.ShapeDtypeStruct((chunks, height, LANES), F32)
    grad_flops = shuf * nodes * own_class * (3 * width + 2 * kept)
    weights = (w_branch, wt_own, wct_own)
    across_rows = swapped(last_rows, ahead, "shuf")
    across = swapped(dlogits, ahead, "shuf")
    close_rows = in_group(last_rows, ahead // 2)
    close = in_group(dlogits, ahead // 2)
    early = call(
        functools.partial(early_kernel, kept, ahead),
        chunks_f32,
        [IN_VMEM] * (5 * ahead + 3),
        1000,
    )(
        *[member for members in gathered for member in members[:ahead]],
        *close_rows, *close, *weights,
    )
    across, across_rows, early = lax.optimization_barrier((across, across_rows, early))
    distant_rows = in_group(across_rows, ahead // 2)
    distant = in_group(across, ahead // 2)
    late_ins = (
        early, *[member for members in gathered for member in members[ahead:]],
        *distant_rows, *distant, *weights,
    )
    last_all = close + distant
    loss_rows = call(
        loss_kernel, jax.ShapeDtypeStruct((1, nodes), F32), [IN_VMEM] * shuf, 1000
    )(*last_all).reshape(nodes)

    outs = [
        jax.ShapeDtypeStruct((branches, width, own), F32),
        jax.ShapeDtypeStruct((classes, own_class), F32),
    ]
    if chunks == dom and dom % 2 == 0 and dom & (dom - 1) == 0:
        half = dom // 2
        one_f32 = jax.ShapeDtypeStruct((height, LANES), F32)
        made = call(
            functools.partial(late_kernel, kept, ahead, half),
            [one_f32] * half + [jax.ShapeDtypeStruct((height, LANES), BF16)] * half,
            [IN_VMEM] * len(late_ins),
            grad_flops,
            [pltpu.VMEM(chunks_f32.shape, F32)],
        )(*late_ins)
        order = list(range(half - 1, -1, -1))
        arrived = {step: swapped(made[half + step], 1) for step in order}
        total = {step: made[step] + arrived[step].astype(F32) for step in order}
        far = {step: swapped(total[step].astype(BF16), 2 * step) for step in order[:-1]}
        summed = total[0]
        for step in order[:-1]:
            summed = lax.optimization_barrier(summed + far[step].astype(F32))
        near = [summed.astype(BF16)]
        near += [swapped(near[0], 2 * step) for step in range(1, half)]
        other = [swapped(value, 1) for value in near]
        results = []
        places = [2 * step for step in range(half)] + [2 * step + 1 for step in range(half)]
        for part in (slice(0, -half // 2), slice(-half // 2, None)):
            results = write_out(kept, places[part], (near + other)[part], outs, results)
        grad_branch, grad_class_t = results
    else:
        grads = call(
            functools.partial(plain_late_kernel, kept, ahead),
            chunks_f32,
            [IN_VMEM] * len(late_ins),
            grad_flops,
        )(*late_ins)
        grad_branch, grad_class_t = call(
            functools.partial(plain_out_kernel, kept), outs, [IN_VMEM], 1000
        )(lax.psum(grads, "dom"))
    return (loss_rows, grad_branch, grad_class_t.T)


def solution(mesh):
    return jax.shard_map(
        body,
        mesh=mesh,
        in_specs=(
            P(("dom", "shuf"), None),
            P(("dom", "shuf"), None, None),
            P(("dom", "shuf")),
            P(("dom", "shuf")),
            P(("dom", "shuf")),
            P(("dom", "shuf")),
            P(("dom", "shuf")),
            P(("dom", "shuf"), None),
            P(("dom", "shuf"), None),
            P(("dom", "shuf")),
            P(),
            P(),
        ),
        out_specs=(P(("dom", "shuf")), P(None, None, "shuf"), P("shuf", None)),
        check_vma=False,
    )
```

```python
import functools
import math

import jax
import jax.numpy as jnp
from jax import lax
from jax.experimental import pallas as pl
from jax.experimental.pallas import tpu as pltpu
from jax.sharding import PartitionSpec as P

HOPS = 3
LANES = 128
VMEM_LIMIT = 24 * 1024 * 1024
VMEM_ALL = 56 * 1024 * 1024

IN_VMEM = pl.BlockSpec(memory_space=pltpu.VMEM)
IN_SMEM = pl.BlockSpec(memory_space=pltpu.SMEM)
ANYWHERE = pl.BlockSpec(memory_space=pl.ANY)
BF16 = jnp.bfloat16
F32 = jnp.float32


def up_to(value, multiple):
    return -(-value // multiple) * multiple


def passed_along(value, axis, steps):
    count = lax.axis_size(axis)
    pairs = [(source, (source + steps) % count) for source in range(count)]
    return lax.ppermute(value, axis, pairs)


def swapped(value, distance, axis="dom"):
    pairs = [(source, source ^ distance) for source in range(lax.axis_size(axis))]
    return lax.ppermute(value, axis, pairs)


def matmul(left, right, dims=((1,), (0,)), precision=None):
    return lax.dot_general(
        left, right, (dims, ((), ())), precision=precision, preferred_element_type=F32
    )


def call(kernel, out_shape, in_specs, flops, scratch=(), after=(), limit=VMEM_LIMIT):
    many = isinstance(out_shape, (list, tuple))
    outs = out_shape if many else [out_shape]
    moved = sum(math.prod(one.shape) * one.dtype.itemsize for one in outs)
    waited = len(after)

    def run(*refs):
        kernel(*refs[waited:])

    made = pl.pallas_call(
        run,
        out_shape=out_shape,
        in_specs=[ANYWHERE] * waited + in_specs,
        out_specs=[IN_VMEM] * len(outs) if many else IN_VMEM,
        scratch_shapes=list(scratch),
        compiler_params=pltpu.CompilerParams(vmem_limit_bytes=limit),
        cost_estimate=pl.CostEstimate(
            flops=flops, bytes_accessed=3 * moved if flops > 1000 else 1000, transcendentals=0
        ),
    )
    return functools.partial(made, *after)


class Plan:
    def __init__(self, tiles, slots):
        self.tiles = tiles
        self.slots = slots
        self.dst = 0
        self.src = tiles
        self.count = 2 * tiles
        self.left = 2 * tiles + 1
        self.right = self.left + slots
        self.sent = self.right + slots


def write_sends(blocks, left_ref, right_ref, ids, counts):
    for slot in range(left_ref.shape[0]):
        for side, out_ref in enumerate((left_ref, right_ref)):
            index = ids(side, slot)
            picked = blocks[0]
            for number in range(1, len(blocks)):
                picked = jnp.where(index == number, blocks[number], picked)
            out_ref[slot] = jnp.where(slot < counts(side), picked, 0.0)


def copied(sources, targets, sems):
    copies = [
        pltpu.make_async_copy(source, target, sems.at[number])
        for number, (source, target) in enumerate(zip(sources, targets))
    ]
    for copy in copies:
        copy.start()
    for copy in copies:
        copy.wait()


def first_kernel(
    sl_ref, sr_ref, sc_ref, feat_ref, label_from,
    left_ref, right_ref, held_ref, b_ref,
    sl_here, sr_here, sc_here, label_ref, sems,
):
    copied(
        (sl_ref, sr_ref, sc_ref, feat_ref, label_from),
        (sl_here, sr_here, sc_here, held_ref, label_ref),
        sems,
    )
    blocks = [held_ref[number] for number in range(held_ref.shape[0])]
    write_sends(
        blocks,
        left_ref,
        right_ref,
        lambda side, slot: (sl_here, sr_here)[side][slot],
        lambda side: sc_here[0, side],
    )
    write_rows(blocks, b_ref)
    nodes = label_ref.shape[1]
    width = b_ref.shape[1]
    per_piece = nodes // width
    place = lax.broadcasted_iota(jnp.int32, (16, width), 0)
    packed = jnp.zeros((16, width), F32)
    for piece in range(2):
        value = label_ref[...] & 255 if piece == 0 else label_ref[...] >> 8
        value = value.astype(F32)
        for part in range(per_piece):
            packed = jnp.where(
                place == piece * per_piece + part,
                value[:, part * width : (part + 1) * width],
                packed,
            )
    b_ref[nodes:] = packed.astype(BF16)


def write_rows(blocks, b_ref):
    for number, block in enumerate(blocks):
        size = block.shape[0]
        b_ref[number * size : (number + 1) * size] = block.astype(BF16)


def next_blocks(plan, plan_ref, cur_ref, tiles_ref, ext_ref):
    local = cur_ref.shape[0]
    ext_ref[:local] = cur_ref[...]
    totals = [jnp.zeros(cur_ref.shape[1:], F32) for _ in range(local)]
    live = plan_ref[plan.count]
    for tile in range(plan.tiles):
        product = matmul(
            tiles_ref[tile],
            ext_ref[plan_ref[plan.src + tile]],
            precision=lax.Precision.HIGHEST,
        )
        wanted = jnp.where(tile < live, plan_ref[plan.dst + tile], -1)
        for number in range(local):
            totals[number] = totals[number] + jnp.where(wanted == number, product, 0.0)
    return totals


def extend(cur_ref, low_ref, high_ref, ext_ref):
    local = cur_ref.shape[0]
    slots = low_ref.shape[0]
    ext_ref[local : local + slots] = low_ref[...]
    ext_ref[local + slots :] = high_ref[...]


def hop_kernel(
    plan, plan_ref, cur_ref, low_ref, high_ref, tiles_ref, next_ref, left_ref, right_ref, *refs
):
    ext_ref = refs[-1]
    extend(cur_ref, low_ref, high_ref, ext_ref)
    blocks = next_blocks(plan, plan_ref, cur_ref, tiles_ref, ext_ref)
    write_sends(
        blocks,
        left_ref,
        right_ref,
        lambda side, slot: plan_ref[(plan.left, plan.right)[side] + slot],
        lambda side: plan_ref[plan.sent + side],
    )
    for number, block in enumerate(blocks):
        next_ref[number] = block
    for b_ref in refs[:-1]:
        write_rows(blocks, b_ref)


def ready_kernel(cur_ref, tiles_ref, wc_ref, cur_out, tiles_out, wc_out):
    cur_out[...] = cur_ref[...]
    tiles_out[...] = tiles_ref[...]
    wc_out[...] = wc_ref[...]


def branch_logits(branch, rows, w_ref, wc_ref):
    hidden = jnp.maximum(matmul(rows, w_ref[branch]), 0.0).astype(BF16)
    hid = hidden.shape[1]
    return matmul(wc_ref[:, branch * hid : (branch + 1) * hid], hidden, ((1,), (1,)))


def forward_kernel(branch, cur_ref, w_ref, wc_ref, *refs):
    rows = cur_ref[...].reshape(-1, cur_ref.shape[2]).astype(BF16)
    part = branch_logits(branch, rows, w_ref, wc_ref)
    if len(refs) == 2:
        part = refs[0][...] + part
    refs[-1][...] = part


def places(order_ref):
    nodes = order_ref.shape[1]
    rows = lax.broadcasted_iota(jnp.int32, (nodes, nodes), 0)
    return (order_ref[...] == rows).astype(F32).astype(BF16)


def wanted_places(nodes, group, step, offset, count):
    share = nodes // group
    mine = lax.axis_index("shuf")
    first = mine * share
    source = lax.broadcasted_iota(jnp.int32, (count, nodes), 0) + offset
    target = lax.broadcasted_iota(jnp.int32, (count, nodes), 1)
    moved = source + ((mine ^ step) - mine) * share
    wanted = (target == moved) & (source >= first) & (source < first + share)
    return wanted.astype(F32).astype(BF16)


def label_kernel(order_ref, *refs):
    nodes = order_ref.shape[1]
    group = len(refs) - 1
    width = refs[0].shape[1]
    per_piece = nodes // width
    ordered = [jnp.zeros((1, nodes), F32) for _ in range(2)]
    for step in range(group):
        tail = refs[step][nodes:]
        for part in range(per_piece):
            moved = matmul(tail, wanted_places(nodes, group, step, part * width, width))
            for piece in range(2):
                row = piece * per_piece + part
                ordered[piece] = ordered[piece] + moved[row : row + 1]
    number = lax.broadcasted_iota(jnp.int32, (16, nodes), 0)
    packed = jnp.where(number == 0, ordered[0], jnp.where(number == 1, ordered[1], 0.0))
    pieces = matmul(packed.astype(BF16), places(order_ref), ((1,), (1,)))
    refs[-1][...] = (pieces[0:1] + 256.0 * pieces[1:2]).astype(jnp.int32)


def loss_kernel(*refs):
    group = len(refs) - 1
    height, nodes = refs[0].shape
    total = jnp.zeros((16, nodes), F32)
    for step in range(group):
        wanted = wanted_places(nodes, group, step, 0, nodes)
        total = total + matmul(refs[step][height - 16 :], wanted)
    refs[-1][...] = total[0:1] + total[1:2] + total[2:3]


def last_hop_kernel(plan, plan_ref, cur_ref, low_ref, high_ref, tiles_ref, out_ref, ext_ref):
    extend(cur_ref, low_ref, high_ref, ext_ref)
    blocks = next_blocks(plan, plan_ref, cur_ref, tiles_ref, ext_ref)
    for number, block in enumerate(blocks):
        width = block.shape[1]
        columns = slice(number * width, (number + 1) * width)
        out_ref[:, columns] = block.astype(BF16)


def stacked(ref, width):
    parts = ref.shape[1] // width
    return [ref[:, part * width : (part + 1) * width] for part in range(parts)]


def loss_and_gradient_kernel(
    row_scale, rows_ref, before_ref, w_ref, wc_ref, order_ref, label_ref, out_ref
):
    rows_b = jnp.concatenate(stacked(rows_ref, w_ref.shape[1]), axis=0)
    logits = before_ref[...] + branch_logits(w_ref.shape[0] - 1, rows_b, w_ref, wc_ref)
    classes, rows = logits.shape
    kept = up_to(classes, 16)
    hit = lax.broadcasted_iota(jnp.int32, (classes, rows), 0) == label_ref[...]
    top = jnp.max(logits, axis=0, keepdims=True)
    log_total = top + jnp.log(jnp.sum(jnp.exp(logits - top), axis=0, keepdims=True))
    loss = log_total - jnp.sum(jnp.where(hit, logits, 0.0), axis=0, keepdims=True)
    dlogits = (jnp.exp(logits - log_total) - jnp.where(hit, 1.0, 0.0)) * row_scale
    out_ref[kept - 16 : kept] = jnp.zeros((16, rows), BF16)
    out_ref[:classes] = dlogits.astype(BF16)
    number = lax.broadcasted_iota(jnp.int32, (16, rows), 0)
    packed = jnp.zeros((16, rows), F32)
    rest = loss
    for piece in range(3):
        part = rest.astype(BF16).astype(F32)
        packed = jnp.where(number == piece, part, packed)
        rest = rest - part
    out_ref[kept:] = matmul(packed.astype(BF16), places(order_ref)).astype(BF16)


def weights_kernel(w_ref, wc_ref, wt_ref, wct_ref, pad_ref):
    branches, own, kept = wct_ref.shape
    classes = wc_ref.shape[0]
    hid = w_ref.shape[2]
    first = lax.axis_index("shuf") * own
    pad_ref[...] = jnp.zeros_like(pad_ref)
    for branch in range(branches):
        columns = w_ref[branch, :, pl.ds(pl.multiple_of(first, LANES), own)]
        wt_ref[branch] = columns.astype(F32).T.astype(BF16)
        columns = wc_ref[:, pl.ds(pl.multiple_of(branch * hid + first, LANES), own)]
        pad_ref[:classes] = columns.astype(F32)
        wct_ref[branch] = pad_ref[...].T[:, :kept].astype(BF16)


def add_chunks(kept, before_ref, row_refs, last_refs, dlogit_refs, w_ref, wt_ref, wct_ref, chunks_ref):
    members = len(last_refs)
    branches, own, width = wt_ref.shape
    nodes = last_refs[0].shape[1]
    hid = w_ref.shape[2]
    all_rows = []
    for branch in range(branches - 1):
        ours = row_refs[branch * members : (branch + 1) * members]
        all_rows.append(jnp.concatenate([ref[:nodes] for ref in ours], axis=0))
    ours = [rows for ref in last_refs for rows in stacked(ref, width)]
    all_rows.append(jnp.concatenate(ours, axis=0))
    dlogits_t = jnp.concatenate([ref[:kept] for ref in dlogit_refs], axis=1)
    own_class = branches * own
    first = lax.axis_index("shuf") * own_class
    which = first // hid
    columns = pl.ds(pl.multiple_of(first - which * hid, LANES), own_class)
    chosen = all_rows[0]
    for branch in range(1, branches):
        chosen = jnp.where(which == branch, all_rows[branch], chosen)

    def put(chunk, rows, value):
        chunks_ref[chunk, rows] = value if before_ref is None else before_ref[chunk, rows] + value

    hidden = jnp.maximum(matmul(chosen, w_ref[which, :, columns]), 0.0).astype(BF16)
    class_t = matmul(dlogits_t, hidden)
    for chunk in range(chunks_ref.shape[0]):
        put(chunk, slice(0, kept), class_t[:, chunk * LANES : (chunk + 1) * LANES])
    per_branch = chunks_ref.shape[0] // branches
    for branch, rows in enumerate(all_rows):
        live = matmul(wt_ref[branch], rows, ((1,), (1,))) > 0.0
        dhidden_t = jnp.where(live, matmul(wct_ref[branch], dlogits_t), 0.0).astype(BF16)
        branch_t = matmul(dhidden_t, rows)
        for part in range(per_branch):
            put(
                branch * per_branch + part,
                slice(kept, kept + width),
                branch_t[part * LANES : (part + 1) * LANES],
            )


def split_refs(members, refs):
    last = len(refs) - 3 - 2 * members
    return (
        refs[:last], refs[last : last + members], refs[last + members : last + 2 * members],
        *refs[last + 2 * members :],
    )


def early_kernel(kept, members, *refs):
    add_chunks(kept, None, *split_refs(members, refs[:-1]), refs[-1])


def late_chunks(kept, members, early_ref, refs, chunks_ref):
    add_chunks(kept, early_ref, *split_refs(members, refs), chunks_ref)


def late_kernel(kept, members, half, early_ref, *refs):
    ins = len(refs) - 2 * half
    outs = refs[ins:-1]
    chunks_ref = refs[-1]
    late_chunks(kept, members, early_ref, refs[:ins], chunks_ref)
    dom = lax.axis_index("dom")
    for step in range(half):
        stays = dom ^ (2 * step)
        outs[step][...] = chunks_ref[stays]
        going = chunks_ref[stays ^ 1].astype(BF16)
        if step < 2:
            outs[half][step] = going
        else:
            outs[half + step - 1][...] = going


def plain_late_kernel(kept, members, early_ref, *refs):
    late_chunks(kept, members, early_ref, refs[:-1], refs[-1])


def write_chunk(kept, chunk, value, branch_ref, class_ref):
    per_branch = branch_ref.shape[2] // LANES
    start = pl.multiple_of(chunk * LANES, LANES)
    class_ref[:, pl.ds(start, LANES)] = value[: class_ref.shape[0]]
    branch = chunk // per_branch
    start = pl.multiple_of((chunk - branch * per_branch) * LANES, LANES)
    branch_ref[branch, :, pl.ds(start, LANES)] = value[kept:].T


def out_kernel(kept, distances, count, *refs):
    values = []
    for ref in refs[-5 - count : -5]:
        values += [ref[...]] if len(ref.shape) == 2 else [ref[n] for n in range(ref.shape[0])]
    branch_ref, class_ref, branch_here, class_here, sems = refs[-5:]
    dom = lax.axis_index("dom")
    per_branch = branch_ref.shape[2] // LANES
    copies = []
    for number, distance in enumerate(distances):
        chunk = dom ^ distance
        value = values[number].astype(F32)
        class_here[number] = value[: class_ref.shape[0]]
        start = pl.multiple_of(chunk * LANES, LANES)
        copies.append(
            pltpu.make_async_copy(
                class_here.at[number], class_ref.at[:, pl.ds(start, LANES)], sems.at[2 * number]
            )
        )
        copies[-1].start()
        branch_here[number] = value[kept:].T
        branch = chunk // per_branch
        start = pl.multiple_of((chunk - branch * per_branch) * LANES, LANES)
        copies.append(
            pltpu.make_async_copy(
                branch_here.at[number],
                branch_ref.at[branch, :, pl.ds(start, LANES)],
                sems.at[2 * number + 1],
            )
        )
        copies[-1].start()
    for copy in copies:
        copy.wait()


def write_out(kept, distances, values, outs, before):
    count = len(distances)
    return pl.pallas_call(
        functools.partial(out_kernel, kept, distances, len(values)),
        out_shape=outs,
        in_specs=[ANYWHERE] * len(before) + [IN_VMEM] * len(values),
        out_specs=[pl.BlockSpec(memory_space=pltpu.HBM)] * 2,
        scratch_shapes=[
            pltpu.VMEM((count, outs[0].shape[1], LANES), F32),
            pltpu.VMEM((count, outs[1].shape[0], LANES), F32),
            pltpu.SemaphoreType.DMA((2 * count,)),
        ],
        input_output_aliases={0: 0, 1: 1} if before else {},
        compiler_params=pltpu.CompilerParams(vmem_limit_bytes=VMEM_LIMIT),
        cost_estimate=pl.CostEstimate(flops=1000, bytes_accessed=1000, transcendentals=0),
    )(*before, *values)


def plain_out_kernel(kept, in_ref, branch_ref, class_ref):
    for chunk in range(in_ref.shape[0]):
        write_chunk(kept, chunk, in_ref[chunk], branch_ref, class_ref)


def in_group(value, distance=None):
    members = [value]
    steps = [0]
    distance = lax.axis_size("shuf") // 2 if distance is None else distance
    while distance:
        members += [swapped(member, distance, "shuf") for member in members]
        steps += [step + distance for step in steps]
        distance //= 2
    return [members[steps.index(step)] for step in range(len(steps))]


def body(
    features, tile_values, tile_dst, tile_src, tile_count, send_left, send_right,
    send_count, batch_order, labels, w_branch, w_class,
):
    block = tile_values.shape[1]
    nodes, width = features.shape
    local = nodes // block
    slots = send_left.shape[0]
    tiles = tile_values.shape[0]
    branches, _, hid = w_branch.shape
    cat, classes = w_class.shape
    dom = lax.axis_size("dom")
    shuf = lax.axis_size("shuf")
    mine = lax.axis_index("shuf")
    share = nodes // shuf
    own = hid // shuf
    own_class = cat // shuf
    kept = up_to(classes, 16)
    row_scale = 1.0 / math.sqrt(float(nodes * dom * shuf))
    plan = Plan(tiles, slots)
    small = jnp.concatenate(
        [tile_dst, tile_src, tile_count, send_left, send_right, send_count.reshape(-1)]
    )
    blocks_f32 = jax.ShapeDtypeStruct((local, block, width), F32)
    slots_f32 = jax.ShapeDtypeStruct((slots, block, width), F32)
    rows_b16 = jax.ShapeDtypeStruct((nodes, width), BF16)
    first_b16 = jax.ShapeDtypeStruct((nodes + 16, width), BF16)
    logits_f32 = jax.ShapeDtypeStruct((classes, nodes), F32)
    w_class_t = w_class.T

    current = features.reshape(local, block, width)
    gathered = []
    logits = None
    hop_flops = 12 * tiles * block * block * width
    forward_flops = 2 * nodes * hid * (width + classes)
    ext = pltpu.VMEM((local + 2 * slots, block, width), F32)
    to_left, to_right, current, *rows = call(
        first_kernel,
        [slots_f32, slots_f32, blocks_f32, first_b16],
        [ANYWHERE] * 5,
        1000,
        [
            pltpu.SMEM((slots,), jnp.int32),
            pltpu.SMEM((slots,), jnp.int32),
            pltpu.SMEM((1, 2), jnp.int32),
            pltpu.VMEM((1, nodes), jnp.int32),
            pltpu.SemaphoreType.DMA((5,)),
        ],
        limit=VMEM_ALL,
    )(send_left, send_right, send_count, current, labels.reshape(1, nodes))
    current, tile_values, w_class_t = call(
        ready_kernel,
        [
            blocks_f32,
            jax.ShapeDtypeStruct(tile_values.shape, F32),
            jax.ShapeDtypeStruct(w_class_t.shape, BF16),
        ],
        [IN_VMEM] * 3,
        1000,
    )(current, tile_values, w_class_t)
    for hop in range(HOPS):
        from_lower = passed_along(to_right, "dom", 1)
        from_upper = passed_along(to_left, "dom", -1)
        for value in rows:
            gathered.append(in_group(value))
        before = [] if logits is None else [logits]
        logits = call(
            functools.partial(forward_kernel, hop),
            logits_f32,
            [IN_VMEM] * (3 + len(before)),
            forward_flops,
            after=[members[shuf // 2] for members in gathered[:2]] if hop == HOPS - 1 else [],
        )(current, w_branch, w_class_t, *before)
        if hop == 0:
            after = []
        else:
            after = [logits]
        if hop < HOPS - 1:
            current, to_left, to_right, *rows = call(
                functools.partial(hop_kernel, plan),
                [blocks_f32, slots_f32, slots_f32, rows_b16],
                [IN_SMEM] + [IN_VMEM] * 4,
                hop_flops,
                [ext],
                after,
            )(small, current, from_lower, from_upper, tile_values)

    label_mine = call(
        label_kernel,
        jax.ShapeDtypeStruct((1, nodes), jnp.int32),
        [IN_VMEM] * (1 + shuf),
        1000,
    )(batch_order, *gathered[0])

    wt_own, wct_own = call(
        weights_kernel,
        [
            jax.ShapeDtypeStruct((branches, own, width), BF16),
            jax.ShapeDtypeStruct((branches, own, kept), BF16),
        ],
        [IN_VMEM] * 2,
        1000,
        [pltpu.VMEM((up_to(classes, LANES), own), F32)],
    )(w_branch, w_class_t)

    last_rows = call(
        functools.partial(last_hop_kernel, plan),
        jax.ShapeDtypeStruct((block, local * width), BF16),
        [IN_SMEM] + [IN_VMEM] * 4,
        hop_flops,
        [ext],
        [logits, label_mine, *gathered[1][1:]],
    )(small, current, from_lower, from_upper, tile_values)
    dlogits = call(
        functools.partial(loss_and_gradient_kernel, row_scale),
        jax.ShapeDtypeStruct((kept + 16, nodes), BF16),
        [IN_VMEM] * 6,
        1000,
        after=[gathered[2][shuf // 2]],
    )(last_rows, logits, w_branch, w_class_t, batch_order, label_mine)
    chunks = own_class // LANES
    height = kept + width
    ahead = shuf // 2
    chunks_f32 = jax.ShapeDtypeStruct((chunks, height, LANES), F32)
    grad_flops = shuf * nodes * own_class * (3 * width + 2 * kept)
    weights = (w_branch, wt_own, wct_own)
    across_rows = swapped(last_rows, ahead, "shuf")
    across = swapped(dlogits, ahead, "shuf")
    close_rows = in_group(last_rows, ahead // 2)
    close = in_group(dlogits, ahead // 2)
    early = call(
        functools.partial(early_kernel, kept, ahead),
        chunks_f32,
        [IN_VMEM] * (5 * ahead + 3),
        1000,
    )(
        *[member for members in gathered for member in members[:ahead]],
        *close_rows, *close, *weights,
    )
    across, across_rows, early = lax.optimization_barrier((across, across_rows, early))
    distant_rows = in_group(across_rows, ahead // 2)
    distant = in_group(across, ahead // 2)
    late_ins = (
        early, *[member for members in gathered for member in members[ahead:]],
        *distant_rows, *distant, *weights,
    )
    last_all = close + distant
    loss_rows = call(
        loss_kernel, jax.ShapeDtypeStruct((1, nodes), F32), [IN_VMEM] * shuf, 1000
    )(*last_all).reshape(nodes)

    outs = [
        jax.ShapeDtypeStruct((branches, width, own), F32),
        jax.ShapeDtypeStruct((classes, own_class), F32),
    ]
    if chunks == dom and dom % 8 == 0 and dom & (dom - 1) == 0:
        half = dom // 2
        one_f32 = jax.ShapeDtypeStruct((height, LANES), F32)
        made = call(
            functools.partial(late_kernel, kept, ahead, half),
            [one_f32] * half
            + [jax.ShapeDtypeStruct((2, height, LANES), BF16)]
            + [jax.ShapeDtypeStruct((height, LANES), BF16)] * (half - 2),
            [IN_VMEM] * len(late_ins),
            grad_flops,
            [pltpu.VMEM(chunks_f32.shape, F32)],
        )(*late_ins)
        order = list(range(half - 1, -1, -1))
        arrived = {step: swapped(made[half + step - 1], 1) for step in order if step > 1}
        together = swapped(made[half], 1)
        arrived |= {step: together[step] for step in range(2)}
        total = {step: made[step] + arrived[step].astype(F32) for step in order}
        far = {step: swapped(total[step].astype(BF16), 2 * step) for step in order[:-1]}
        summed = total[0]
        for step in order[:-1]:
            summed = lax.optimization_barrier(summed + far[step].astype(F32))
        near = [summed.astype(BF16)]
        near += [swapped(near[0], 2 * step) for step in range(1, half)]
        other = [swapped(value, 1) for value in near]
        results = []
        places = [2 * step for step in range(half)] + [2 * step + 1 for step in range(half)]
        for values, part in (
            (near + other[: half // 2], slice(0, half + half // 2)),
            (other[half // 2 :], slice(half + half // 2, None)),
        ):
            results = write_out(kept, places[part], values, outs, results)
        grad_branch, grad_class_t = results
    else:
        grads = call(
            functools.partial(plain_late_kernel, kept, ahead),
            chunks_f32,
            [IN_VMEM] * len(late_ins),
            grad_flops,
        )(*late_ins)
        grad_branch, grad_class_t = call(
            functools.partial(plain_out_kernel, kept), outs, [IN_VMEM], 1000
        )(lax.psum(grads, "dom"))
    return (loss_rows, grad_branch, grad_class_t.T)


def solution(mesh):
    return jax.shard_map(
        body,
        mesh=mesh,
        in_specs=(
            P(("dom", "shuf"), None),
            P(("dom", "shuf"), None, None),
            P(("dom", "shuf")),
            P(("dom", "shuf")),
            P(("dom", "shuf")),
            P(("dom", "shuf")),
            P(("dom", "shuf")),
            P(("dom", "shuf"), None),
            P(("dom", "shuf"), None),
            P(("dom", "shuf")),
            P(),
            P(),
        ),
        out_specs=(P(("dom", "shuf")), P(None, None, "shuf"), P("shuf", None)),
        check_vma=False,
    )
```

```python
import functools
import math

import jax
import jax.numpy as jnp
from jax import lax
from jax.experimental import pallas as pl
from jax.experimental.pallas import tpu as pltpu
from jax.sharding import PartitionSpec as P

HOPS = 3
LANES = 128
VMEM_LIMIT = 24 * 1024 * 1024
VMEM_ALL = 56 * 1024 * 1024

IN_VMEM = pl.BlockSpec(memory_space=pltpu.VMEM)
IN_SMEM = pl.BlockSpec(memory_space=pltpu.SMEM)
ANYWHERE = pl.BlockSpec(memory_space=pl.ANY)
BF16 = jnp.bfloat16
F32 = jnp.float32


def up_to(value, multiple):
    return -(-value // multiple) * multiple


def exchanged(to_wrap, to_right, to_left):
    last = lax.axis_size("dom") - 1
    return (
        lax.ppermute(to_wrap, "dom", [(0, last), (last, 0)]),
        lax.ppermute(to_right, "dom", [(d, d + 1) for d in range(last)]),
        lax.ppermute(to_left, "dom", [(d + 1, d) for d in range(last)]),
    )


def swapped(value, distance, axis="dom"):
    pairs = [(source, source ^ distance) for source in range(lax.axis_size(axis))]
    return lax.ppermute(value, axis, pairs)


def matmul(left, right, dims=((1,), (0,)), precision=None):
    return lax.dot_general(
        left, right, (dims, ((), ())), precision=precision, preferred_element_type=F32
    )


def call(kernel, out_shape, in_specs, flops, scratch=(), after=(), limit=VMEM_LIMIT):
    many = isinstance(out_shape, (list, tuple))
    outs = out_shape if many else [out_shape]
    moved = sum(math.prod(one.shape) * one.dtype.itemsize for one in outs)
    waited = len(after)

    def run(*refs):
        kernel(*refs[waited:])

    made = pl.pallas_call(
        run,
        out_shape=out_shape,
        in_specs=[ANYWHERE] * waited + in_specs,
        out_specs=[IN_VMEM] * len(outs) if many else IN_VMEM,
        scratch_shapes=list(scratch),
        compiler_params=pltpu.CompilerParams(vmem_limit_bytes=limit),
        cost_estimate=pl.CostEstimate(
            flops=flops, bytes_accessed=3 * moved if flops > 1000 else 1000, transcendentals=0
        ),
    )
    return functools.partial(made, *after)


class Plan:
    def __init__(self, tiles, slots):
        self.tiles = tiles
        self.slots = slots
        self.dst = 0
        self.src = tiles
        self.count = 2 * tiles
        self.left = 2 * tiles + 1
        self.right = self.left + slots
        self.sent = self.right + slots


def write_sends(blocks, left_ref, right_ref, wrap_ref, ids, counts):
    start = lax.axis_index("dom") == 0
    for slot in range(left_ref.shape[0]):
        values = []
        for side, out_ref in enumerate((left_ref, right_ref)):
            index = ids(side, slot)
            picked = blocks[0]
            for number in range(1, len(blocks)):
                picked = jnp.where(index == number, blocks[number], picked)
            values.append(jnp.where(slot < counts(side), picked, 0.0))
            out_ref[slot] = values[-1]
        wrap_ref[slot] = jnp.where(start, values[0], values[1])


def copied(sources, targets, sems):
    copies = [
        pltpu.make_async_copy(source, target, sems.at[number])
        for number, (source, target) in enumerate(zip(sources, targets))
    ]
    for copy in copies:
        copy.start()
    for copy in copies:
        copy.wait()


def first_kernel(
    sl_ref, sr_ref, sc_ref, feat_ref, label_from,
    left_ref, right_ref, wrap_ref, held_ref, b_ref,
    sl_here, sr_here, sc_here, label_ref, sems,
):
    copied(
        (sl_ref, sr_ref, sc_ref, feat_ref, label_from),
        (sl_here, sr_here, sc_here, held_ref, label_ref),
        sems,
    )
    blocks = [held_ref[number] for number in range(held_ref.shape[0])]
    write_sends(
        blocks,
        left_ref,
        right_ref,
        wrap_ref,
        lambda side, slot: (sl_here, sr_here)[side][slot],
        lambda side: sc_here[0, side],
    )
    write_rows(blocks, b_ref)
    nodes = label_ref.shape[1]
    width = b_ref.shape[1]
    per_piece = nodes // width
    place = lax.broadcasted_iota(jnp.int32, (16, width), 0)
    packed = jnp.zeros((16, width), F32)
    for piece in range(2):
        value = label_ref[...] & 255 if piece == 0 else label_ref[...] >> 8
        value = value.astype(F32)
        for part in range(per_piece):
            packed = jnp.where(
                place == piece * per_piece + part,
                value[:, part * width : (part + 1) * width],
                packed,
            )
    b_ref[nodes:] = packed.astype(BF16)


def write_rows(blocks, b_ref):
    for number, block in enumerate(blocks):
        size = block.shape[0]
        b_ref[number * size : (number + 1) * size] = block.astype(BF16)


def next_blocks(plan, plan_ref, cur_ref, tiles_ref, ext_ref):
    local = cur_ref.shape[0]
    ext_ref[:local] = cur_ref[...]
    totals = [jnp.zeros(cur_ref.shape[1:], F32) for _ in range(local)]
    live = plan_ref[plan.count]
    for tile in range(plan.tiles):
        product = matmul(
            tiles_ref[tile],
            ext_ref[plan_ref[plan.src + tile]],
            precision=lax.Precision.HIGHEST,
        )
        wanted = jnp.where(tile < live, plan_ref[plan.dst + tile], -1)
        for number in range(local):
            totals[number] = totals[number] + jnp.where(wanted == number, product, 0.0)
    return totals


def extend(cur_ref, wrap_ref, low_ref, high_ref, ext_ref):
    local = cur_ref.shape[0]
    slots = low_ref.shape[0]
    dom = lax.axis_index("dom")
    last = lax.axis_size("dom") - 1
    ext_ref[local : local + slots] = jnp.where(dom == 0, wrap_ref[...], low_ref[...])
    ext_ref[local + slots :] = jnp.where(dom == last, wrap_ref[...], high_ref[...])


def hop_kernel(
    plan, plan_ref, cur_ref, wrap_in_ref, low_ref, high_ref, tiles_ref,
    next_ref, left_ref, right_ref, wrap_ref, *refs
):
    ext_ref = refs[-1]
    extend(cur_ref, wrap_in_ref, low_ref, high_ref, ext_ref)
    blocks = next_blocks(plan, plan_ref, cur_ref, tiles_ref, ext_ref)
    write_sends(
        blocks,
        left_ref,
        right_ref,
        wrap_ref,
        lambda side, slot: plan_ref[(plan.left, plan.right)[side] + slot],
        lambda side: plan_ref[plan.sent + side],
    )
    for number, block in enumerate(blocks):
        next_ref[number] = block
    for b_ref in refs[:-1]:
        write_rows(blocks, b_ref)


def ready_kernel(cur_ref, tiles_ref, wc_ref, cur_out, tiles_out, wc_out):
    cur_out[...] = cur_ref[...]
    tiles_out[...] = tiles_ref[...]
    wc_out[...] = wc_ref[...]


def branch_logits(branch, rows, w_ref, wc_ref):
    hidden = jnp.maximum(matmul(rows, w_ref[branch]), 0.0).astype(BF16)
    hid = hidden.shape[1]
    return matmul(wc_ref[:, branch * hid : (branch + 1) * hid], hidden, ((1,), (1,)))


def forward_kernel(branch, cur_ref, w_ref, wc_ref, *refs):
    rows = cur_ref[...].reshape(-1, cur_ref.shape[2]).astype(BF16)
    part = branch_logits(branch, rows, w_ref, wc_ref)
    if len(refs) == 2:
        part = refs[0][...] + part
    refs[-1][...] = part


def places(order_ref):
    nodes = order_ref.shape[1]
    rows = lax.broadcasted_iota(jnp.int32, (nodes, nodes), 0)
    return (order_ref[...] == rows).astype(F32).astype(BF16)


def wanted_places(nodes, group, step, offset, count):
    share = nodes // group
    mine = lax.axis_index("shuf")
    first = mine * share
    source = lax.broadcasted_iota(jnp.int32, (count, nodes), 0) + offset
    target = lax.broadcasted_iota(jnp.int32, (count, nodes), 1)
    moved = source + ((mine ^ step) - mine) * share
    wanted = (target == moved) & (source >= first) & (source < first + share)
    return wanted.astype(F32).astype(BF16)


def label_kernel(order_ref, *refs):
    nodes = order_ref.shape[1]
    group = len(refs) - 1
    width = refs[0].shape[1]
    per_piece = nodes // width
    ordered = [jnp.zeros((1, nodes), F32) for _ in range(2)]
    for step in range(group):
        tail = refs[step][nodes:]
        for part in range(per_piece):
            moved = matmul(tail, wanted_places(nodes, group, step, part * width, width))
            for piece in range(2):
                row = piece * per_piece + part
                ordered[piece] = ordered[piece] + moved[row : row + 1]
    number = lax.broadcasted_iota(jnp.int32, (16, nodes), 0)
    packed = jnp.where(number == 0, ordered[0], jnp.where(number == 1, ordered[1], 0.0))
    pieces = matmul(packed.astype(BF16), places(order_ref), ((1,), (1,)))
    refs[-1][...] = (pieces[0:1] + 256.0 * pieces[1:2]).astype(jnp.int32)


def loss_kernel(*refs):
    group = len(refs) - 1
    height, nodes = refs[0].shape
    total = jnp.zeros((16, nodes), F32)
    for step in range(group):
        wanted = wanted_places(nodes, group, step, 0, nodes)
        total = total + matmul(refs[step][height - 16 :], wanted)
    refs[-1][...] = total[0:1] + total[1:2] + total[2:3]


def last_hop_kernel(
    plan, plan_ref, cur_ref, wrap_ref, low_ref, high_ref, tiles_ref, out_ref, ext_ref
):
    extend(cur_ref, wrap_ref, low_ref, high_ref, ext_ref)
    blocks = next_blocks(plan, plan_ref, cur_ref, tiles_ref, ext_ref)
    for number, block in enumerate(blocks):
        width = block.shape[1]
        columns = slice(number * width, (number + 1) * width)
        out_ref[:, columns] = block.astype(BF16)


def stacked(ref, width):
    parts = ref.shape[1] // width
    return [ref[:, part * width : (part + 1) * width] for part in range(parts)]


def loss_and_gradient_kernel(
    row_scale, rows_ref, before_ref, w_ref, wc_ref, order_ref, label_ref, out_ref
):
    rows_b = jnp.concatenate(stacked(rows_ref, w_ref.shape[1]), axis=0)
    logits = before_ref[...] + branch_logits(w_ref.shape[0] - 1, rows_b, w_ref, wc_ref)
    classes, rows = logits.shape
    kept = up_to(classes, 16)
    hit = lax.broadcasted_iota(jnp.int32, (classes, rows), 0) == label_ref[...]
    top = jnp.max(logits, axis=0, keepdims=True)
    log_total = top + jnp.log(jnp.sum(jnp.exp(logits - top), axis=0, keepdims=True))
    loss = log_total - jnp.sum(jnp.where(hit, logits, 0.0), axis=0, keepdims=True)
    dlogits = (jnp.exp(logits - log_total) - jnp.where(hit, 1.0, 0.0)) * row_scale
    out_ref[kept - 16 : kept] = jnp.zeros((16, rows), BF16)
    out_ref[:classes] = dlogits.astype(BF16)
    number = lax.broadcasted_iota(jnp.int32, (16, rows), 0)
    packed = jnp.zeros((16, rows), F32)
    rest = loss
    for piece in range(3):
        part = rest.astype(BF16).astype(F32)
        packed = jnp.where(number == piece, part, packed)
        rest = rest - part
    out_ref[kept:] = matmul(packed.astype(BF16), places(order_ref)).astype(BF16)


def weights_kernel(w_ref, wc_ref, wt_ref, wct_ref, pad_ref):
    branches, own, kept = wct_ref.shape
    classes = wc_ref.shape[0]
    hid = w_ref.shape[2]
    first = lax.axis_index("shuf") * own
    pad_ref[...] = jnp.zeros_like(pad_ref)
    for branch in range(branches):
        columns = w_ref[branch, :, pl.ds(pl.multiple_of(first, LANES), own)]
        wt_ref[branch] = columns.astype(F32).T.astype(BF16)
        columns = wc_ref[:, pl.ds(pl.multiple_of(branch * hid + first, LANES), own)]
        pad_ref[:classes] = columns.astype(F32)
        wct_ref[branch] = pad_ref[...].T[:, :kept].astype(BF16)


def add_chunks(kept, before_ref, row_refs, last_refs, dlogit_refs, w_ref, wt_ref, wct_ref, chunks_ref):
    members = len(last_refs)
    branches, own, width = wt_ref.shape
    nodes = last_refs[0].shape[1]
    hid = w_ref.shape[2]
    all_rows = []
    for branch in range(branches - 1):
        ours = row_refs[branch * members : (branch + 1) * members]
        all_rows.append(jnp.concatenate([ref[:nodes] for ref in ours], axis=0))
    ours = [rows for ref in last_refs for rows in stacked(ref, width)]
    all_rows.append(jnp.concatenate(ours, axis=0))
    dlogits_t = jnp.concatenate([ref[:kept] for ref in dlogit_refs], axis=1)
    own_class = branches * own
    first = lax.axis_index("shuf") * own_class
    which = first // hid
    columns = pl.ds(pl.multiple_of(first - which * hid, LANES), own_class)
    chosen = all_rows[0]
    for branch in range(1, branches):
        chosen = jnp.where(which == branch, all_rows[branch], chosen)

    def put(chunk, rows, value):
        chunks_ref[chunk, rows] = value if before_ref is None else before_ref[chunk, rows] + value

    hidden = jnp.maximum(matmul(chosen, w_ref[which, :, columns]), 0.0).astype(BF16)
    class_t = matmul(dlogits_t, hidden)
    for chunk in range(chunks_ref.shape[0]):
        put(chunk, slice(0, kept), class_t[:, chunk * LANES : (chunk + 1) * LANES])
    per_branch = chunks_ref.shape[0] // branches
    for branch, rows in enumerate(all_rows):
        live = matmul(wt_ref[branch], rows, ((1,), (1,))) > 0.0
        dhidden_t = jnp.where(live, matmul(wct_ref[branch], dlogits_t), 0.0).astype(BF16)
        branch_t = matmul(dhidden_t, rows)
        for part in range(per_branch):
            put(
                branch * per_branch + part,
                slice(kept, kept + width),
                branch_t[part * LANES : (part + 1) * LANES],
            )


def split_refs(members, refs):
    last = len(refs) - 3 - 2 * members
    return (
        refs[:last], refs[last : last + members], refs[last + members : last + 2 * members],
        *refs[last + 2 * members :],
    )


def early_kernel(kept, members, *refs):
    add_chunks(kept, None, *split_refs(members, refs[:-1]), refs[-1])


def late_chunks(kept, members, early_ref, refs, chunks_ref):
    add_chunks(kept, early_ref, *split_refs(members, refs), chunks_ref)


def late_kernel(kept, members, half, early_ref, *refs):
    ins = len(refs) - 1 - 2 * half
    outs = refs[ins:-1]
    chunks_ref = refs[-1]
    late_chunks(kept, members, early_ref, refs[:ins], chunks_ref)
    dom = lax.axis_index("dom")
    for step in range(half):
        stays = dom ^ (2 * step)
        outs[step][...] = chunks_ref[stays]
        outs[half + step][...] = chunks_ref[stays ^ 1].astype(BF16)


def plain_late_kernel(kept, members, early_ref, *refs):
    late_chunks(kept, members, early_ref, refs[:-1], refs[-1])


def write_chunk(kept, chunk, value, branch_ref, class_ref):
    per_branch = branch_ref.shape[2] // LANES
    start = pl.multiple_of(chunk * LANES, LANES)
    class_ref[:, pl.ds(start, LANES)] = value[: class_ref.shape[0]]
    branch = chunk // per_branch
    start = pl.multiple_of((chunk - branch * per_branch) * LANES, LANES)
    branch_ref[branch, :, pl.ds(start, LANES)] = value[kept:].T


def out_kernel(kept, distances, *refs):
    count = len(distances)
    ins = refs[-5 - count : -5]
    branch_ref, class_ref, branch_here, class_here, sems = refs[-5:]
    dom = lax.axis_index("dom")
    per_branch = branch_ref.shape[2] // LANES
    copies = []
    for number, distance in enumerate(distances):
        chunk = dom ^ distance
        value = ins[number][...].astype(F32)
        class_here[number] = value[: class_ref.shape[0]]
        start = pl.multiple_of(chunk * LANES, LANES)
        copies.append(
            pltpu.make_async_copy(
                class_here.at[number], class_ref.at[:, pl.ds(start, LANES)], sems.at[2 * number]
            )
        )
        copies[-1].start()
        branch_here[number] = value[kept:].T
        branch = chunk // per_branch
        start = pl.multiple_of((chunk - branch * per_branch) * LANES, LANES)
        copies.append(
            pltpu.make_async_copy(
                branch_here.at[number],
                branch_ref.at[branch, :, pl.ds(start, LANES)],
                sems.at[2 * number + 1],
            )
        )
        copies[-1].start()
    for copy in copies:
        copy.wait()


def write_out(kept, distances, values, outs, before):
    count = len(distances)
    return pl.pallas_call(
        functools.partial(out_kernel, kept, distances),
        out_shape=outs,
        in_specs=[ANYWHERE] * len(before) + [IN_VMEM] * count,
        out_specs=[pl.BlockSpec(memory_space=pltpu.HBM)] * 2,
        scratch_shapes=[
            pltpu.VMEM((count, outs[0].shape[1], LANES), F32),
            pltpu.VMEM((count, outs[1].shape[0], LANES), F32),
            pltpu.SemaphoreType.DMA((2 * count,)),
        ],
        input_output_aliases={0: 0, 1: 1} if before else {},
        compiler_params=pltpu.CompilerParams(vmem_limit_bytes=VMEM_LIMIT),
        cost_estimate=pl.CostEstimate(flops=1000, bytes_accessed=1000, transcendentals=0),
    )(*before, *values)


def plain_out_kernel(kept, in_ref, branch_ref, class_ref):
    for chunk in range(in_ref.shape[0]):
        write_chunk(kept, chunk, in_ref[chunk], branch_ref, class_ref)


def in_group(value, distance=None):
    members = [value]
    steps = [0]
    distance = lax.axis_size("shuf") // 2 if distance is None else distance
    while distance:
        members += [swapped(member, distance, "shuf") for member in members]
        steps += [step + distance for step in steps]
        distance //= 2
    return [members[steps.index(step)] for step in range(len(steps))]


def body(
    features, tile_values, tile_dst, tile_src, tile_count, send_left, send_right,
    send_count, batch_order, labels, w_branch, w_class,
):
    block = tile_values.shape[1]
    nodes, width = features.shape
    local = nodes // block
    slots = send_left.shape[0]
    tiles = tile_values.shape[0]
    branches, _, hid = w_branch.shape
    cat, classes = w_class.shape
    dom = lax.axis_size("dom")
    shuf = lax.axis_size("shuf")
    mine = lax.axis_index("shuf")
    share = nodes // shuf
    own = hid // shuf
    own_class = cat // shuf
    kept = up_to(classes, 16)
    row_scale = 1.0 / math.sqrt(float(nodes * dom * shuf))
    plan = Plan(tiles, slots)
    small = jnp.concatenate(
        [tile_dst, tile_src, tile_count, send_left, send_right, send_count.reshape(-1)]
    )
    blocks_f32 = jax.ShapeDtypeStruct((local, block, width), F32)
    slots_f32 = jax.ShapeDtypeStruct((slots, block, width), F32)
    rows_b16 = jax.ShapeDtypeStruct((nodes, width), BF16)
    first_b16 = jax.ShapeDtypeStruct((nodes + 16, width), BF16)
    logits_f32 = jax.ShapeDtypeStruct((classes, nodes), F32)
    w_class_t = w_class.T

    current = features.reshape(local, block, width)
    gathered = []
    logits = None
    hop_flops = 12 * tiles * block * block * width
    forward_flops = 2 * nodes * hid * (width + classes)
    ext = pltpu.VMEM((local + 2 * slots, block, width), F32)
    to_left, to_right, to_wrap, current, *rows = call(
        first_kernel,
        [slots_f32, slots_f32, slots_f32, blocks_f32, first_b16],
        [ANYWHERE] * 5,
        1000,
        [
            pltpu.SMEM((slots,), jnp.int32),
            pltpu.SMEM((slots,), jnp.int32),
            pltpu.SMEM((1, 2), jnp.int32),
            pltpu.VMEM((1, nodes), jnp.int32),
            pltpu.SemaphoreType.DMA((5,)),
        ],
        limit=VMEM_ALL,
    )(send_left, send_right, send_count, current, labels.reshape(1, nodes))
    current, tile_values, w_class_t = call(
        ready_kernel,
        [
            blocks_f32,
            jax.ShapeDtypeStruct(tile_values.shape, F32),
            jax.ShapeDtypeStruct(w_class_t.shape, BF16),
        ],
        [IN_VMEM] * 3,
        1000,
    )(current, tile_values, w_class_t)
    crossing = []
    for hop in range(HOPS):
        came = exchanged(to_wrap, to_right, to_left)
        for value in rows:
            if hop < HOPS - 1:
                crossing.append((value, swapped(value, shuf // 2, "shuf")))
            else:
                crossing, _ = lax.optimization_barrier((crossing, current))
                for mine_here, across in crossing:
                    gathered.append(
                        in_group(mine_here, shuf // 4) + in_group(across, shuf // 4)
                    )
                gathered.append(in_group(value))
        before = [] if logits is None else [logits]
        logits = call(
            functools.partial(forward_kernel, hop),
            logits_f32,
            [IN_VMEM] * (3 + len(before)),
            forward_flops,
            after=[members[shuf // 2] for members in gathered[:2]] if hop == HOPS - 1 else [],
        )(current, w_branch, w_class_t, *before)
        if hop == 0:
            first_logits = logits
            after = []
        else:
            after = [first_logits]
        if hop < HOPS - 1:
            current, to_left, to_right, to_wrap, *rows = call(
                functools.partial(hop_kernel, plan),
                [blocks_f32, slots_f32, slots_f32, slots_f32, rows_b16],
                [IN_SMEM] + [IN_VMEM] * 5,
                hop_flops,
                [ext],
                after,
            )(small, current, *came, tile_values)

    label_mine = call(
        label_kernel,
        jax.ShapeDtypeStruct((1, nodes), jnp.int32),
        [IN_VMEM] * (1 + shuf),
        1000,
    )(batch_order, *gathered[0])

    wt_own, wct_own = call(
        weights_kernel,
        [
            jax.ShapeDtypeStruct((branches, own, width), BF16),
            jax.ShapeDtypeStruct((branches, own, kept), BF16),
        ],
        [IN_VMEM] * 2,
        1000,
        [pltpu.VMEM((up_to(classes, LANES), own), F32)],
    )(w_branch, w_class_t)

    last_rows = call(
        functools.partial(last_hop_kernel, plan),
        jax.ShapeDtypeStruct((block, local * width), BF16),
        [IN_SMEM] + [IN_VMEM] * 5,
        hop_flops,
        [ext],
        [logits, label_mine, *gathered[1][1:]],
    )(small, current, *came, tile_values)
    dlogits = call(
        functools.partial(loss_and_gradient_kernel, row_scale),
        jax.ShapeDtypeStruct((kept + 16, nodes), BF16),
        [IN_VMEM] * 6,
        1000,
        after=[gathered[2][shuf // 2]],
    )(last_rows, logits, w_branch, w_class_t, batch_order, label_mine)
    chunks = own_class // LANES
    height = kept + width
    ahead = shuf // 2
    chunks_f32 = jax.ShapeDtypeStruct((chunks, height, LANES), F32)
    grad_flops = shuf * nodes * own_class * (3 * width + 2 * kept)
    weights = (w_branch, wt_own, wct_own)
    across_rows = swapped(last_rows, ahead, "shuf")
    across = swapped(dlogits, ahead, "shuf")
    close_rows = in_group(last_rows, ahead // 2)
    close = in_group(dlogits, ahead // 2)
    early = call(
        functools.partial(early_kernel, kept, ahead),
        chunks_f32,
        [IN_VMEM] * (5 * ahead + 3),
        1000,
    )(
        *[member for members in gathered for member in members[:ahead]],
        *close_rows, *close, *weights,
    )
    across, across_rows, early = lax.optimization_barrier((across, across_rows, early))
    distant_rows = in_group(across_rows, ahead // 2)
    distant = in_group(across, ahead // 2)
    late_ins = (
        early, *[member for members in gathered for member in members[ahead:]],
        *distant_rows, *distant, *weights,
    )
    last_all = close + distant
    loss_rows = call(
        loss_kernel, jax.ShapeDtypeStruct((1, nodes), F32), [IN_VMEM] * shuf, 1000
    )(*last_all).reshape(nodes)

    outs = [
        jax.ShapeDtypeStruct((branches, width, own), F32),
        jax.ShapeDtypeStruct((classes, own_class), F32),
    ]
    if chunks == dom and dom % 2 == 0 and dom & (dom - 1) == 0:
        half = dom // 2
        one_f32 = jax.ShapeDtypeStruct((height, LANES), F32)
        made = call(
            functools.partial(late_kernel, kept, ahead, half),
            [one_f32] * half + [jax.ShapeDtypeStruct((height, LANES), BF16)] * half,
            [IN_VMEM] * len(late_ins),
            grad_flops,
            [pltpu.VMEM(chunks_f32.shape, F32)],
        )(*late_ins)
        order = list(range(half - 1, -1, -1))
        arrived = {step: swapped(made[half + step], 1) for step in order}
        total = {step: made[step] + arrived[step].astype(F32) for step in order}
        far = {step: swapped(total[step].astype(BF16), 2 * step) for step in order[:-1]}
        summed = total[0]
        for step in order[:-1]:
            summed = lax.optimization_barrier(summed + far[step].astype(F32))
        near = [summed.astype(BF16)]
        near += [swapped(near[0], 2 * step) for step in range(1, half)]
        other = [swapped(value, 1) for value in near]
        results = []
        places = [2 * step for step in range(half)] + [2 * step + 1 for step in range(half)]
        for part in (slice(0, -half // 2), slice(-half // 2, None)):
            results = write_out(kept, places[part], (near + other)[part], outs, results)
        grad_branch, grad_class_t = results
    else:
        grads = call(
            functools.partial(plain_late_kernel, kept, ahead),
            chunks_f32,
            [IN_VMEM] * len(late_ins),
            grad_flops,
        )(*late_ins)
        grad_branch, grad_class_t = call(
            functools.partial(plain_out_kernel, kept), outs, [IN_VMEM], 1000
        )(lax.psum(grads, "dom"))
    return (loss_rows, grad_branch, grad_class_t.T)


def solution(mesh):
    return jax.shard_map(
        body,
        mesh=mesh,
        in_specs=(
            P(("dom", "shuf"), None),
            P(("dom", "shuf"), None, None),
            P(("dom", "shuf")),
            P(("dom", "shuf")),
            P(("dom", "shuf")),
            P(("dom", "shuf")),
            P(("dom", "shuf")),
            P(("dom", "shuf"), None),
            P(("dom", "shuf"), None),
            P(("dom", "shuf")),
            P(),
            P(),
        ),
        out_specs=(P(("dom", "shuf")), P(None, None, "shuf"), P("shuf", None)),
        check_vma=False,
    )
```

```python
import functools
import math

import jax
import jax.numpy as jnp
from jax import lax
from jax.experimental import pallas as pl
from jax.experimental.pallas import tpu as pltpu
from jax.sharding import PartitionSpec as P

HOPS = 3
LANES = 128
VMEM_LIMIT = 24 * 1024 * 1024
VMEM_ALL = 56 * 1024 * 1024

IN_VMEM = pl.BlockSpec(memory_space=pltpu.VMEM)
IN_SMEM = pl.BlockSpec(memory_space=pltpu.SMEM)
ANYWHERE = pl.BlockSpec(memory_space=pl.ANY)
BF16 = jnp.bfloat16
F32 = jnp.float32


def up_to(value, multiple):
    return -(-value // multiple) * multiple


def passed_along(value, axis, steps):
    count = lax.axis_size(axis)
    pairs = [(source, (source + steps) % count) for source in range(count)]
    return lax.ppermute(value, axis, pairs)


def swapped(value, distance, axis="dom"):
    pairs = [(source, source ^ distance) for source in range(lax.axis_size(axis))]
    return lax.ppermute(value, axis, pairs)


def matmul(left, right, dims=((1,), (0,)), precision=None):
    return lax.dot_general(
        left, right, (dims, ((), ())), precision=precision, preferred_element_type=F32
    )


def call(kernel, out_shape, in_specs, flops, scratch=(), after=(), limit=VMEM_LIMIT):
    many = isinstance(out_shape, (list, tuple))
    outs = out_shape if many else [out_shape]
    moved = sum(math.prod(one.shape) * one.dtype.itemsize for one in outs)
    waited = len(after)

    def run(*refs):
        kernel(*refs[waited:])

    made = pl.pallas_call(
        run,
        out_shape=out_shape,
        in_specs=[ANYWHERE] * waited + in_specs,
        out_specs=[IN_VMEM] * len(outs) if many else IN_VMEM,
        scratch_shapes=list(scratch),
        compiler_params=pltpu.CompilerParams(vmem_limit_bytes=limit),
        cost_estimate=pl.CostEstimate(
            flops=flops, bytes_accessed=3 * moved if flops > 1000 else 1000, transcendentals=0
        ),
    )
    return functools.partial(made, *after)


class Plan:
    def __init__(self, tiles, slots):
        self.tiles = tiles
        self.slots = slots
        self.dst = 0
        self.src = tiles
        self.count = 2 * tiles
        self.left = 2 * tiles + 1
        self.right = self.left + slots
        self.sent = self.right + slots


def write_sends(blocks, left_ref, right_ref, ids, counts):
    for slot in range(left_ref.shape[0]):
        for side, out_ref in enumerate((left_ref, right_ref)):
            index = ids(side, slot)
            picked = blocks[0]
            for number in range(1, len(blocks)):
                picked = jnp.where(index == number, blocks[number], picked)
            out_ref[slot] = jnp.where(slot < counts(side), picked, 0.0)


def copied(sources, targets, sems):
    copies = [
        pltpu.make_async_copy(source, target, sems.at[number])
        for number, (source, target) in enumerate(zip(sources, targets))
    ]
    for copy in copies:
        copy.start()
    for copy in copies:
        copy.wait()


def first_kernel(
    sl_ref, sr_ref, sc_ref, feat_ref, label_from,
    left_ref, right_ref, held_ref, b_ref,
    sl_here, sr_here, sc_here, label_ref, sems,
):
    copied(
        (sl_ref, sr_ref, sc_ref, feat_ref, label_from),
        (sl_here, sr_here, sc_here, held_ref, label_ref),
        sems,
    )
    blocks = [held_ref[number] for number in range(held_ref.shape[0])]
    write_sends(
        blocks,
        left_ref,
        right_ref,
        lambda side, slot: (sl_here, sr_here)[side][slot],
        lambda side: sc_here[0, side],
    )
    write_rows(blocks, b_ref)
    nodes = label_ref.shape[1]
    width = b_ref.shape[1]
    per_piece = nodes // width
    place = lax.broadcasted_iota(jnp.int32, (16, width), 0)
    packed = jnp.zeros((16, width), F32)
    for piece in range(2):
        value = label_ref[...] & 255 if piece == 0 else label_ref[...] >> 8
        value = value.astype(F32)
        for part in range(per_piece):
            packed = jnp.where(
                place == piece * per_piece + part,
                value[:, part * width : (part + 1) * width],
                packed,
            )
    b_ref[nodes:] = packed.astype(BF16)


def write_rows(blocks, b_ref):
    for number, block in enumerate(blocks):
        size = block.shape[0]
        b_ref[number * size : (number + 1) * size] = block.astype(BF16)


def next_blocks(plan, plan_ref, cur_ref, tiles_ref, ext_ref):
    local = cur_ref.shape[0]
    ext_ref[:local] = cur_ref[...]
    totals = [jnp.zeros(cur_ref.shape[1:], F32) for _ in range(local)]
    live = plan_ref[plan.count]
    for tile in range(plan.tiles):
        product = matmul(
            tiles_ref[tile],
            ext_ref[plan_ref[plan.src + tile]],
            precision=lax.Precision.HIGHEST,
        )
        wanted = jnp.where(tile < live, plan_ref[plan.dst + tile], -1)
        for number in range(local):
            totals[number] = totals[number] + jnp.where(wanted == number, product, 0.0)
    return totals


def extend(cur_ref, low_ref, high_ref, ext_ref):
    local = cur_ref.shape[0]
    slots = low_ref.shape[0]
    ext_ref[local : local + slots] = low_ref[...]
    ext_ref[local + slots :] = high_ref[...]


def hop_kernel(
    plan, plan_ref, cur_ref, low_ref, high_ref, tiles_ref, next_ref, left_ref, right_ref, *refs
):
    ext_ref = refs[-1]
    extend(cur_ref, low_ref, high_ref, ext_ref)
    blocks = next_blocks(plan, plan_ref, cur_ref, tiles_ref, ext_ref)
    write_sends(
        blocks,
        left_ref,
        right_ref,
        lambda side, slot: plan_ref[(plan.left, plan.right)[side] + slot],
        lambda side: plan_ref[plan.sent + side],
    )
    for number, block in enumerate(blocks):
        next_ref[number] = block
    for b_ref in refs[:-1]:
        write_rows(blocks, b_ref)


def ready_kernel(cur_ref, tiles_ref, wc_ref, cur_out, tiles_out, wc_out):
    cur_out[...] = cur_ref[...]
    tiles_out[...] = tiles_ref[...]
    wc_out[...] = wc_ref[...]


def branch_logits(branch, rows, w_ref, wc_ref):
    hidden = jnp.maximum(matmul(rows, w_ref[branch]), 0.0).astype(BF16)
    hid = hidden.shape[1]
    return matmul(wc_ref[:, branch * hid : (branch + 1) * hid], hidden, ((1,), (1,)))


def forward_kernel(branch, cur_ref, w_ref, wc_ref, *refs):
    rows = cur_ref[...].reshape(-1, cur_ref.shape[2]).astype(BF16)
    part = branch_logits(branch, rows, w_ref, wc_ref)
    if len(refs) == 2:
        part = refs[0][...] + part
    refs[-1][...] = part


def places(order_ref):
    nodes = order_ref.shape[1]
    rows = lax.broadcasted_iota(jnp.int32, (nodes, nodes), 0)
    return (order_ref[...] == rows).astype(F32).astype(BF16)


def wanted_places(nodes, group, step, offset, count):
    share = nodes // group
    mine = lax.axis_index("shuf")
    first = mine * share
    source = lax.broadcasted_iota(jnp.int32, (count, nodes), 0) + offset
    target = lax.broadcasted_iota(jnp.int32, (count, nodes), 1)
    moved = source + ((mine ^ step) - mine) * share
    wanted = (target == moved) & (source >= first) & (source < first + share)
    return wanted.astype(F32).astype(BF16)


def label_kernel(order_ref, *refs):
    nodes = order_ref.shape[1]
    group = len(refs) - 1
    width = refs[0].shape[1]
    per_piece = nodes // width
    ordered = [jnp.zeros((1, nodes), F32) for _ in range(2)]
    for step in range(group):
        tail = refs[step][nodes:]
        for part in range(per_piece):
            moved = matmul(tail, wanted_places(nodes, group, step, part * width, width))
            for piece in range(2):
                row = piece * per_piece + part
                ordered[piece] = ordered[piece] + moved[row : row + 1]
    number = lax.broadcasted_iota(jnp.int32, (16, nodes), 0)
    packed = jnp.where(number == 0, ordered[0], jnp.where(number == 1, ordered[1], 0.0))
    pieces = matmul(packed.astype(BF16), places(order_ref), ((1,), (1,)))
    refs[-1][...] = (pieces[0:1] + 256.0 * pieces[1:2]).astype(jnp.int32)


def loss_kernel(*refs):
    group = len(refs) - 1
    height, nodes = refs[0].shape
    total = jnp.zeros((16, nodes), F32)
    for step in range(group):
        wanted = wanted_places(nodes, group, step, 0, nodes)
        total = total + matmul(refs[step][height - 16 :], wanted)
    refs[-1][...] = total[0:1] + total[1:2] + total[2:3]


def last_hop_kernel(plan, plan_ref, cur_ref, low_ref, high_ref, tiles_ref, out_ref, ext_ref):
    extend(cur_ref, low_ref, high_ref, ext_ref)
    blocks = next_blocks(plan, plan_ref, cur_ref, tiles_ref, ext_ref)
    for number, block in enumerate(blocks):
        width = block.shape[1]
        columns = slice(number * width, (number + 1) * width)
        out_ref[:, columns] = block.astype(BF16)


def stacked(ref, width):
    parts = ref.shape[1] // width
    return [ref[:, part * width : (part + 1) * width] for part in range(parts)]


def loss_and_gradient_kernel(
    row_scale, rows_ref, before_ref, w_ref, wc_ref, order_ref, label_ref, out_ref
):
    rows_b = jnp.concatenate(stacked(rows_ref, w_ref.shape[1]), axis=0)
    logits = before_ref[...] + branch_logits(w_ref.shape[0] - 1, rows_b, w_ref, wc_ref)
    classes, rows = logits.shape
    kept = up_to(classes, 16)
    hit = lax.broadcasted_iota(jnp.int32, (classes, rows), 0) == label_ref[...]
    top = jnp.max(logits, axis=0, keepdims=True)
    log_total = top + jnp.log(jnp.sum(jnp.exp(logits - top), axis=0, keepdims=True))
    loss = log_total - jnp.sum(jnp.where(hit, logits, 0.0), axis=0, keepdims=True)
    dlogits = (jnp.exp(logits - log_total) - jnp.where(hit, 1.0, 0.0)) * row_scale
    out_ref[kept - 16 : kept] = jnp.zeros((16, rows), BF16)
    out_ref[:classes] = dlogits.astype(BF16)
    number = lax.broadcasted_iota(jnp.int32, (16, rows), 0)
    packed = jnp.zeros((16, rows), F32)
    rest = loss
    for piece in range(3):
        part = rest.astype(BF16).astype(F32)
        packed = jnp.where(number == piece, part, packed)
        rest = rest - part
    out_ref[kept:] = matmul(packed.astype(BF16), places(order_ref)).astype(BF16)


def weights_kernel(w_ref, wc_ref, wt_ref, wct_ref, pad_ref):
    branches, own, kept = wct_ref.shape
    classes = wc_ref.shape[0]
    hid = w_ref.shape[2]
    first = lax.axis_index("shuf") * own
    pad_ref[...] = jnp.zeros_like(pad_ref)
    for branch in range(branches):
        columns = w_ref[branch, :, pl.ds(pl.multiple_of(first, LANES), own)]
        wt_ref[branch] = columns.astype(F32).T.astype(BF16)
        columns = wc_ref[:, pl.ds(pl.multiple_of(branch * hid + first, LANES), own)]
        pad_ref[:classes] = columns.astype(F32)
        wct_ref[branch] = pad_ref[...].T[:, :kept].astype(BF16)


def add_chunks(kept, before_ref, row_refs, last_refs, dlogit_refs, w_ref, wt_ref, wct_ref, chunks_ref):
    members = len(last_refs)
    branches, own, width = wt_ref.shape
    nodes = last_refs[0].shape[1]
    hid = w_ref.shape[2]
    all_rows = []
    for branch in range(branches - 1):
        ours = row_refs[branch * members : (branch + 1) * members]
        all_rows.append(jnp.concatenate([ref[:nodes] for ref in ours], axis=0))
    ours = [rows for ref in last_refs for rows in stacked(ref, width)]
    all_rows.append(jnp.concatenate(ours, axis=0))
    dlogits_t = jnp.concatenate([ref[:kept] for ref in dlogit_refs], axis=1)
    own_class = branches * own
    first = lax.axis_index("shuf") * own_class
    which = first // hid
    columns = pl.ds(pl.multiple_of(first - which * hid, LANES), own_class)
    chosen = all_rows[0]
    for branch in range(1, branches):
        chosen = jnp.where(which == branch, all_rows[branch], chosen)

    def put(chunk, rows, value):
        chunks_ref[chunk, rows] = value if before_ref is None else before_ref[chunk, rows] + value

    hidden = jnp.maximum(matmul(chosen, w_ref[which, :, columns]), 0.0).astype(BF16)
    class_t = matmul(dlogits_t, hidden)
    for chunk in range(chunks_ref.shape[0]):
        put(chunk, slice(0, kept), class_t[:, chunk * LANES : (chunk + 1) * LANES])
    per_branch = chunks_ref.shape[0] // branches
    for branch, rows in enumerate(all_rows):
        live = matmul(wt_ref[branch], rows, ((1,), (1,))) > 0.0
        dhidden_t = jnp.where(live, matmul(wct_ref[branch], dlogits_t), 0.0).astype(BF16)
        branch_t = matmul(dhidden_t, rows)
        for part in range(per_branch):
            put(
                branch * per_branch + part,
                slice(kept, kept + width),
                branch_t[part * LANES : (part + 1) * LANES],
            )


def split_refs(members, refs):
    last = len(refs) - 3 - 2 * members
    return (
        refs[:last], refs[last : last + members], refs[last + members : last + 2 * members],
        *refs[last + 2 * members :],
    )


def early_kernel(kept, members, *refs):
    add_chunks(kept, None, *split_refs(members, refs[:-1]), refs[-1])


def late_chunks(kept, members, early_ref, refs, chunks_ref):
    add_chunks(kept, early_ref, *split_refs(members, refs), chunks_ref)


def late_kernel(kept, members, half, early_ref, *refs):
    ins = len(refs) - 1 - 2 * half
    outs = refs[ins:-1]
    chunks_ref = refs[-1]
    late_chunks(kept, members, early_ref, refs[:ins], chunks_ref)
    dom = lax.axis_index("dom")
    for step in range(half):
        stays = dom ^ (2 * step)
        outs[step][...] = chunks_ref[stays]
        outs[half + step][...] = chunks_ref[stays ^ 1].astype(BF16)


def plain_late_kernel(kept, members, early_ref, *refs):
    late_chunks(kept, members, early_ref, refs[:-1], refs[-1])


def write_chunk(kept, chunk, value, branch_ref, class_ref):
    per_branch = branch_ref.shape[2] // LANES
    start = pl.multiple_of(chunk * LANES, LANES)
    class_ref[:, pl.ds(start, LANES)] = value[: class_ref.shape[0]]
    branch = chunk // per_branch
    start = pl.multiple_of((chunk - branch * per_branch) * LANES, LANES)
    branch_ref[branch, :, pl.ds(start, LANES)] = value[kept:].T


def out_kernel(kept, distances, *refs):
    count = len(distances)
    ins = refs[-5 - count : -5]
    branch_ref, class_ref, branch_here, class_here, sems = refs[-5:]
    dom = lax.axis_index("dom")
    per_branch = branch_ref.shape[2] // LANES
    copies = []
    for number, distance in enumerate(distances):
        chunk = dom ^ distance
        value = ins[number][...].astype(F32)
        class_here[number] = value[: class_ref.shape[0]]
        start = pl.multiple_of(chunk * LANES, LANES)
        copies.append(
            pltpu.make_async_copy(
                class_here.at[number], class_ref.at[:, pl.ds(start, LANES)], sems.at[2 * number]
            )
        )
        copies[-1].start()
        branch_here[number] = value[kept:].T
        branch = chunk // per_branch
        start = pl.multiple_of((chunk - branch * per_branch) * LANES, LANES)
        copies.append(
            pltpu.make_async_copy(
                branch_here.at[number],
                branch_ref.at[branch, :, pl.ds(start, LANES)],
                sems.at[2 * number + 1],
            )
        )
        copies[-1].start()
    for copy in copies:
        copy.wait()


def write_out(kept, distances, values, outs, before):
    count = len(distances)
    return pl.pallas_call(
        functools.partial(out_kernel, kept, distances),
        out_shape=outs,
        in_specs=[ANYWHERE] * len(before) + [IN_VMEM] * count,
        out_specs=[pl.BlockSpec(memory_space=pltpu.HBM)] * 2,
        scratch_shapes=[
            pltpu.VMEM((count, outs[0].shape[1], LANES), F32),
            pltpu.VMEM((count, outs[1].shape[0], LANES), F32),
            pltpu.SemaphoreType.DMA((2 * count,)),
        ],
        input_output_aliases={0: 0, 1: 1} if before else {},
        compiler_params=pltpu.CompilerParams(vmem_limit_bytes=VMEM_LIMIT),
        cost_estimate=pl.CostEstimate(flops=1000, bytes_accessed=1000, transcendentals=0),
    )(*before, *values)


def plain_out_kernel(kept, in_ref, branch_ref, class_ref):
    for chunk in range(in_ref.shape[0]):
        write_chunk(kept, chunk, in_ref[chunk], branch_ref, class_ref)


def in_group(value, distance=None):
    members = [value]
    steps = [0]
    distance = lax.axis_size("shuf") // 2 if distance is None else distance
    while distance:
        members += [swapped(member, distance, "shuf") for member in members]
        steps += [step + distance for step in steps]
        distance //= 2
    return [members[steps.index(step)] for step in range(len(steps))]


def body(
    features, tile_values, tile_dst, tile_src, tile_count, send_left, send_right,
    send_count, batch_order, labels, w_branch, w_class,
):
    block = tile_values.shape[1]
    nodes, width = features.shape
    local = nodes // block
    slots = send_left.shape[0]
    tiles = tile_values.shape[0]
    branches, _, hid = w_branch.shape
    cat, classes = w_class.shape
    dom = lax.axis_size("dom")
    shuf = lax.axis_size("shuf")
    mine = lax.axis_index("shuf")
    share = nodes // shuf
    own = hid // shuf
    own_class = cat // shuf
    kept = up_to(classes, 16)
    row_scale = 1.0 / math.sqrt(float(nodes * dom * shuf))
    plan = Plan(tiles, slots)
    small = jnp.concatenate(
        [tile_dst, tile_src, tile_count, send_left, send_right, send_count.reshape(-1)]
    )
    blocks_f32 = jax.ShapeDtypeStruct((local, block, width), F32)
    slots_f32 = jax.ShapeDtypeStruct((slots, block, width), F32)
    rows_b16 = jax.ShapeDtypeStruct((nodes, width), BF16)
    first_b16 = jax.ShapeDtypeStruct((nodes + 16, width), BF16)
    logits_f32 = jax.ShapeDtypeStruct((classes, nodes), F32)
    w_class_t = w_class.T

    current = features.reshape(local, block, width)
    gathered = []
    logits = None
    hop_flops = 12 * tiles * block * block * width
    forward_flops = 2 * nodes * hid * (width + classes)
    ext = pltpu.VMEM((local + 2 * slots, block, width), F32)
    to_left, to_right, current, *rows = call(
        first_kernel,
        [slots_f32, slots_f32, blocks_f32, first_b16],
        [ANYWHERE] * 5,
        1000,
        [
            pltpu.SMEM((slots,), jnp.int32),
            pltpu.SMEM((slots,), jnp.int32),
            pltpu.SMEM((1, 2), jnp.int32),
            pltpu.VMEM((1, nodes), jnp.int32),
            pltpu.SemaphoreType.DMA((5,)),
        ],
        limit=VMEM_ALL,
    )(send_left, send_right, send_count, current, labels.reshape(1, nodes))
    current, tile_values, w_class_t = call(
        ready_kernel,
        [
            blocks_f32,
            jax.ShapeDtypeStruct(tile_values.shape, F32),
            jax.ShapeDtypeStruct(w_class_t.shape, BF16),
        ],
        [IN_VMEM] * 3,
        1000,
    )(current, tile_values, w_class_t)
    for hop in range(HOPS):
        from_lower = passed_along(to_right, "dom", 1)
        from_upper = passed_along(to_left, "dom", -1)
        for value in rows:
            gathered.append(in_group(value))
        before = [] if logits is None else [logits]
        logits = call(
            functools.partial(forward_kernel, hop),
            logits_f32,
            [IN_VMEM] * (3 + len(before)),
            forward_flops,
            after=[members[shuf // 2] for members in gathered[:2]] if hop == HOPS - 1 else [],
        )(current, w_branch, w_class_t, *before)
        if hop == 0:
            after = []
        else:
            after = [logits]
        if hop < HOPS - 1:
            current, to_left, to_right, *rows = call(
                functools.partial(hop_kernel, plan),
                [blocks_f32, slots_f32, slots_f32, rows_b16],
                [IN_SMEM] + [IN_VMEM] * 4,
                hop_flops,
                [ext],
                after,
            )(small, current, from_lower, from_upper, tile_values)

    label_mine = call(
        label_kernel,
        jax.ShapeDtypeStruct((1, nodes), jnp.int32),
        [IN_VMEM] * (1 + shuf),
        1000,
    )(batch_order, *gathered[0])

    wt_own, wct_own = call(
        weights_kernel,
        [
            jax.ShapeDtypeStruct((branches, own, width), BF16),
            jax.ShapeDtypeStruct((branches, own, kept), BF16),
        ],
        [IN_VMEM] * 2,
        1000,
        [pltpu.VMEM((up_to(classes, LANES), own), F32)],
    )(w_branch, w_class_t)

    last_rows = call(
        functools.partial(last_hop_kernel, plan),
        jax.ShapeDtypeStruct((block, local * width), BF16),
        [IN_SMEM] + [IN_VMEM] * 4,
        hop_flops,
        [ext],
        [logits, label_mine, *gathered[1][1:]],
    )(small, current, from_lower, from_upper, tile_values)
    dlogits = call(
        functools.partial(loss_and_gradient_kernel, row_scale),
        jax.ShapeDtypeStruct((kept + 16, nodes), BF16),
        [IN_VMEM] * 6,
        1000,
        after=[gathered[2][shuf // 2]],
    )(last_rows, logits, w_branch, w_class_t, batch_order, label_mine)
    chunks = own_class // LANES
    height = kept + width
    ahead = shuf // 2
    chunks_f32 = jax.ShapeDtypeStruct((chunks, height, LANES), F32)
    grad_flops = shuf * nodes * own_class * (3 * width + 2 * kept)
    weights = (w_branch, wt_own, wct_own)
    across_rows = swapped(last_rows, ahead, "shuf")
    across = swapped(dlogits, ahead, "shuf")
    close_rows = in_group(last_rows, ahead // 2)
    close = in_group(dlogits, ahead // 2)
    early = call(
        functools.partial(early_kernel, kept, ahead),
        chunks_f32,
        [IN_VMEM] * (5 * ahead + 3),
        1000,
    )(
        *[member for members in gathered for member in members[:ahead]],
        *close_rows, *close, *weights,
    )
    across, across_rows, early = lax.optimization_barrier((across, across_rows, early))
    distant_rows = in_group(across_rows, ahead // 2)
    distant = in_group(across, ahead // 2)
    late_ins = (
        early, *[member for members in gathered for member in members[ahead:]],
        *distant_rows, *distant, *weights,
    )
    last_all = close + distant
    loss_rows = call(
        loss_kernel, jax.ShapeDtypeStruct((1, nodes), F32), [IN_VMEM] * shuf, 1000
    )(*last_all).reshape(nodes)

    outs = [
        jax.ShapeDtypeStruct((branches, width, own), F32),
        jax.ShapeDtypeStruct((classes, own_class), F32),
    ]
    if chunks == dom and dom % 2 == 0 and dom & (dom - 1) == 0:
        half = dom // 2
        one_f32 = jax.ShapeDtypeStruct((height, LANES), F32)
        made = call(
            functools.partial(late_kernel, kept, ahead, half),
            [one_f32] * half + [jax.ShapeDtypeStruct((height, LANES), BF16)] * half,
            [IN_VMEM] * len(late_ins),
            grad_flops,
            [pltpu.VMEM(chunks_f32.shape, F32)],
        )(*late_ins)
        order = list(range(half - 1, -1, -1))
        arrived = {step: swapped(made[half + step], 1) for step in order}
        total = {step: made[step] + arrived[step].astype(F32) for step in order}
        far = {step: swapped(total[step].astype(BF16), 2 * step) for step in order[:-1]}
        summed = total[0]
        for step in order[:-1]:
            summed = lax.optimization_barrier(summed + far[step].astype(F32))
        near = [summed.astype(BF16)]
        near += [swapped(near[0], 2 * step) for step in range(1, half)]
        other = [swapped(value, 1) for value in near]
        results = []
        places = [2 * step for step in range(half)] + [2 * step + 1 for step in range(half)]
        for part in (slice(0, -half // 2), slice(-half // 2, None)):
            results = write_out(kept, places[part], (near + other)[part], outs, results)
        grad_branch, grad_class_t = results
    else:
        grads = call(
            functools.partial(plain_late_kernel, kept, ahead),
            chunks_f32,
            [IN_VMEM] * len(late_ins),
            grad_flops,
        )(*late_ins)
        grad_branch, grad_class_t = call(
            functools.partial(plain_out_kernel, kept), outs, [IN_VMEM], 1000
        )(lax.psum(grads, "dom"))
    return (loss_rows, grad_branch, grad_class_t.T)


def solution(mesh):
    return jax.shard_map(
        body,
        mesh=mesh,
        in_specs=(
            P(("dom", "shuf"), None),
            P(("dom", "shuf"), None, None),
            P(("dom", "shuf")),
            P(("dom", "shuf")),
            P(("dom", "shuf")),
            P(("dom", "shuf")),
            P(("dom", "shuf")),
            P(("dom", "shuf"), None),
            P(("dom", "shuf"), None),
            P(("dom", "shuf")),
            P(),
            P(),
        ),
        out_specs=(P(("dom", "shuf")), P(None, None, "shuf"), P("shuf", None)),
        check_vma=False,
    )
```

```python
import functools
import math

import jax
import jax.numpy as jnp
from jax import lax
from jax.experimental import pallas as pl
from jax.experimental.pallas import tpu as pltpu
from jax.sharding import PartitionSpec as P

HOPS = 3
LANES = 128
VMEM_LIMIT = 24 * 1024 * 1024
VMEM_ALL = 56 * 1024 * 1024

IN_VMEM = pl.BlockSpec(memory_space=pltpu.VMEM)
IN_SMEM = pl.BlockSpec(memory_space=pltpu.SMEM)
ANYWHERE = pl.BlockSpec(memory_space=pl.ANY)
BF16 = jnp.bfloat16
F32 = jnp.float32


def up_to(value, multiple):
    return -(-value // multiple) * multiple


def passed_along(value, axis, steps):
    count = lax.axis_size(axis)
    pairs = [(source, (source + steps) % count) for source in range(count)]
    return lax.ppermute(value, axis, pairs)


def swapped(value, distance, axis="dom"):
    pairs = [(source, source ^ distance) for source in range(lax.axis_size(axis))]
    return lax.ppermute(value, axis, pairs)


def matmul(left, right, dims=((1,), (0,)), precision=None):
    return lax.dot_general(
        left, right, (dims, ((), ())), precision=precision, preferred_element_type=F32
    )


def call(kernel, out_shape, in_specs, flops, scratch=(), after=(), limit=VMEM_LIMIT):
    many = isinstance(out_shape, (list, tuple))
    outs = out_shape if many else [out_shape]
    moved = sum(math.prod(one.shape) * one.dtype.itemsize for one in outs)
    waited = len(after)

    def run(*refs):
        kernel(*refs[waited:])

    made = pl.pallas_call(
        run,
        out_shape=out_shape,
        in_specs=[ANYWHERE] * waited + in_specs,
        out_specs=[IN_VMEM] * len(outs) if many else IN_VMEM,
        scratch_shapes=list(scratch),
        compiler_params=pltpu.CompilerParams(vmem_limit_bytes=limit),
        cost_estimate=pl.CostEstimate(
            flops=flops, bytes_accessed=3 * moved if flops > 1000 else 1000, transcendentals=0
        ),
    )
    return functools.partial(made, *after)


class Plan:
    def __init__(self, tiles, slots):
        self.tiles = tiles
        self.slots = slots
        self.dst = 0
        self.src = tiles
        self.count = 2 * tiles
        self.left = 2 * tiles + 1
        self.right = self.left + slots
        self.sent = self.right + slots


def write_sends(blocks, left_ref, right_ref, ids, counts):
    for slot in range(left_ref.shape[0]):
        for side, out_ref in enumerate((left_ref, right_ref)):
            index = ids(side, slot)
            picked = blocks[0]
            for number in range(1, len(blocks)):
                picked = jnp.where(index == number, blocks[number], picked)
            out_ref[slot] = jnp.where(slot < counts(side), picked, 0.0)


def copied(sources, targets, sems):
    copies = [
        pltpu.make_async_copy(source, target, sems.at[number])
        for number, (source, target) in enumerate(zip(sources, targets))
    ]
    for copy in copies:
        copy.start()
    for copy in copies:
        copy.wait()


def first_kernel(
    sl_ref, sr_ref, sc_ref, feat_ref, label_from,
    left_ref, right_ref, held_ref, b_ref,
    sl_here, sr_here, sc_here, label_ref, sems,
):
    copied(
        (sl_ref, sr_ref, sc_ref, feat_ref, label_from),
        (sl_here, sr_here, sc_here, held_ref, label_ref),
        sems,
    )
    blocks = [held_ref[number] for number in range(held_ref.shape[0])]
    write_sends(
        blocks,
        left_ref,
        right_ref,
        lambda side, slot: (sl_here, sr_here)[side][slot],
        lambda side: sc_here[0, side],
    )
    write_rows(blocks, b_ref)
    nodes = label_ref.shape[1]
    width = b_ref.shape[1]
    per_piece = nodes // width
    place = lax.broadcasted_iota(jnp.int32, (16, width), 0)
    packed = jnp.zeros((16, width), F32)
    for piece in range(2):
        value = label_ref[...] & 255 if piece == 0 else label_ref[...] >> 8
        value = value.astype(F32)
        for part in range(per_piece):
            packed = jnp.where(
                place == piece * per_piece + part,
                value[:, part * width : (part + 1) * width],
                packed,
            )
    b_ref[nodes:] = packed.astype(BF16)


def write_rows(blocks, b_ref):
    for number, block in enumerate(blocks):
        size = block.shape[0]
        b_ref[number * size : (number + 1) * size] = block.astype(BF16)


def next_blocks(plan, plan_ref, cur_ref, tiles_ref, ext_ref):
    local = cur_ref.shape[0]
    ext_ref[:local] = cur_ref[...]
    totals = [jnp.zeros(cur_ref.shape[1:], F32) for _ in range(local)]
    live = plan_ref[plan.count]
    for tile in range(plan.tiles):
        product = matmul(
            tiles_ref[tile],
            ext_ref[plan_ref[plan.src + tile]],
            precision=lax.Precision.HIGHEST,
        )
        wanted = jnp.where(tile < live, plan_ref[plan.dst + tile], -1)
        for number in range(local):
            totals[number] = totals[number] + jnp.where(wanted == number, product, 0.0)
    return totals


def extend(cur_ref, low_ref, high_ref, ext_ref):
    local = cur_ref.shape[0]
    slots = low_ref.shape[0]
    ext_ref[local : local + slots] = low_ref[...]
    ext_ref[local + slots :] = high_ref[...]


def hop_kernel(
    plan, plan_ref, cur_ref, low_ref, high_ref, tiles_ref, next_ref, left_ref, right_ref, *refs
):
    ext_ref = refs[-1]
    extend(cur_ref, low_ref, high_ref, ext_ref)
    blocks = next_blocks(plan, plan_ref, cur_ref, tiles_ref, ext_ref)
    write_sends(
        blocks,
        left_ref,
        right_ref,
        lambda side, slot: plan_ref[(plan.left, plan.right)[side] + slot],
        lambda side: plan_ref[plan.sent + side],
    )
    for number, block in enumerate(blocks):
        next_ref[number] = block
    for b_ref in refs[:-1]:
        write_rows(blocks, b_ref)


def ready_kernel(cur_ref, tiles_ref, wc_ref, cur_out, tiles_out, wc_out):
    cur_out[...] = cur_ref[...]
    tiles_out[...] = tiles_ref[...]
    wc_out[...] = wc_ref[...]


def branch_logits(branch, rows, w_ref, wc_ref):
    hidden = jnp.maximum(matmul(rows, w_ref[branch]), 0.0).astype(BF16)
    hid = hidden.shape[1]
    return matmul(wc_ref[:, branch * hid : (branch + 1) * hid], hidden, ((1,), (1,)))


def forward_kernel(branch, cur_ref, w_ref, wc_ref, *refs):
    rows = cur_ref[...].reshape(-1, cur_ref.shape[2]).astype(BF16)
    part = branch_logits(branch, rows, w_ref, wc_ref)
    if len(refs) == 2:
        part = refs[0][...] + part
    refs[-1][...] = part


def places(order_ref):
    nodes = order_ref.shape[1]
    rows = lax.broadcasted_iota(jnp.int32, (nodes, nodes), 0)
    return (order_ref[...] == rows).astype(F32).astype(BF16)


def wanted_places(nodes, group, step, offset, count):
    share = nodes // group
    mine = lax.axis_index("shuf")
    first = mine * share
    source = lax.broadcasted_iota(jnp.int32, (count, nodes), 0) + offset
    target = lax.broadcasted_iota(jnp.int32, (count, nodes), 1)
    moved = source + ((mine ^ step) - mine) * share
    wanted = (target == moved) & (source >= first) & (source < first + share)
    return wanted.astype(F32).astype(BF16)


def label_kernel(order_ref, *refs):
    nodes = order_ref.shape[1]
    group = len(refs) - 1
    width = refs[0].shape[1]
    per_piece = nodes // width
    ordered = [jnp.zeros((1, nodes), F32) for _ in range(2)]
    for step in range(group):
        tail = refs[step][nodes:]
        for part in range(per_piece):
            moved = matmul(tail, wanted_places(nodes, group, step, part * width, width))
            for piece in range(2):
                row = piece * per_piece + part
                ordered[piece] = ordered[piece] + moved[row : row + 1]
    number = lax.broadcasted_iota(jnp.int32, (16, nodes), 0)
    packed = jnp.where(number == 0, ordered[0], jnp.where(number == 1, ordered[1], 0.0))
    pieces = matmul(packed.astype(BF16), places(order_ref), ((1,), (1,)))
    refs[-1][...] = (pieces[0:1] + 256.0 * pieces[1:2]).astype(jnp.int32)


def loss_kernel(*refs):
    group = len(refs) - 1
    height, nodes = refs[0].shape
    total = jnp.zeros((16, nodes), F32)
    for step in range(group):
        wanted = wanted_places(nodes, group, step, 0, nodes)
        total = total + matmul(refs[step][height - 16 :], wanted)
    refs[-1][...] = total[0:1] + total[1:2] + total[2:3]


def last_hop_kernel(plan, plan_ref, cur_ref, low_ref, high_ref, tiles_ref, out_ref, ext_ref):
    extend(cur_ref, low_ref, high_ref, ext_ref)
    blocks = next_blocks(plan, plan_ref, cur_ref, tiles_ref, ext_ref)
    for number, block in enumerate(blocks):
        width = block.shape[1]
        columns = slice(number * width, (number + 1) * width)
        out_ref[:, columns] = block.astype(BF16)


def stacked(ref, width):
    parts = ref.shape[1] // width
    return [ref[:, part * width : (part + 1) * width] for part in range(parts)]


def loss_and_gradient_kernel(
    row_scale, rows_ref, before_ref, w_ref, wc_ref, order_ref, label_ref, out_ref
):
    rows_b = jnp.concatenate(stacked(rows_ref, w_ref.shape[1]), axis=0)
    logits = before_ref[...] + branch_logits(w_ref.shape[0] - 1, rows_b, w_ref, wc_ref)
    classes, rows = logits.shape
    kept = up_to(classes, 16)
    hit = lax.broadcasted_iota(jnp.int32, (classes, rows), 0) == label_ref[...]
    top = jnp.max(logits, axis=0, keepdims=True)
    log_total = top + jnp.log(jnp.sum(jnp.exp(logits - top), axis=0, keepdims=True))
    loss = log_total - jnp.sum(jnp.where(hit, logits, 0.0), axis=0, keepdims=True)
    dlogits = (jnp.exp(logits - log_total) - jnp.where(hit, 1.0, 0.0)) * row_scale
    out_ref[kept - 16 : kept] = jnp.zeros((16, rows), BF16)
    out_ref[:classes] = dlogits.astype(BF16)
    number = lax.broadcasted_iota(jnp.int32, (16, rows), 0)
    packed = jnp.zeros((16, rows), F32)
    rest = loss
    for piece in range(3):
        part = rest.astype(BF16).astype(F32)
        packed = jnp.where(number == piece, part, packed)
        rest = rest - part
    out_ref[kept:] = matmul(packed.astype(BF16), places(order_ref)).astype(BF16)


def weights_kernel(w_ref, wc_ref, wt_ref, wct_ref, pad_ref):
    branches, own, kept = wct_ref.shape
    classes = wc_ref.shape[0]
    hid = w_ref.shape[2]
    first = lax.axis_index("shuf") * own
    pad_ref[...] = jnp.zeros_like(pad_ref)
    for branch in range(branches):
        columns = w_ref[branch, :, pl.ds(pl.multiple_of(first, LANES), own)]
        wt_ref[branch] = columns.astype(F32).T.astype(BF16)
        columns = wc_ref[:, pl.ds(pl.multiple_of(branch * hid + first, LANES), own)]
        pad_ref[:classes] = columns.astype(F32)
        wct_ref[branch] = pad_ref[...].T[:, :kept].astype(BF16)


def add_chunks(kept, before_ref, row_refs, last_refs, dlogit_refs, w_ref, wt_ref, wct_ref, chunks_ref):
    members = len(last_refs)
    branches, own, width = wt_ref.shape
    nodes = last_refs[0].shape[1]
    hid = w_ref.shape[2]
    all_rows = []
    for branch in range(branches - 1):
        ours = row_refs[branch * members : (branch + 1) * members]
        all_rows.append(jnp.concatenate([ref[:nodes] for ref in ours], axis=0))
    ours = [rows for ref in last_refs for rows in stacked(ref, width)]
    all_rows.append(jnp.concatenate(ours, axis=0))
    dlogits_t = jnp.concatenate([ref[:kept] for ref in dlogit_refs], axis=1)
    own_class = branches * own
    first = lax.axis_index("shuf") * own_class
    which = first // hid
    columns = pl.ds(pl.multiple_of(first - which * hid, LANES), own_class)
    chosen = all_rows[0]
    for branch in range(1, branches):
        chosen = jnp.where(which == branch, all_rows[branch], chosen)

    def put(chunk, rows, value):
        chunks_ref[chunk, rows] = value if before_ref is None else before_ref[chunk, rows] + value

    hidden = jnp.maximum(matmul(chosen, w_ref[which, :, columns]), 0.0).astype(BF16)
    class_t = matmul(dlogits_t, hidden)
    for chunk in range(chunks_ref.shape[0]):
        put(chunk, slice(0, kept), class_t[:, chunk * LANES : (chunk + 1) * LANES])
    per_branch = chunks_ref.shape[0] // branches
    for branch, rows in enumerate(all_rows):
        live = matmul(wt_ref[branch], rows, ((1,), (1,))) > 0.0
        dhidden_t = jnp.where(live, matmul(wct_ref[branch], dlogits_t), 0.0).astype(BF16)
        branch_t = matmul(dhidden_t, rows)
        for part in range(per_branch):
            put(
                branch * per_branch + part,
                slice(kept, kept + width),
                branch_t[part * LANES : (part + 1) * LANES],
            )


def split_refs(members, refs):
    last = len(refs) - 3 - 2 * members
    return (
        refs[:last], refs[last : last + members], refs[last + members : last + 2 * members],
        *refs[last + 2 * members :],
    )


def early_kernel(kept, members, *refs):
    add_chunks(kept, None, *split_refs(members, refs[:-1]), refs[-1])


def late_chunks(kept, members, early_ref, refs, chunks_ref):
    add_chunks(kept, early_ref, *split_refs(members, refs), chunks_ref)


def late_kernel(kept, members, half, early_ref, *refs):
    ins = len(refs) - 1 - 2 * half
    outs = refs[ins:-1]
    chunks_ref = refs[-1]
    late_chunks(kept, members, early_ref, refs[:ins], chunks_ref)
    dom = lax.axis_index("dom")
    for step in range(half):
        stays = dom ^ (2 * step)
        outs[step][...] = chunks_ref[stays]
        outs[half + step][...] = chunks_ref[stays ^ 1].astype(BF16)


def plain_late_kernel(kept, members, early_ref, *refs):
    late_chunks(kept, members, early_ref, refs[:-1], refs[-1])


def write_chunk(kept, chunk, value, branch_ref, class_ref):
    per_branch = branch_ref.shape[2] // LANES
    start = pl.multiple_of(chunk * LANES, LANES)
    class_ref[:, pl.ds(start, LANES)] = value[: class_ref.shape[0]]
    branch = chunk // per_branch
    start = pl.multiple_of((chunk - branch * per_branch) * LANES, LANES)
    branch_ref[branch, :, pl.ds(start, LANES)] = value[kept:].T


def out_kernel(kept, distances, *refs):
    count = len(distances)
    ins = refs[-5 - count : -5]
    branch_ref, class_ref, branch_here, class_here, sems = refs[-5:]
    dom = lax.axis_index("dom")
    per_branch = branch_ref.shape[2] // LANES
    copies = []
    for number, distance in enumerate(distances):
        chunk = dom ^ distance
        value = ins[number][...].astype(F32)
        class_here[number] = value[: class_ref.shape[0]]
        start = pl.multiple_of(chunk * LANES, LANES)
        copies.append(
            pltpu.make_async_copy(
                class_here.at[number], class_ref.at[:, pl.ds(start, LANES)], sems.at[2 * number]
            )
        )
        copies[-1].start()
        branch_here[number] = value[kept:].T
        branch = chunk // per_branch
        start = pl.multiple_of((chunk - branch * per_branch) * LANES, LANES)
        copies.append(
            pltpu.make_async_copy(
                branch_here.at[number],
                branch_ref.at[branch, :, pl.ds(start, LANES)],
                sems.at[2 * number + 1],
            )
        )
        copies[-1].start()
    for copy in copies:
        copy.wait()


def write_out(kept, distances, values, outs, before):
    count = len(distances)
    return pl.pallas_call(
        functools.partial(out_kernel, kept, distances),
        out_shape=outs,
        in_specs=[ANYWHERE] * len(before) + [IN_VMEM] * count,
        out_specs=[pl.BlockSpec(memory_space=pltpu.HBM)] * 2,
        scratch_shapes=[
            pltpu.VMEM((count, outs[0].shape[1], LANES), F32),
            pltpu.VMEM((count, outs[1].shape[0], LANES), F32),
            pltpu.SemaphoreType.DMA((2 * count,)),
        ],
        input_output_aliases={0: 0, 1: 1} if before else {},
        compiler_params=pltpu.CompilerParams(vmem_limit_bytes=VMEM_LIMIT),
        cost_estimate=pl.CostEstimate(flops=1000, bytes_accessed=1000, transcendentals=0),
    )(*before, *values)


def plain_out_kernel(kept, in_ref, branch_ref, class_ref):
    for chunk in range(in_ref.shape[0]):
        write_chunk(kept, chunk, in_ref[chunk], branch_ref, class_ref)


def in_group(value, distance=None):
    members = [value]
    steps = [0]
    distance = lax.axis_size("shuf") // 2 if distance is None else distance
    while distance:
        members += [swapped(member, distance, "shuf") for member in members]
        steps += [step + distance for step in steps]
        distance //= 2
    return [members[steps.index(step)] for step in range(len(steps))]


def body(
    features, tile_values, tile_dst, tile_src, tile_count, send_left, send_right,
    send_count, batch_order, labels, w_branch, w_class,
):
    block = tile_values.shape[1]
    nodes, width = features.shape
    local = nodes // block
    slots = send_left.shape[0]
    tiles = tile_values.shape[0]
    branches, _, hid = w_branch.shape
    cat, classes = w_class.shape
    dom = lax.axis_size("dom")
    shuf = lax.axis_size("shuf")
    mine = lax.axis_index("shuf")
    share = nodes // shuf
    own = hid // shuf
    own_class = cat // shuf
    kept = up_to(classes, 16)
    row_scale = 1.0 / math.sqrt(float(nodes * dom * shuf))
    plan = Plan(tiles, slots)
    small = jnp.concatenate(
        [tile_dst, tile_src, tile_count, send_left, send_right, send_count.reshape(-1)]
    )
    blocks_f32 = jax.ShapeDtypeStruct((local, block, width), F32)
    slots_f32 = jax.ShapeDtypeStruct((slots, block, width), F32)
    rows_b16 = jax.ShapeDtypeStruct((nodes, width), BF16)
    first_b16 = jax.ShapeDtypeStruct((nodes + 16, width), BF16)
    logits_f32 = jax.ShapeDtypeStruct((classes, nodes), F32)
    w_class_t = w_class.T

    current = features.reshape(local, block, width)
    gathered = []
    logits = None
    hop_flops = 12 * tiles * block * block * width
    forward_flops = 2 * nodes * hid * (width + classes)
    ext = pltpu.VMEM((local + 2 * slots, block, width), F32)
    to_left, to_right, current, *rows = call(
        first_kernel,
        [slots_f32, slots_f32, blocks_f32, first_b16],
        [ANYWHERE] * 5,
        1000,
        [
            pltpu.SMEM((slots,), jnp.int32),
            pltpu.SMEM((slots,), jnp.int32),
            pltpu.SMEM((1, 2), jnp.int32),
            pltpu.VMEM((1, nodes), jnp.int32),
            pltpu.SemaphoreType.DMA((5,)),
        ],
        limit=VMEM_ALL,
    )(send_left, send_right, send_count, current, labels.reshape(1, nodes))
    current, tile_values, w_class_t = call(
        ready_kernel,
        [
            blocks_f32,
            jax.ShapeDtypeStruct(tile_values.shape, F32),
            jax.ShapeDtypeStruct(w_class_t.shape, BF16),
        ],
        [IN_VMEM] * 3,
        1000,
    )(current, tile_values, w_class_t)
    for hop in range(HOPS):
        from_lower = passed_along(to_right, "dom", 1)
        from_upper = passed_along(to_left, "dom", -1)
        for value in rows:
            gathered.append(in_group(value))
        before = [] if logits is None else [logits]
        logits = call(
            functools.partial(forward_kernel, hop),
            logits_f32,
            [IN_VMEM] * (3 + len(before)),
            forward_flops,
            after=[members[shuf // 2] for members in gathered[:2]] if hop == HOPS - 1 else [],
        )(current, w_branch, w_class_t, *before)
        if hop == 0:
            first_logits = logits
            after = []
        else:
            after = [first_logits]
        if hop < HOPS - 1:
            current, to_left, to_right, *rows = call(
                functools.partial(hop_kernel, plan),
                [blocks_f32, slots_f32, slots_f32, rows_b16],
                [IN_SMEM] + [IN_VMEM] * 4,
                hop_flops,
                [ext],
                after,
            )(small, current, from_lower, from_upper, tile_values)

    label_mine = call(
        label_kernel,
        jax.ShapeDtypeStruct((1, nodes), jnp.int32),
        [IN_VMEM] * (1 + shuf),
        1000,
    )(batch_order, *gathered[0])

    wt_own, wct_own = call(
        weights_kernel,
        [
            jax.ShapeDtypeStruct((branches, own, width), BF16),
            jax.ShapeDtypeStruct((branches, own, kept), BF16),
        ],
        [IN_VMEM] * 2,
        1000,
        [pltpu.VMEM((up_to(classes, LANES), own), F32)],
    )(w_branch, w_class_t)

    last_rows = call(
        functools.partial(last_hop_kernel, plan),
        jax.ShapeDtypeStruct((block, local * width), BF16),
        [IN_SMEM] + [IN_VMEM] * 4,
        hop_flops,
        [ext],
        [logits, label_mine, *gathered[1][1:]],
    )(small, current, from_lower, from_upper, tile_values)
    dlogits = call(
        functools.partial(loss_and_gradient_kernel, row_scale),
        jax.ShapeDtypeStruct((kept + 16, nodes), BF16),
        [IN_VMEM] * 6,
        1000,
        after=[gathered[2][shuf // 2]],
    )(last_rows, logits, w_branch, w_class_t, batch_order, label_mine)
    chunks = own_class // LANES
    height = kept + width
    ahead = shuf // 2
    chunks_f32 = jax.ShapeDtypeStruct((chunks, height, LANES), F32)
    grad_flops = shuf * nodes * own_class * (3 * width + 2 * kept)
    weights = (w_branch, wt_own, wct_own)
    across_rows = swapped(last_rows, ahead, "shuf")
    across = swapped(dlogits, ahead, "shuf")
    close_rows = in_group(last_rows, ahead // 2)
    close = in_group(dlogits, ahead // 2)
    early = call(
        functools.partial(early_kernel, kept, ahead),
        chunks_f32,
        [IN_VMEM] * (5 * ahead + 3),
        1000,
    )(
        *[member for members in gathered for member in members[:ahead]],
        *close_rows, *close, *weights,
    )
    across, across_rows, early = lax.optimization_barrier((across, across_rows, early))
    distant_rows = in_group(across_rows, ahead // 2)
    distant = in_group(across, ahead // 2)
    late_ins = (
        early, *[member for members in gathered for member in members[ahead:]],
        *distant_rows, *distant, *weights,
    )
    last_all = close + distant
    loss_rows = call(
        loss_kernel, jax.ShapeDtypeStruct((1, nodes), F32), [IN_VMEM] * shuf, 1000
    )(*last_all).reshape(nodes)

    outs = [
        jax.ShapeDtypeStruct((branches, width, own), F32),
        jax.ShapeDtypeStruct((classes, own_class), F32),
    ]
    if chunks == dom and dom % 2 == 0 and dom & (dom - 1) == 0:
        half = dom // 2
        one_f32 = jax.ShapeDtypeStruct((height, LANES), F32)
        made = call(
            functools.partial(late_kernel, kept, ahead, half),
            [one_f32] * half + [jax.ShapeDtypeStruct((height, LANES), BF16)] * half,
            [IN_VMEM] * len(late_ins),
            grad_flops,
            [pltpu.VMEM(chunks_f32.shape, F32)],
        )(*late_ins)
        order = list(range(half - 1, -1, -1))
        arrived = {step: swapped(made[half + step], 1) for step in order}
        total = {step: made[step] + arrived[step].astype(F32) for step in order}
        far = {step: swapped(total[step].astype(BF16), 2 * step) for step in order[:-1]}
        summed = total[0]
        for step in order[:-1]:
            summed = lax.optimization_barrier(summed + far[step].astype(F32))
        near = [summed.astype(BF16)]
        near += [swapped(near[0], 2 * step) for step in range(1, half)]
        other = [swapped(value, 1) for value in near]
        results = []
        places = [2 * step for step in range(half)] + [2 * step + 1 for step in range(half)]
        for part in (slice(0, -2), slice(-2, -1), slice(-1, None)):
            results = write_out(kept, places[part], (near + other)[part], outs, results)
        grad_branch, grad_class_t = results
    else:
        grads = call(
            functools.partial(plain_late_kernel, kept, ahead),
            chunks_f32,
            [IN_VMEM] * len(late_ins),
            grad_flops,
        )(*late_ins)
        grad_branch, grad_class_t = call(
            functools.partial(plain_out_kernel, kept), outs, [IN_VMEM], 1000
        )(lax.psum(grads, "dom"))
    return (loss_rows, grad_branch, grad_class_t.T)


def solution(mesh):
    return jax.shard_map(
        body,
        mesh=mesh,
        in_specs=(
            P(("dom", "shuf"), None),
            P(("dom", "shuf"), None, None),
            P(("dom", "shuf")),
            P(("dom", "shuf")),
            P(("dom", "shuf")),
            P(("dom", "shuf")),
            P(("dom", "shuf")),
            P(("dom", "shuf"), None),
            P(("dom", "shuf"), None),
            P(("dom", "shuf")),
            P(),
            P(),
        ),
        out_specs=(P(("dom", "shuf")), P(None, None, "shuf"), P("shuf", None)),
        check_vma=False,
    )
```
